32 devices in a mesh: dp: 8 (over y, x, core), seq: 4 (over z).
Axes of the slice: x: 2, y: 2, z: 4, core: 2. Of those that a mesh axis runs over, the one named last changes fastest.
Arguments:
- long_tokens: bfloat16 [8, 512, 512], P('dp', 'seq'), may hold values from -6 to 6
- short_tokens: bfloat16 [16, 256, 512], P('dp', 'seq'), may hold values from -6 to 6
- long_cot: bfloat16 [8, 512, 512], P('dp', 'seq'), may hold values from -6 to 6
- short_cot: bfloat16 [16, 256, 512], P('dp', 'seq'), may hold values from -6 to 6
- long_lengths: int32 [8], P('dp'), may hold values from 1 to 512, as said below
- short_lengths: int32 [16], P('dp'), may hold values from 1 to 256, as said below
- w_query: bfloat16 [512, 512], P(('dp', 'seq')), may hold values from -0.375 to 0.375
- w_key: bfloat16 [512, 512], P(('dp', 'seq')), may hold values from -0.25 to 0.25
- w_value: bfloat16 [512, 512], P(('dp', 'seq')), may hold values from -0.25 to 0.25
- w_out: bfloat16 [512, 512], P(('dp', 'seq')), may hold values from -2 to 2
- w_up: bfloat16 [512, 2048], P(('dp', 'seq')), may hold values from -0.25 to 0.25
- w_down: bfloat16 [2048, 512], P(None, ('dp', 'seq')), may hold values from -0.125 to 0.125
- pos_table: bfloat16 [512, 512], P(None, ('dp', 'seq')), may hold values from -3 to 3
- norm_gain: bfloat16 [2, 512], P(None, ('dp', 'seq')), may hold values from 0.5 to 1.5
- norm_bias: bfloat16 [2, 512], P(None, ('dp', 'seq')), may hold values from -1.5 to 1.5
Outputs:
- long_out: bfloat16 [8, 512, 512], P('dp', 'seq')
- short_out: bfloat16 [16, 256, 512], P('dp', 'seq')
- long_grad: bfloat16 [8, 512, 512], P('dp', 'seq')
- short_grad: bfloat16 [16, 256, 512], P('dp', 'seq')
- grad_query: float32 [512, 512], P(('dp', 'seq'))
- grad_key: float32 [512, 512], P(('dp', 'seq'))
- grad_value: float32 [512, 512], P(('dp', 'seq'))
- grad_out: float32 [512, 512], P(('dp', 'seq'))
- grad_up: float32 [512, 2048], P(('dp', 'seq'))
- grad_down: float32 [2048, 512], P(None, ('dp', 'seq'))
- grad_pos: float32 [512, 512], P(None, ('dp', 'seq'))
- grad_gain: float32 [2, 512], P(None, ('dp', 'seq'))
- grad_bias: float32 [2, 512], P(None, ('dp', 'seq'))
The draws below stay inside these ranges and needn't reach their ends.
Inputs may be any that keep to these rules, and one draw needn't show every extreme that they name: `long_lengths`: characters at or after a window's length are padding: no query attends to them. Some long window has length exactly 512. `short_lengths`: characters at or after a window's length are padding: no query attends to them. Some short window has length exactly 256.
All inputs are finite; a program needn't handle non-finite values.
Results may differ from the reference program's by a relative error of at most 0.014.
The reference program's roundings to bfloat16 on the way count: a program that leaves them out, or rounds other values in their place, can miss the bound.
Values may be sent and summed in bfloat16 or wider, within the bound.
No kernel may reach another device: no remote copies, remote signals or barrier semaphores. Data moves between devices by JAX's collectives and lax.ppermute only.
A program may use at most 128 MiB of HBM per device.

```python
import math
import jax
import jax.numpy as jnp
from jax import lax

D = 512
HEADS = 8
FF = 2048
HEAD_DIM = 64
LONG = 512
SHORT = 256
LONG_WIN = 8
SHORT_WIN = 16


def full_length_draw(key, window_total, window_len):
    pick_key, value_key = jax.random.split(key)
    drawn_lengths = jax.random.randint(value_key, (window_total,), 1, window_len + 1)
    chosen = jax.random.randint(pick_key, (), 0, window_total)
    return jnp.where(jnp.arange(window_total) == chosen, window_len, drawn_lengths).astype(jnp.int32)


def draw_long_lengths(key, part):
    key = jax.random.fold_in(key, 7)
    return full_length_draw(key, LONG_WIN, LONG)


def draw_short_lengths(key, part):
    key = jax.random.fold_in(key, 13)
    return full_length_draw(key, SHORT_WIN, SHORT)


def level_of(rng, extent, pieces, low, high):
    def one(position, blocks):
        draws = jax.random.uniform(jax.random.fold_in(jax.random.fold_in(rng, 6), position), (blocks,), jnp.float32, low / len(pieces), high / len(pieces))
        return jnp.repeat(jnp.exp(draws), extent[position] // blocks).reshape((-1,) + (1,) * (len(extent) - position - 1))

    level = one(*pieces[0])
    for cut in pieces[1:]:
        level = level * one(*cut)
    return level


def bell_draw(own_key, dims, width, bound, shards=(), dtype=jnp.bfloat16):
    values = width * jax.random.normal(own_key, dims, jnp.float32)
    if shards:
        values = values * level_of(own_key, dims, shards, -0.22, 0.18)
    return jnp.clip(values, -bound, bound).astype(dtype)


def setup_inputs(seed: int = 0) -> dict:
    key_of = jax.random.split(jax.random.key(seed), 16)
    return {
        "long_tokens": bell_draw(key_of[0], (LONG_WIN, LONG, D), 1.0, 6.0, ((0, 8), (1, 4))),
        "short_tokens": bell_draw(key_of[1], (SHORT_WIN, SHORT, D), 1.0, 6.0, ((0, 8), (1, 4))),
        "long_cot": bell_draw(key_of[2], (LONG_WIN, LONG, D), 1.0, 6.0, ((0, 8), (1, 4))),
        "short_cot": bell_draw(key_of[3], (SHORT_WIN, SHORT, D), 1.0, 6.0, ((0, 8), (1, 4))),
        "long_lengths": draw_long_lengths(jax.random.fold_in(key_of[15], 71), 0),
        "short_lengths": draw_short_lengths(jax.random.fold_in(key_of[15], 71), 0),
        "w_query": bell_draw(key_of[6], (D, D), (D // 2) ** -0.5, 0.375, ((0, 32),)),
        "w_key": bell_draw(key_of[7], (D, D), D ** -0.5, 0.25, ((0, 32),)),
        "w_value": bell_draw(key_of[8], (D, D), D ** -0.5, 0.25, ((0, 32),)),
        "w_out": bell_draw(key_of[9], (D, D), (D // 64) ** -0.5, 2.0, ((0, 32),)),
        "w_up": bell_draw(key_of[10], (D, FF), D ** -0.5, 0.25, ((0, 32),)),
        "w_down": bell_draw(key_of[11], (FF, D), FF ** -0.5, 0.125, ((1, 32),)),
        "pos_table": bell_draw(key_of[12], (LONG, D), 0.5, 3.0, ((1, 32),)),
        "norm_gain": jnp.clip(1.0 + 0.1 * jax.random.normal(key_of[13], (2, D), jnp.float32), 0.5, 1.5).astype(jnp.bfloat16),
        "norm_bias": bell_draw(key_of[14], (2, D), 0.3, 1.5, ((1, 32),)),
    }


@jax.custom_vjp
def low(v):
    return lax.optimization_barrier(v.astype(jnp.bfloat16)).astype(jnp.float32)

@jax.custom_vjp
def low_back(v):
    return v

def low_keep(v):
    return (low(v), None)

def low_pass(kept, grad):
    return (grad,)

def back_keep(v):
    return (v, None)

def back_low(kept, grad):
    return (low(grad),)
low.defvjp(low_keep, low_pass)
low_back.defvjp(back_keep, back_low)

def layer_norm(values, gain, bias):
    row_mean = lax.optimization_barrier(jnp.mean(values, axis=-1, keepdims=True))
    centred = values - row_mean
    variance = lax.optimization_barrier(jnp.mean(centred * centred, axis=-1, keepdims=True))
    return centred * lax.rsqrt(variance + 1e-05) * gain + bias

def product(left, weight):
    return jnp.einsum('bld,de->ble', left, weight, precision=lax.Precision.HIGHEST)

def window_attend(window_args):
    queries, key_rows, values, length = window_args
    window_len = queries.shape[0]
    scores = jnp.einsum('qhd,khd->hqk', queries, key_rows, precision=lax.Precision.HIGHEST) * HEAD_DIM ** (-0.5)
    scores = low_back(scores)
    row_ids = jnp.arange(window_len)[:, None]
    col_ids = jnp.arange(window_len)[None, :]
    allowed = (col_ids <= row_ids) & (col_ids < length)
    scores = jnp.where(allowed[None], scores, -1e+30)
    row_max = lax.optimization_barrier(jnp.max(scores, axis=-1, keepdims=True))
    shifted = jnp.exp(scores - row_max)
    attn_weights = shifted / lax.optimization_barrier(jnp.sum(shifted, axis=-1, keepdims=True))
    mixed = jnp.einsum('hqk,khd->qhd', low(attn_weights), values, precision=lax.Precision.HIGHEST)
    return low_back(low(mixed))

def forward(params, tokens, lengths):
    w_query, w_key, w_value, w_out, w_up, w_down, pos_table, norm_gain, norm_bias = params
    windows, window_len, _ = tokens.shape
    first = tokens + pos_table[:window_len][None]
    first_low = low(first)
    queries = low_back(low(product(first_low, w_query))).reshape(windows, window_len, HEADS, HEAD_DIM)
    key_rows = low_back(low(product(first_low, w_key))).reshape(windows, window_len, HEADS, HEAD_DIM)
    values = low_back(low(product(first_low, w_value))).reshape(windows, window_len, HEADS, HEAD_DIM)
    mixed = lax.map(jax.checkpoint(window_attend), (queries, key_rows, values, lengths))
    mixed = mixed.reshape(windows, window_len, D)
    first_sum = first + low_back(product(mixed, w_out))
    normed = layer_norm(first_sum, norm_gain[0], norm_bias[0])
    hidden = low_back(product(low(normed), w_up))
    act = low(jax.nn.gelu(hidden, approximate=False))
    second = normed + low_back(product(act, w_down))
    return layer_norm(second, norm_gain[1], norm_bias[1])

def run_group(params, tokens, cotangent, lengths):
    window_total, window_len, _ = tokens.shape
    per_batch = math.gcd(window_total, max(1, 4096 // window_len))
    batch_count = window_total // per_batch
    batches_in = (tokens.reshape(batch_count, per_batch, window_len, D), cotangent.reshape(batch_count, per_batch, window_len, D), lengths.reshape(batch_count, per_batch))

    def step(summed, batch):
        tok_batch, cot_batch, len_batch = batch
        result, pull = jax.vjp(lambda weights_in, tokens_in: forward(weights_in, tokens_in, len_batch), params, tok_batch.astype(jnp.float32))
        grad_params, grad_tokens = pull(cot_batch.astype(jnp.float32))
        summed = jax.tree.map(lambda left, right: left + right, summed, grad_params)
        return (summed, (result.astype(jnp.bfloat16), grad_tokens.astype(jnp.bfloat16)))
    zeros_start = jax.tree.map(jnp.zeros_like, params)
    summed, (results, grads) = lax.scan(step, zeros_start, batches_in)
    return (summed, results.reshape(window_total, window_len, D), grads.reshape(window_total, window_len, D))

def reference(long_tokens, short_tokens, long_cot, short_cot, long_lengths, short_lengths, w_query, w_key, w_value, w_out, w_up, w_down, pos_table, norm_gain, norm_bias):
    params = tuple((item.astype(jnp.float32) for item in (w_query, w_key, w_value, w_out, w_up, w_down, pos_table, norm_gain, norm_bias)))
    long_sum, long_out, long_grad = run_group(params, long_tokens, long_cot, long_lengths)
    short_sum, short_out, short_grad = run_group(params, short_tokens, short_cot, short_lengths)
    total = jax.tree.map(lambda left, right: left + right, long_sum, short_sum)
    return (long_out, short_out, long_grad, short_grad, total[0], total[1], total[2], total[3], total[4], total[5], total[6], total[7], total[8])
```

```python
import functools
import math

import jax
import jax.numpy as jnp
from jax import lax
from jax.experimental import pallas as pl
from jax.experimental.pallas import tpu as pltpu
from jax.sharding import PartitionSpec as P

HEAD_DIM = 64
LANES = 128
BAND = 16
BF = jnp.bfloat16
F32 = jnp.float32
VMEM = pl.BlockSpec(memory_space=pltpu.VMEM)
SMEM = pl.BlockSpec(memory_space=pltpu.SMEM)
ANY = pl.BlockSpec(memory_space=pl.ANY)
NN = (((1,), (0,)), ((), ()))
NT = (((1,), (1,)), ((), ()))
TN = (((0,), (0,)), ((), ()))


def mm(left, right, dims=NN):
    return lax.dot_general(left, right, dims, preferred_element_type=F32)


def call(body, outs, ins, scratch, flops, moved, name):
    return pl.pallas_call(
        body,
        out_shape=[jax.ShapeDtypeStruct(shape, dtype) for shape, dtype, _ in outs],
        out_specs=[spec for _, _, spec in outs],
        in_specs=ins,
        scratch_shapes=scratch,
        compiler_params=pltpu.CompilerParams(vmem_limit_bytes=50 * 1024 * 1024),
        cost_estimate=pl.CostEstimate(flops=flops, bytes_accessed=moved, transcendentals=0),
        name=name,
    )


def slot_device(slot, slots, me):
    half = slots // 2
    core, rest = divmod(slot, half)
    layer, place = divmod(rest, 4)
    return lax.bitwise_xor(jnp.int32((layer * 2 + core) * 4 + place), me)


def fetch_weights(near, far, weights, sem, me):
    half = near.shape[0]
    for slot in range(2 * half):
        start = pl.multiple_of(slot_device(slot, 2 * half, me) * BAND, BAND)
        source = near if slot < half else far
        pltpu.make_async_copy(
            source.at[slot % half], weights.at[:, pl.ds(start, BAND), :], sem
        ).start()


def store_slots(grads, near, far, sem, me):
    half = near.shape[0]
    for slot in range(2 * half):
        start = pl.multiple_of(slot_device(slot, 2 * half, me) * BAND, BAND)
        target = near if slot < half else far
        pltpu.make_async_copy(
            grads.at[:, pl.ds(start, BAND), :], target.at[slot % half], sem
        ).start()
    pltpu.make_async_copy(grads, grads, sem).wait()


def split_rows(seq_count, long_len, short_len, short_win):
    total_long = seq_count * long_len

    def parts(k):
        found = [(k * long_len, long_len)]
        for w in range(short_win):
            found.append((total_long + (w * seq_count + k) * short_len, short_len))
        return found

    return parts


def stack_heads(block, lane):
    zero = jnp.zeros_like(block)
    return jnp.concatenate([jnp.where(lane, block, zero), jnp.where(lane, zero, block)], 0)


def join_heads(stacked, lane):
    half = stacked.shape[0] // 2
    return jnp.where(lane, stacked[:half], stacked[half:])


def attend_body(dims, ids, long_len, short_len, *refs):
    seq_count, n_long, n_short, short_win = dims
    tokens = refs[:seq_count]
    near, far = refs[seq_count : seq_count + 2]
    first_o, low_o, q_o, k_o, v_o, pl_o, ps_o, mix_o = refs[seq_count + 2 : seq_count + 10]
    weights, table, sem = refs[seq_count + 10 :]
    me, seq = (ids[0], ids[1])
    width = first_o.shape[1]
    fetch_weights(near, far, weights, sem, me)
    pltpu.make_async_copy(weights, weights, sem).wait()
    table[...] = weights[3].astype(F32).T
    parts = split_rows(seq_count, n_long, n_short, short_win)
    for k in range(seq_count):
        owner = lax.bitwise_xor(seq, jnp.int32(k))
        rows_in = 0
        for at, size in parts(k):
            place = pl.multiple_of(owner * size, size)
            first = tokens[k][rows_in : rows_in + size, :].astype(F32) + table[pl.ds(place, size), :]
            low_o[at : at + size, :] = first.astype(BF)
            if k == 0:
                first_o[rows_in : rows_in + size, :] = first
            rows_in += size
    k_o[...] = mm(low_o[...], weights[1]).astype(BF)
    v_o[...] = mm(low_o[...], weights[2]).astype(BF)
    own = jnp.concatenate([low_o[at : at + size, :] for at, size in parts(0)], 0)
    q_o[...] = mm(own, weights[0]).astype(BF) * BF(HEAD_DIM**-0.5)
    lane = lax.broadcasted_iota(jnp.int32, (1, LANES), 1) < HEAD_DIM
    groups = width // LANES

    def window(row, size, key_at, length, save):
        keys = seq_count * size
        row_pos = seq * size + lax.broadcasted_iota(jnp.int32, (size, keys), 0)
        col = lax.broadcasted_iota(jnp.int32, (size, keys), 1)
        col_pos = lax.bitwise_xor(col // size, jnp.full_like(col, seq)) * size + col % size
        allowed = (col_pos <= row_pos) & (col_pos < length)
        allowed = jnp.concatenate([allowed.astype(jnp.int32)] * 2, 0) > 0
        for g in range(groups):
            cols = slice(g * LANES, (g + 1) * LANES)
            queries = stack_heads(q_o[row : row + size, cols], lane)
            scores = mm(queries, k_o[key_at : key_at + keys, cols], NT)
            scores = jnp.where(allowed, scores, -1e30)
            top = jnp.max(scores, axis=-1, keepdims=True)
            shifted = jnp.exp(scores - top)
            probs = (shifted / jnp.sum(shifted, axis=-1, keepdims=True)).astype(BF)
            save(g, probs)
            mixed = mm(probs, v_o[key_at : key_at + keys, cols])
            mix_o[row : row + size, cols] = join_heads(mixed, lane).astype(BF)

    def save_long(g, probs):
        pl_o[g] = probs

    window(0, n_long, 0, long_len[0], save_long)
    for w in range(short_win):

        def save_short(g, probs, w=w):
            ps_o[w, g] = probs

        window(
            n_long + w * n_short,
            n_short,
            seq_count * (n_long + w * n_short),
            short_len[w],
            save_short,
        )


def norm_parts(values):
    mean = jnp.mean(values, axis=-1, keepdims=True)
    centred = values - mean
    scale = lax.rsqrt(jnp.mean(centred * centred, axis=-1, keepdims=True) + 1e-05)
    return centred * scale, scale


def norm_back(cot, gain, xhat, scale):
    scaled = cot * gain
    mean = jnp.mean(scaled, axis=-1, keepdims=True)
    inner = jnp.mean(scaled * xhat, axis=-1, keepdims=True)
    return scale * (scaled - mean - xhat * inner)


def middle_body(ids, first, mixed, cot, near, far, out_o, gsum_o, gmix_o, gnear, gfar, weights, grads, act, slope, sem):
    me = ids[0]
    fetch_weights(near, far, weights, sem, me)
    pltpu.make_async_copy(weights, weights, sem).wait()
    width = first.shape[1]
    chunks = (weights.shape[0] - 2) // 2
    norm = weights.shape[0] - 1
    vectors = jnp.sum(weights[norm].astype(F32).reshape(-1, BAND, width), axis=0)
    gain0, gain1, bias0, bias1 = (vectors[i : i + 1] for i in range(4))
    mixed_low = mixed[...]
    xhat0, scale0 = norm_parts(first[...] + mm(mixed_low, weights[0]))
    normed = xhat0 * gain0 + bias0
    normed_low = normed.astype(BF)
    second = normed
    for c in range(chunks):
        hidden = mm(normed_low, weights[1 + c])
        cdf = 0.5 + 0.5 * lax.erf(hidden * (0.5**0.5))
        slope[c] = cdf + hidden * jnp.exp(-0.5 * hidden * hidden) * ((2 * math.pi) ** -0.5)
        act[c] = (hidden * cdf).astype(BF)
        second = second + mm(act[c], weights[1 + chunks + c], NT)
    xhat1, scale1 = norm_parts(second)
    out_o[...] = (xhat1 * gain1 + bias1).astype(BF)
    cot_wide = cot[...].astype(F32)
    grad_second = norm_back(cot_wide, gain1, xhat1, scale1)
    second_low = grad_second.astype(BF)
    grad_normed = grad_second
    for c in range(chunks):
        hidden_low = (mm(second_low, weights[1 + chunks + c]) * slope[c]).astype(BF)
        grads[1 + chunks + c] = mm(second_low, act[c], TN).astype(BF)
        grads[1 + c] = mm(normed_low, hidden_low, TN).astype(BF)
        grad_normed = grad_normed + mm(hidden_low, weights[1 + c], NT)
    grad_sum = norm_back(grad_normed, gain0, xhat0, scale0)
    gsum_o[...] = grad_sum
    sum_low = grad_sum.astype(BF)
    gmix_o[...] = mm(sum_low, weights[0], NT).astype(BF)
    grads[0] = mm(mixed_low, sum_low, TN).astype(BF)
    terms = jnp.concatenate(
        [
            jnp.sum(grad_normed * xhat0, axis=0, keepdims=True),
            jnp.sum(cot_wide * xhat1, axis=0, keepdims=True),
            jnp.sum(grad_normed, axis=0, keepdims=True),
            jnp.sum(cot_wide, axis=0, keepdims=True),
            jnp.zeros((BAND - 4, width), F32),
        ],
        0,
    ).astype(BF)
    for d in range(width // BAND):
        grads[norm, d * BAND : (d + 1) * BAND, :] = terms
    store_slots(grads, gnear, gfar, sem, me)


def attend_back_body(dims, gmix, q, k, v, pl_i, ps_i, dq_o, dk_o, dv_o):
    seq_count, n_long, n_short, short_win = dims
    lane = lax.broadcasted_iota(jnp.int32, (1, LANES), 1) < HEAD_DIM
    groups = gmix.shape[1] // LANES
    scale = HEAD_DIM**-0.5

    def window(row, size, key_at, load):
        keys = seq_count * size
        for g in range(groups):
            cols = slice(g * LANES, (g + 1) * LANES)
            grads = stack_heads(gmix[row : row + size, cols], lane)
            queries = stack_heads(q[row : row + size, cols], lane)
            probs = load(g)
            grad_probs = mm(grads, v[key_at : key_at + keys, cols], NT)
            wide = probs.astype(F32)
            inner = jnp.sum(wide * grad_probs, axis=-1, keepdims=True)
            grad_scores = (wide * (grad_probs - inner)).astype(BF)
            grad_q = mm(grad_scores, k[key_at : key_at + keys, cols])
            dq_o[row : row + size, cols] = (join_heads(grad_q, lane) * scale).astype(BF)
            dk_o[key_at : key_at + keys, cols] = mm(grad_scores, queries, TN).astype(BF)
            dv_o[key_at : key_at + keys, cols] = mm(probs, grads, TN).astype(BF)

    window(0, n_long, 0, lambda g: pl_i[g])
    for w in range(short_win):
        window(
            n_long + w * n_short,
            n_short,
            seq_count * (n_long + w * n_short),
            lambda g, w=w: ps_i[w, g],
        )


def leave_body(dims, ids, low, dq, dk, dv, gsum, near, far, *refs):
    seq_count, n_long, n_short, short_win = dims
    own_o = refs[0]
    sent = refs[1:seq_count]
    gnear, gfar, weights, grads, table, sem = refs[seq_count:]
    me, seq = (ids[0], ids[1])
    fetch_weights(near, far, weights, sem, me)
    parts = split_rows(seq_count, n_long, n_short, short_win)
    own = jnp.concatenate([low[at : at + size, :] for at, size in parts(0)], 0)
    grads[0] = mm(own, dq[...], TN).astype(BF)
    grads[1] = mm(low[...], dk[...], TN).astype(BF)
    grads[2] = mm(low[...], dv[...], TN).astype(BF)
    pltpu.make_async_copy(weights, weights, sem).wait()
    back = mm(dk[...], weights[1], NT) + mm(dv[...], weights[2], NT)
    from_q = gsum[...] + mm(dq[...], weights[0], NT)
    order = []
    for k in range(seq_count):
        owner = lax.bitwise_xor(seq, jnp.int32(k))
        rows_in = 0
        for which, (at, size) in enumerate(parts(k)):
            piece = back[at : at + size]
            if k == 0:
                piece = piece + from_q[rows_in : rows_in + size]
                own_o[rows_in : rows_in + size, :] = piece
            else:
                sent[k - 1][rows_in : rows_in + size, :] = piece.astype(BF)
            order.append((min(which, 1), pl.multiple_of(owner * size, size), size, piece))
            rows_in += size
    table[...] = jnp.zeros_like(table)
    for which in range(2):
        for kind, place, size, piece in order:
            if kind == which:
                table[pl.ds(place, size), :] += piece
    grads[3] = table[...].T.astype(BF)
    store_slots(grads, gnear, gfar, sem, me)


def sum_stage(parts, groups, name):
    count, pieces, band, width = parts[0].shape
    size = count // groups

    def body(*refs):
        ins, outs = (refs[: len(parts)], refs[len(parts) :])
        for g in range(groups):
            rows = slice(g * size, (g + 1) * size)
            total = ins[0][rows].astype(F32)
            for item in ins[1:]:
                total = total + item[rows].astype(F32)
            outs[g][...] = total.astype(outs[g].dtype)

    def block(n):
        return pl.BlockSpec((n, 1, band, width), lambda i: (0, i, 0, 0))

    return pl.pallas_call(
        body,
        grid=(pieces,),
        out_shape=[
            jax.ShapeDtypeStruct((size, pieces, band, width), F32 if g == 0 else BF)
            for g in range(groups)
        ],
        in_specs=[block(count)] * len(parts),
        out_specs=[block(size)] * groups,
        compiler_params=pltpu.CompilerParams(vmem_limit_bytes=50 * 1024 * 1024),
        cost_estimate=pl.CostEstimate(
            flops=count * pieces * band * width * len(parts),
            bytes_accessed=2 * count * pieces * band * width * (len(parts) + 1),
            transcendentals=0,
        ),
        name=name,
    )(*parts)


def swap(value, axis, size, mask, keep=lambda source, target: True):
    pairs = [(i, i ^ mask) for i in range(size) if keep(i, i ^ mask)]
    return lax.ppermute(value, axis, pairs)


def local(
    dp_count,
    seq_count,
    long_tokens,
    short_tokens,
    long_cot,
    short_cot,
    long_lengths,
    short_lengths,
    w_query,
    w_key,
    w_value,
    w_out,
    w_up,
    w_down,
    pos_table,
    norm_gain,
    norm_bias,
):
    width = w_key.shape[1]
    hidden = w_up.shape[1]
    chunks = hidden // width
    shard = w_key.shape[0]
    slots = width // BAND
    direct = shard == BAND and seq_count == 4
    device = lax.axis_index("dp") * seq_count + lax.axis_index("seq")
    seq = lax.axis_index("seq")
    ids = jnp.stack([device if direct else device * 0, seq]).astype(jnp.int32)

    n_long, n_short, short_win = (long_tokens.shape[1], short_tokens.shape[1], short_tokens.shape[0])
    dims = (seq_count, n_long, n_short, short_win)
    rows = n_long + short_win * n_short
    group_rows = seq_count * rows

    def flat(long_part, short_part):
        return jnp.concatenate([long_part.reshape(-1, width), short_part.reshape(-1, width)], 0)

    vectors = jnp.concatenate([norm_gain, norm_bias], 0)
    norm_rows = lax.dynamic_update_slice(
        jnp.zeros((shard if direct else 8, width), BF), vectors, (0, device * shard)
    )
    early = jnp.stack([w_query, w_key, w_value, pos_table.T])

    def columns(weight):
        return weight.reshape(weight.shape[0], chunks, width).transpose(1, 0, 2)

    late = [w_out[None], columns(w_up), columns(w_down.T)]

    def gather(piece):
        layer = jnp.stack([piece] + [swap(piece, "seq", seq_count, k) for k in range(1, seq_count)])
        near = jnp.concatenate(
            [layer] + [swap(layer, "dp", dp_count, k) for k in range(2, dp_count, 2)], 0
        )
        return near, swap(near, "dp", dp_count, 1)

    def gather_plain(piece):
        whole = lax.all_gather(piece, ("dp", "seq"), axis=1, tiled=True)
        return to_slots(whole)

    def to_slots(whole):
        count = whole.shape[0]
        cut = whole.reshape(count, slots // 8, 2, 4, BAND, width).transpose(2, 1, 3, 0, 4, 5)
        cut = cut.reshape(2, slots // 2, count, BAND, width)
        return cut[0], cut[1]

    def from_slots(near, far):
        count = near.shape[1]
        cut = jnp.stack([near, far]).reshape(2, slots // 8, 4, count, BAND, width)
        return cut.transpose(3, 1, 0, 2, 4, 5).reshape(count, width, width)

    tokens = flat(long_tokens, short_tokens)
    cots = flat(long_cot, short_cot)
    if direct:
        early_full = gather(early)
    else:
        early_full = gather_plain(early)
    group_tokens = [tokens] + [
        swap(tokens, "seq", seq_count, k, lambda source, target: source < target)
        for k in range(1, seq_count)
    ]
    if direct:
        late_full = gather(jnp.concatenate(late + [norm_rows[None]], 0))
    else:
        norm_whole = lax.psum(norm_rows.astype(F32), ("dp", "seq")).astype(BF)
        norm_slots = to_slots(jnp.pad(norm_whole, ((0, width - 8), (0, 0)))[None])
        late_full = [
            jnp.concatenate([a, b], 1)
            for a, b in zip(gather_plain(jnp.concatenate(late, 0)), norm_slots)
        ]

    groups = width // LANES
    long_probs = (groups, 2 * n_long, seq_count * n_long)
    short_probs = (short_win, groups, 2 * n_short, seq_count * n_short)
    square = width * width
    early_pieces, late_pieces = (4, 2 + 2 * chunks)
    first, low, queries, key_rows, values, p_long, p_short, mixed = call(
        functools.partial(attend_body, dims),
        [
            ((rows, width), F32, VMEM),
            ((group_rows, width), BF, VMEM),
            ((rows, width), BF, VMEM),
            ((group_rows, width), BF, VMEM),
            ((group_rows, width), BF, VMEM),
            (long_probs, BF, VMEM),
            (short_probs, BF, VMEM),
            ((rows, width), BF, VMEM),
        ],
        [SMEM] * 3 + [VMEM] * seq_count + [ANY] * 2,
        [
            pltpu.VMEM((early_pieces, width, width), BF),
            pltpu.VMEM((width, width), F32),
            pltpu.SemaphoreType.DMA,
        ],
        6 * group_rows * square,
        20 * 1024 * 1024,
        "attend",
    )(ids, long_lengths, short_lengths, *group_tokens, *early_full)

    slot_half = (slots // 2, late_pieces, BAND, width)
    out, grad_sum, grad_mixed, late_near, late_far = call(
        middle_body,
        [
            ((rows, width), BF, VMEM),
            ((rows, width), F32, VMEM),
            ((rows, width), BF, VMEM),
            (slot_half, BF, ANY),
            (slot_half, BF, ANY),
        ],
        [SMEM] + [VMEM] * 3 + [ANY] * 2,
        [
            pltpu.VMEM((late_pieces, width, width), BF),
            pltpu.VMEM((late_pieces, width, width), BF),
            pltpu.VMEM((chunks, rows, width), BF),
            pltpu.VMEM((chunks, rows, width), F32),
            pltpu.SemaphoreType.DMA,
        ],
        12 * rows * square * chunks,
        20 * 1024 * 1024,
        "middle",
    )(ids, first, mixed, cots, *late_full)

    grad_q, grad_k, grad_v = call(
        functools.partial(attend_back_body, dims),
        [
            ((rows, width), BF, VMEM),
            ((group_rows, width), BF, VMEM),
            ((group_rows, width), BF, VMEM),
        ],
        [VMEM] * 6,
        [],
        4 * group_rows * square,
        16 * 1024 * 1024,
        "attend_back",
    )(grad_mixed, queries, key_rows, values, p_long, p_short)
    slot_half = (slots // 2, early_pieces, BAND, width)
    leave_outs = call(
        functools.partial(leave_body, dims),
        [((rows, width), F32, VMEM)]
        + [((rows, width), BF, VMEM)] * (seq_count - 1)
        + [(slot_half, BF, ANY)] * 2,
        [SMEM] + [VMEM] * 5 + [ANY] * 2,
        [
            pltpu.VMEM((early_pieces, width, width), BF),
            pltpu.VMEM((early_pieces, width, width), BF),
            pltpu.VMEM((width, width), F32),
            pltpu.SemaphoreType.DMA,
        ],
        8 * group_rows * square,
        16 * 1024 * 1024,
        "leave",
    )(ids, low, grad_q, grad_k, grad_v, grad_sum, *early_full)
    grad_first, sent = (leave_outs[0], leave_outs[1:seq_count])
    early_near, early_far = leave_outs[seq_count:]

    for k in range(1, seq_count):
        grad_first = grad_first + swap(
            sent[k - 1], "seq", seq_count, k, lambda source, target: source > target
        ).astype(F32)
    grads = grad_first.astype(BF)

    def scatter(near, far, name):
        arrived = swap(far, "dp", dp_count, 1)
        layers = sum_stage([near, arrived], dp_count // 2, name + "_core")
        layers = [layers[0]] + [
            swap(layers[k], "dp", dp_count, 2 * k) for k in range(1, dp_count // 2)
        ]
        places = sum_stage(layers, seq_count, name + "_layer")
        total = places[0].astype(F32)
        for k in range(1, seq_count):
            total = total + swap(places[k], "seq", seq_count, k).astype(F32)
        return total[0]

    def scatter_plain(near, far):
        return lax.psum_scatter(
            from_slots(near, far).astype(F32), ("dp", "seq"), scatter_dimension=1, tiled=True
        )

    if direct:
        late_sum = scatter(late_near, late_far, "late")
        early_sum = scatter(early_near, early_far, "early")
        norm_sum = late_sum[-1]
    else:
        late_sum = scatter_plain(late_near, late_far)
        early_sum = scatter_plain(early_near, early_far)
        norm_sum = lax.psum(from_slots(late_near, late_far)[-1, :8].astype(F32), ("dp", "seq"))
    norm_sum = lax.dynamic_slice(norm_sum, (0, device * shard), (4, shard))

    def join(pieces):
        return pieces.transpose(1, 0, 2).reshape(shard, hidden)

    return (
        out[:n_long].reshape(long_tokens.shape),
        out[n_long:].reshape(short_tokens.shape),
        grads[:n_long].reshape(long_tokens.shape),
        grads[n_long:].reshape(short_tokens.shape),
        early_sum[0],
        early_sum[1],
        early_sum[2],
        late_sum[0],
        join(late_sum[1 : 1 + chunks]),
        join(late_sum[1 + chunks : 1 + 2 * chunks]).T,
        early_sum[3].T,
        norm_sum[:2],
        norm_sum[2:],
    )


def solution(mesh):
    rows = P(("dp", "seq"), None)
    cols = P(None, ("dp", "seq"))
    acts = P("dp", "seq", None)
    return jax.shard_map(
        functools.partial(local, mesh.shape["dp"], mesh.shape["seq"]),
        mesh=mesh,
        in_specs=(acts,) * 4 + (P("dp"),) * 2 + (rows,) * 5 + (cols,) * 4,
        out_specs=(acts,) * 4 + (rows,) * 5 + (cols,) * 4,
        check_vma=False,
    )
```

```python
import functools
import math

import jax
import jax.numpy as jnp
from jax import lax
from jax.experimental import pallas as pl
from jax.experimental.pallas import tpu as pltpu
from jax.sharding import PartitionSpec as P

HEAD_DIM = 64
LANES = 128
BAND = 16
MIB = 1024 * 1024
BF = jnp.bfloat16
F32 = jnp.float32
VMEM = pl.BlockSpec(memory_space=pltpu.VMEM)
SMEM = pl.BlockSpec(memory_space=pltpu.SMEM)
HBM = pl.BlockSpec(memory_space=pltpu.HBM)
NN = (((1,), (0,)), ((), ()))
NT = (((1,), (1,)), ((), ()))
TN = (((0,), (0,)), ((), ()))


def mm(left, right, dims=NN, precision=None):
    return lax.dot_general(left, right, dims, precision, preferred_element_type=F32)


def call(body, outs, ins, scratch, cost, name, limit):
    flops, moved = cost
    return pl.pallas_call(
        body,
        out_shape=[jax.ShapeDtypeStruct(shape, dtype) for shape, dtype, _ in outs],
        out_specs=[spec for _, _, spec in outs],
        in_specs=ins,
        scratch_shapes=scratch,
        compiler_params=pltpu.CompilerParams(vmem_limit_bytes=limit * MIB),
        cost_estimate=pl.CostEstimate(flops=flops, bytes_accessed=moved, transcendentals=0),
        name=name,
    )


def slot_rows(core, layer, place, me):
    device = lax.bitwise_xor(jnp.int32((layer * 2 + core) * 4 + place), me)
    return pl.ds(pl.multiple_of(device * BAND, BAND), BAND)


def each_slot(parts, by_layer, me):
    for i, part in enumerate(parts):
        core, outer = divmod(i, len(parts) // 2)
        for inner in range(part.shape[0]):
            layer, place = (outer, inner) if by_layer else (inner, outer)
            yield part.at[inner], slot_rows(core, layer, place, me)


def fetch_weights(parts, by_layer, weights, sem, me):
    for slot, rows in each_slot(parts, by_layer, me):
        pltpu.make_async_copy(slot, weights.at[:, rows, :], sem).start()


def cut_last(parts):
    return list(parts[:-1]) + [parts[-1].at[pl.ds(4 * k, 4)] for k in range(len(parts) - 1)]


def store_slots(grads, parts, by_layer, sem, me):
    for slot, rows in each_slot(cut_last(parts), by_layer, me):
        pltpu.make_async_copy(grads.at[:, rows, :], slot, sem).start()
    pltpu.make_async_copy(grads, grads, sem).wait()


def pick(seq, *options):
    chosen = options[-1]
    for i in range(len(options) - 2, -1, -1):
        chosen = jnp.where(seq == i, options[i], chosen)
    return chosen


def pad_rows(part, rows):
    return jnp.concatenate([part, jnp.zeros((rows - part.shape[0], part.shape[1]), part.dtype)], 0)


def pack_body(with_weights, ids, *refs):
    seq = ids[1]
    count = 11 if with_weights else 4
    sources, refs = (refs[:count], refs[count:])
    if with_weights:
        norms, refs = (refs[0], refs[1:])
    outs = 6 if with_weights else 4
    targets, held, sem = (refs[:outs], refs[outs : outs + count], refs[-1])
    pay1, pay_u2, pay_u3, pay_d = targets[:4]
    ins = [
        pltpu.make_async_copy(source, there, sem.at[i])
        for i, (source, there) in enumerate(zip(sources, held))
    ]
    for item in ins:
        item.start()
    long_tok, short_tok, long_cot, short_cot = held[:4]
    n_long, n_short = (long_tok.shape[1], short_tok.shape[1])
    copies = []

    def copy(source, target):
        item = pltpu.make_async_copy(source, target, sem.at[len(copies)])
        item.start()
        copies.append(item)

    if with_weights:
        early, late = targets[4:]
        row = refs[outs + count]
        width = early.shape[2]
        shard = norms.shape[1]
        col = lax.broadcasted_iota(jnp.int32, (shard, width), 1)
        at = lax.broadcasted_iota(jnp.int32, (shard, width), 0)
        spread = (col == at + ids[0] * shard).astype(BF)
        row[...] = pad_rows(mm(norms[...], spread), BAND).astype(BF)
    for item in ins:
        item.wait()
    if with_weights:
        wq, wk, wv, pos, wo, up, down = held[4:]
        chunks = up.shape[1] // width
        for i, weight in enumerate((wq, wk, wv, pos)):
            copy(weight, early.at[i])
        copy(wo, late.at[0])
        for c in range(chunks):
            cols = pl.ds(c * width, width)
            copy(up.at[:, cols], late.at[1 + c])
            copy(down.at[:, cols], late.at[1 + chunks + c])
        copy(row, late.at[1 + 2 * chunks])
    first = (seq > 0).astype(jnp.int32)
    for i, (longs, shorts) in enumerate(((long_tok, short_tok), (long_cot, short_cot))):
        copy(shorts.at[first], pay_u2.at[pl.ds(i * n_short, n_short), :])
        copy(shorts.at[1 - first], pay_u3.at[pl.ds(i * n_short, n_short), :])
        copy(longs.at[0], pay_d.at[pl.ds(i * n_long, n_long), :])
    last = len(copies)

    def both(sources, rows):
        ends = [
            pltpu.make_async_copy(source, pay1.at[pl.ds(i * n_long, rows), :], sem.at[last + i])
            for i, source in enumerate(sources)
        ]
        for item in ends:
            item.start()
        for item in ends:
            item.wait()

    @pl.when(seq < 2)
    def _():
        both((long_tok.at[0], long_cot.at[0]), n_long)

    @pl.when(seq > 1)
    def _():
        both((short_tok.at[3 - seq], short_cot.at[3 - seq]), n_short)

    for item in copies:
        item.wait()


def stack_heads(block, lane):
    zero = jnp.zeros_like(block)
    return jnp.concatenate([jnp.where(lane, block, zero), jnp.where(lane, zero, block)], 0)


def join_heads(stacked, lane):
    half = stacked.shape[0] // 2
    return jnp.where(lane, stacked[:half], stacked[half:])


def head_lanes():
    return lax.broadcasted_iota(jnp.int32, (1, LANES), 1) < HEAD_DIM


def block_base(seq, k, size):
    owner = lax.bitwise_xor(seq, jnp.int32(k))
    return pl.multiple_of(owner * jnp.where(seq < 2, size, size // 2), size // 2)


def gather_queries(seq, source, target):
    size = source.shape[0] // 4
    half = size // 2

    @pl.when(seq == 0)
    def _():
        target[...] = source[: 2 * size, :]

    @pl.when(seq == 1)
    def _():
        target[:size, :] = source[3 * size :, :]
        target[size:, :] = source[2 * size : 3 * size, :]

    @pl.when(seq > 1)
    def _():
        for k in range(4):
            target[k * half : (k + 1) * half, :] = source[k * size : k * size + half, :]


def spread_queries(seq, value, target):
    size = target.shape[0] // 4
    half = size // 2

    @pl.when(seq == 0)
    def _():
        target[: 2 * size, :] += value

    @pl.when(seq == 1)
    def _():
        target[3 * size :, :] += value[:size]
        target[2 * size : 3 * size, :] += value[size:]

    @pl.when(seq > 1)
    def _():
        for k in range(4):
            target[k * size : k * size + half, :] += value[k * half : (k + 1) * half]


def attend_body(layers, ids, long_len, short_len, *refs):
    long_tok, short_tok, long_cot, short_cot, got1, got_u2, got_u3, got_d2, got_d3 = refs[:9]
    parts = refs[9 : 9 + 2 * layers]
    first_o, cot_o, low_o, lowq_o, q_o, k_o, v_o, probs_o, mix_o = refs[9 + 2 * layers : 18 + 2 * layers]
    weights, table, first, cots, sem = refs[18 + 2 * layers :]
    me, seq = (ids[0], ids[1])
    fetch_weights(parts, True, weights, sem, me)
    n_long, n_short = (long_tok.shape[1], short_tok.shape[1])
    longs = seq < 2
    for i, (target, whole, shorts) in enumerate(
        ((first, long_tok, short_tok), (cots, long_cot, short_cot))
    ):
        big = slice(i * n_long, (i + 1) * n_long)
        small = slice(i * n_short, (i + 1) * n_short)
        own_short = pad_rows(jnp.where(seq == 2, shorts[0], shorts[1]), n_long)
        blocks = (
            jnp.where(longs, whole[0], own_short),
            jnp.where(longs, got1[big, :], pad_rows(got1[i * n_long : i * n_long + n_short, :], n_long)),
            jnp.where(longs, got_d2[big, :], pad_rows(got_u2[small, :], n_long)),
            jnp.where(longs, got_d3[big, :], pad_rows(got_u3[small, :], n_long)),
        )
        for k, block in enumerate(blocks):
            target[k * n_long : (k + 1) * n_long, :] = block.astype(target.dtype)
    gather_queries(seq, cots, cot_o)
    pltpu.make_async_copy(weights, weights, sem).wait()
    table[...] = weights[3].astype(F32).T
    for k in range(4):
        rows = slice(k * n_long, (k + 1) * n_long)
        first[rows, :] += table[pl.ds(block_base(seq, k, n_long), n_long), :]
    gather_queries(seq, first, first_o)
    lowq_o[...] = first_o[...].astype(BF)
    low_o[...] = first[...].astype(BF)
    k_o[...] = mm(low_o[...], weights[1]).astype(BF)
    v_o[...] = mm(low_o[...], weights[2]).astype(BF)
    q_o[...] = mm(lowq_o[...], weights[0]).astype(BF) * BF(HEAD_DIM**-0.5)
    rows, keys = (first_o.shape[0], first.shape[0])
    row = lax.broadcasted_iota(jnp.int32, (rows, 1), 0)
    row_pos = jnp.where(
        longs,
        row + seq * rows,
        lax.bitwise_xor(row // n_short, jnp.full_like(row, seq)) * n_short + row % n_short,
    )
    row_pos = jnp.concatenate([row_pos, row_pos], 0)
    col = lax.broadcasted_iota(jnp.int32, (1, keys), 1)
    owner = lax.bitwise_xor(col // n_long, jnp.full_like(col, seq))
    inner = col % n_long
    col_pos = jnp.where(longs, owner * n_long + inner, owner * n_short + inner)
    length = pick(seq, long_len[0], long_len[0], short_len[0], short_len[1])
    seen = (col_pos < length) & (longs | (inner < n_short))
    col_pos = jnp.where(seen, col_pos, jnp.int32(1 << 20))
    allowed = col_pos <= row_pos
    lane = head_lanes()
    for g in range(first_o.shape[1] // LANES):
        cols = slice(g * LANES, (g + 1) * LANES)
        scores = mm(stack_heads(q_o[:, cols], lane), k_o[:, cols], NT)
        scores = jnp.where(allowed, scores, -1e30)
        shifted = jnp.exp(scores - jnp.max(scores, axis=-1, keepdims=True))
        probs_o[g] = (shifted / jnp.sum(shifted, axis=-1, keepdims=True)).astype(BF)
        mix_o[:, cols] = join_heads(mm(probs_o[g], v_o[:, cols]), lane).astype(BF)


def norm_parts(values):
    mean = jnp.mean(values, axis=-1, keepdims=True)
    centred = values - mean
    scale = lax.rsqrt(jnp.mean(centred * centred, axis=-1, keepdims=True) + 1e-05)
    return centred * scale, scale


def norm_back(cot, gain, xhat, scale):
    scaled = cot * gain
    mean = jnp.mean(scaled, axis=-1, keepdims=True)
    inner = jnp.mean(scaled * xhat, axis=-1, keepdims=True)
    return scale * (scaled - mean - xhat * inner)


def middle_body(layers, ids, first, mixed, cot, *refs):
    parts = refs[: 2 * layers]
    block_outs = refs[2 * layers : 2 * layers + 4]
    gsum_o, gmix_o = refs[2 * layers + 4 : 2 * layers + 6]
    grad_parts = refs[2 * layers + 6 : 3 * layers + 7]
    weights, grads, act, slope, blocks, sem = refs[3 * layers + 7 :]
    me, seq = (ids[0], ids[1])
    fetch_weights(parts, True, weights, sem, me)
    blocks[...] = jnp.zeros_like(blocks)
    pltpu.make_async_copy(weights, weights, sem).wait()
    width = first.shape[1]
    chunks = (weights.shape[0] - 2) // 2
    norm = weights.shape[0] - 1
    vectors = jnp.sum(weights[norm].astype(F32).reshape(-1, BAND, width), axis=0)
    gain0, gain1, bias0, bias1 = (vectors[i : i + 1] for i in range(4))
    mixed_low = mixed[...]
    xhat0, scale0 = norm_parts(first[...] + mm(mixed_low, weights[0]))
    normed = xhat0 * gain0 + bias0
    normed_low = normed.astype(BF)
    second = normed
    for c in range(chunks):
        hidden = mm(normed_low, weights[1 + c])
        cdf = 0.5 + 0.5 * lax.erf(hidden * (0.5**0.5))
        slope[c] = cdf + hidden * jnp.exp(-0.5 * hidden * hidden) * ((2 * math.pi) ** -0.5)
        act[c] = (hidden * cdf).astype(BF)
        second = second + mm(act[c], weights[1 + chunks + c], NT)
    xhat1, scale1 = norm_parts(second)
    spread_queries(seq, xhat1 * gain1 + bias1, blocks)
    size = block_outs[0].shape[0]
    for k, target in enumerate(block_outs):
        target[...] = blocks[k * size : (k + 1) * size, :].astype(BF)
    cot_wide = cot[...].astype(F32)
    grad_second = norm_back(cot_wide, gain1, xhat1, scale1)
    second_low = grad_second.astype(BF)
    grad_normed = grad_second
    for c in range(chunks):
        hidden_low = (mm(second_low, weights[1 + chunks + c]) * slope[c]).astype(BF)
        grads[1 + chunks + c] = mm(second_low, act[c], TN).astype(BF)
        grads[1 + c] = mm(normed_low, hidden_low, TN).astype(BF)
        grad_normed = grad_normed + mm(hidden_low, weights[1 + c], NT)
    grad_sum = norm_back(grad_normed, gain0, xhat0, scale0)
    gsum_o[...] = grad_sum
    sum_low = grad_sum.astype(BF)
    gmix_o[...] = mm(sum_low, weights[0], NT).astype(BF)
    grads[0] = mm(mixed_low, sum_low, TN).astype(BF)
    terms = jnp.concatenate(
        [
            jnp.sum(grad_normed * xhat0, axis=0, keepdims=True),
            jnp.sum(cot_wide * xhat1, axis=0, keepdims=True),
            jnp.sum(grad_normed, axis=0, keepdims=True),
            jnp.sum(cot_wide, axis=0, keepdims=True),
            jnp.zeros((BAND - 4, width), F32),
        ],
        0,
    ).astype(BF)
    for d in range(width // BAND):
        grads[norm, d * BAND : (d + 1) * BAND, :] = terms
    store_slots(grads, grad_parts, True, sem, me)


def attend_back_body(gmix, q, k, v, probs_i, dq_o, dk_o, dv_o):
    lane = head_lanes()
    scale = HEAD_DIM**-0.5
    for g in range(gmix.shape[1] // LANES):
        cols = slice(g * LANES, (g + 1) * LANES)
        grads = stack_heads(gmix[:, cols], lane)
        queries = stack_heads(q[:, cols], lane)
        probs = probs_i[g]
        grad_probs = mm(grads, v[:, cols], NT)
        wide = probs.astype(F32)
        inner = jnp.sum(wide * grad_probs, axis=-1, keepdims=True)
        grad_scores = (wide * (grad_probs - inner)).astype(BF)
        grad_q = mm(grad_scores, k[:, cols])
        dq_o[:, cols] = (join_heads(grad_q, lane) * scale).astype(BF)
        dk_o[:, cols] = mm(grad_scores, queries, TN).astype(BF)
        dv_o[:, cols] = mm(probs, grads, TN).astype(BF)


def leave_body(layers, ids, low, lowq, dq, dk, dv, gsum, *refs):
    parts = refs[: 2 * layers]
    own_o, sent1_o, sent2_o, sent3_o = refs[2 * layers : 2 * layers + 4]
    grad_parts = refs[2 * layers + 4 : 3 * layers + 5]
    weights, grads, table, back, sem = refs[3 * layers + 5 :]
    me, seq = (ids[0], ids[1])
    fetch_weights(parts, True, weights, sem, me)
    grads[0] = mm(lowq[...], dq[...], TN).astype(BF)
    grads[1] = mm(low[...], dk[...], TN).astype(BF)
    grads[2] = mm(low[...], dv[...], TN).astype(BF)
    pltpu.make_async_copy(weights, weights, sem).wait()
    back[...] = mm(dk[...], weights[1], NT) + mm(dv[...], weights[2], NT)
    spread_queries(seq, gsum[...] + mm(dq[...], weights[0], NT), back)
    size = own_o.shape[0]
    table[...] = jnp.zeros_like(table)
    for k, target in enumerate((own_o, sent1_o, sent2_o, sent3_o)):
        piece = back[k * size : (k + 1) * size, :]
        target[...] = piece.astype(target.dtype)
        table[pl.ds(block_base(seq, k, size), size), :] += piece
    grads[3] = table[...].T.astype(BF)
    store_slots(grads, grad_parts, True, sem, me)


def return_rows(ids, *refs):
    seq = ids[1]
    for i in range(2):
        mine, one, two, three = (item[...].astype(F32) for item in refs[4 * i : 4 * i + 4])
        long_o, short_o = refs[8 + 2 * i : 10 + 2 * i]
        half = short_o.shape[1]
        long_o[0] = jnp.where(seq < 2, mine + one, two + three).astype(BF)
        mine, one, two, three = (item[:half] for item in (mine, one, two, three))
        short_o[0] = pick(seq, two, three, mine, one).astype(BF)
        short_o[1] = pick(seq, three, two, one, mine).astype(BF)


def four_body(*refs):
    ins, outs = (refs[:-4], refs[-4:])
    for place, out in enumerate(outs):
        total = ins[0][place].astype(F32)
        for item in ins[1:]:
            total = total + item[place].astype(F32)
        out[...] = total.astype(out.dtype)


def four_sums(parts, name):
    _, pieces, band, width = parts[0].shape
    step = 2
    block_in = pl.BlockSpec((4, step, band, width), lambda i: (0, i, 0, 0))
    block_out = pl.BlockSpec((step, band, width), lambda i: (i, 0, 0))
    return pl.pallas_call(
        four_body,
        grid=(pieces // step,),
        out_shape=[
            jax.ShapeDtypeStruct((pieces, band, width), F32 if place == 0 else BF)
            for place in range(4)
        ],
        in_specs=[block_in] * len(parts),
        out_specs=[block_out] * 4,
        compiler_params=pltpu.CompilerParams(vmem_limit_bytes=16 * MIB),
        name=name,
    )(*parts)


def finish_body(ids, *refs):
    late, early, rows = (refs[:4], refs[4:8], refs[8:16])
    row_outs, early_outs = (refs[16:20], refs[20:24])
    out_o, up_o, down_o, norm_o = refs[24:]
    width = out_o.shape[1]
    chunks = up_o.shape[1] // width

    def total(parts, i):
        own, one, two, three = parts
        return own[i] + (one[i].astype(F32) + two[i].astype(F32) + three[i].astype(F32))

    return_rows(ids, *rows, *row_outs)
    out_o[...] = total(late, 0)
    for c in range(chunks):
        up_o[:, c * width : (c + 1) * width] = total(late, 1 + c)
        down_o[:, c * width : (c + 1) * width] = total(late, 1 + chunks + c)
    shard = norm_o.shape[1]
    row = lax.broadcasted_iota(jnp.int32, (width, shard), 0)
    col = lax.broadcasted_iota(jnp.int32, (width, shard), 1)
    chosen = (row == col + ids[0] * shard).astype(F32)
    norm_o[...] = mm(total(late, 1 + 2 * chunks), chosen, NN, lax.Precision.HIGHEST)
    for i, out in enumerate(early_outs):
        out[...] = total(early, i)


def after(value, *others):
    return lax.optimization_barrier((value,) + others)[0]


def local(
    dp_count,
    seq_count,
    long_tokens,
    short_tokens,
    long_cot,
    short_cot,
    long_lengths,
    short_lengths,
    w_query,
    w_key,
    w_value,
    w_out,
    w_up,
    w_down,
    pos_table,
    norm_gain,
    norm_bias,
):
    width = w_key.shape[1]
    hidden = w_up.shape[1]
    chunks = hidden // width
    shard = w_key.shape[0]
    direct = shard == BAND and dp_count == 8
    layers = 4
    device = lax.axis_index("dp") * seq_count + lax.axis_index("seq")
    seq = lax.axis_index("seq")
    true_ids = jnp.stack([device, seq]).astype(jnp.int32)
    ids = true_ids if direct else jnp.stack([device * 0, seq]).astype(jnp.int32)
    n_long, n_short = (long_tokens.shape[1], short_tokens.shape[1])
    rows, keys = (2 * n_long, 4 * n_long)
    square = width * width
    early_pieces, late_pieces = (4, 2 + 2 * chunks)

    def swap_seq(value, mask, keep=lambda source, target: True):
        pairs = [(i, i ^ mask) for i in range(seq_count) if keep(i, i ^ mask)]
        return lax.ppermute(value, "seq", pairs)

    def swap_dp(value, mask):
        return lax.ppermute(value, "dp", [(i, i ^ mask) for i in range(dp_count)])

    acts = [long_tokens, short_tokens, long_cot, short_cot]
    packed = [
        ((2 * n_long, width), BF, HBM),
        ((2 * n_short, width), BF, HBM),
        ((2 * n_short, width), BF, HBM),
        ((2 * n_long, width), BF, HBM),
    ]
    own, specs, scratch = ([], [HBM] * 4, [])
    held = list(acts)
    if direct:
        own = [w_query, w_key, w_value, pos_table.T, w_out, w_up, w_down.T]
        held += own
        own.append(jnp.concatenate([norm_gain, norm_bias], 0))
        packed += [((count, BAND, width), BF, HBM) for count in (early_pieces, late_pieces)]
        specs += [HBM] * 7 + [VMEM]
        scratch = [pltpu.VMEM((BAND, width), BF)]
    pays = call(
        functools.partial(pack_body, direct),
        packed,
        [SMEM] + specs,
        [pltpu.VMEM(item.shape, BF) for item in held] + scratch + [pltpu.SemaphoreType.DMA((32,))],
        (0, 4 * MIB),
        "pack",
        60,
    )(true_ids, *acts, *own)
    pay1, pay_u2, pay_u3, pay_d = pays[:4]

    def to_slots(whole, by_layer):
        count = whole.shape[0]
        order = (2, 1, 3, 0, 4, 5) if by_layer else (2, 3, 1, 0, 4, 5)
        cut = whole.reshape(count, 4, 2, 4, BAND, width).transpose(*order)
        return [cut[core, outer] for core in range(2) for outer in range(4)]

    def slot_outs(pieces):
        near = ((4, pieces, BAND, width), BF, HBM)
        return [near] * layers + [((4 * layers, pieces, BAND, width), BF, HBM)]

    def from_slots(parts, by_layer):
        count = parts[0].shape[1]
        cut = jnp.concatenate(parts, 0).reshape(2, 4, 4, count, BAND, width)
        order = (3, 1, 0, 2, 4, 5) if by_layer else (3, 2, 0, 1, 4, 5)
        return cut.transpose(*order).reshape(count, width, width)

    def places(piece):
        return [piece] + [swap_seq(piece, k) for k in range(1, 4)]

    def spread(column):
        near = [column] + [swap_dp(column, 2 * k) for k in range(1, layers)]
        return near

    def cross(near):
        return list(near) + [swap_dp(part, 1) for part in near]

    if direct:
        early, late = pays[4:]
        early_places = places(early)
        pay1, pay_u2, pay_u3, pay_d, late = lax.optimization_barrier(
            (pay1, pay_u2, pay_u3, pay_d, late, *early_places)
        )[:5]
    up_only = lambda source, target: source < target and source < 2 and target > 1
    down_only = lambda source, target: source > 1 and target == 1
    got = [
        swap_seq(pay1, 1),
        swap_seq(pay_u2, 2, up_only),
        swap_seq(pay_u3, 3, up_only),
        swap_seq(pay_d, 2, down_only),
        swap_seq(pay_d, 3, down_only),
    ]
    if direct:
        late_places = places(late)
        early_near = spread(jnp.stack(early_places))
        late_column = after(jnp.stack(late_places), *early_near)
        early_full = cross(early_near)
        late_full = cross(spread(late_column))
    else:

        def columns(weight):
            return weight.reshape(weight.shape[0], chunks, width).transpose(1, 0, 2)

        def whole(pieces):
            return lax.all_gather(pieces, ("dp", "seq"), axis=1, tiled=True)

        early_full = to_slots(whole(jnp.stack([w_query, w_key, w_value, pos_table.T])), True)
        vectors = jnp.concatenate([norm_gain, norm_bias], 0)
        vectors = lax.all_gather(vectors, ("dp", "seq"), axis=1, tiled=True)
        vectors = jnp.pad(vectors, ((0, width - 4), (0, 0)))
        late_whole = whole(jnp.concatenate([w_out[None], columns(w_up), columns(w_down.T)], 0))
        late_full = to_slots(jnp.concatenate([late_whole, vectors[None]], 0), True)

    groups = width // LANES
    first, cots, low, low_queries, queries, key_rows, values, probs, mixed = call(
        functools.partial(attend_body, layers),
        [
            ((rows, width), F32, VMEM),
            ((rows, width), BF, VMEM),
            ((keys, width), BF, VMEM),
            ((rows, width), BF, VMEM),
            ((rows, width), BF, VMEM),
            ((keys, width), BF, VMEM),
            ((keys, width), BF, VMEM),
            ((groups, 2 * rows, keys), BF, VMEM),
            ((rows, width), BF, VMEM),
        ],
        [SMEM] * 3 + [VMEM] * 9 + [HBM] * (2 * layers),
        [
            pltpu.VMEM((early_pieces, width, width), BF),
            pltpu.VMEM((width, width), F32),
            pltpu.VMEM((keys, width), F32),
            pltpu.VMEM((keys, width), BF),
            pltpu.SemaphoreType.DMA,
        ],
        (8 * keys * square, 10 * MIB),
        "attend",
        24,
    )(ids, long_lengths, short_lengths, *acts, *got, *early_full)

    block = (n_long, width)
    middle_outs = call(
        functools.partial(middle_body, layers),
        [(block, BF, VMEM)] * 4
        + [((rows, width), F32, VMEM), ((rows, width), BF, VMEM)]
        + slot_outs(late_pieces),
        [SMEM] + [VMEM] * 3 + [HBM] * (2 * layers),
        [
            pltpu.VMEM((late_pieces, width, width), BF),
            pltpu.VMEM((late_pieces, width, width), BF),
            pltpu.VMEM((chunks, rows, width), BF),
            pltpu.VMEM((chunks, rows, width), F32),
            pltpu.VMEM((keys, width), F32),
            pltpu.SemaphoreType.DMA,
        ],
        (16 * rows * square * chunks, 20 * MIB),
        "middle",
        32,
    )(ids, first, mixed, cots, *late_full)
    out_blocks, (grad_sum, grad_mixed) = (middle_outs[:4], middle_outs[4:6])
    late_parts = middle_outs[6:]

    def core_sums(parts, arrived):
        return [
            (parts[k].astype(F32) + arrived[4 * k : 4 * k + 4].astype(F32)).astype(BF)
            for k in range(1, layers)
        ]

    if direct:
        late_arrived = swap_dp(late_parts[-1], 1)

    grad_q, grad_k, grad_v = call(
        attend_back_body,
        [
            ((rows, width), BF, VMEM),
            ((keys, width), BF, VMEM),
            ((keys, width), BF, VMEM),
        ],
        [VMEM] * 5,
        [],
        (8 * keys * square, 8 * MIB),
        "attend_back",
        24,
    )(grad_mixed, queries, key_rows, values, probs)
    leave_outs = call(
        functools.partial(leave_body, layers),
        [(block, F32, VMEM)] + [(block, BF, VMEM)] * 3 + slot_outs(early_pieces),
        [SMEM] + [VMEM] * 6 + [HBM] * (2 * layers),
        [
            pltpu.VMEM((early_pieces, width, width), BF),
            pltpu.VMEM((early_pieces, width, width), BF),
            pltpu.VMEM((width, width), F32),
            pltpu.VMEM((keys, width), F32),
            pltpu.SemaphoreType.DMA,
        ],
        (10 * keys * square, 8 * MIB),
        "leave",
        24,
    )(ids, low, low_queries, grad_q, grad_k, grad_v, grad_sum, *early_full)
    grad_blocks, early_parts = (leave_outs[:4], leave_outs[4:])

    def rows_back(blocks):
        back = lambda source, target: (source > 1 and target < 2) or (source == 1 and target > 1)
        return [swap_seq(blocks[1], 1)] + [swap_seq(blocks[k], k, back) for k in (2, 3)]

    got = rows_back(grad_blocks)
    got_out = rows_back(out_blocks)
    row_ins = [grad_blocks[0], *got, out_blocks[0], *got_out]
    row_outs = [(item.shape, BF, VMEM) for item in (long_tokens, short_tokens)] * 2
    if direct:
        late_sums = core_sums(late_parts, late_arrived)
        late_layers = [swap_dp(part, 2 * k) for k, part in enumerate(late_sums, 1)]
        early_far = after(early_parts[-1], *late_sums)
        early_arrived = swap_dp(early_far, 1)
        early_sums = core_sums(early_parts, early_arrived)
        late_layers, early_sums, got = lax.optimization_barrier((late_layers, early_sums, got))
        row_ins[1:4] = got
        late_cut = four_sums([late_parts[0], late_arrived] + late_layers, "late_sum")
        early_layers = [swap_dp(part, 2 * k) for k, part in enumerate(early_sums, 1)]
        late_ends = [late_cut[0]] + [swap_seq(late_cut[k], k) for k in range(1, 4)]
        late_ends, early_layers = lax.optimization_barrier((late_ends, early_layers))
        early_cut = four_sums([early_parts[0], early_arrived] + early_layers, "early_sum")
        early_ends = [early_cut[0]] + [swap_seq(early_cut[k], k) for k in range(1, 4)]
        ends = call(
            finish_body,
            row_outs
            + [((shard, width), F32, VMEM)] * 5
            + [((shard, hidden), F32, VMEM)] * 2
            + [((BAND, shard), F32, VMEM)],
            [SMEM] + [VMEM] * 16,
            [],
            (0, MIB),
            "finish",
            16,
        )(ids, *late_ends, *early_ends, *row_ins)
        row_grads, early_sum, (grad_out, grad_up, grad_down, norms) = (ends[:4], ends[4:8], ends[8:])
    else:

        def scatter(parts, by_layer):
            wide = from_slots(parts, by_layer).astype(F32)
            return lax.psum_scatter(wide, ("dp", "seq"), scatter_dimension=1, tiled=True)

        def join(pieces):
            return pieces.transpose(1, 0, 2).reshape(shard, hidden)

        late_sum = scatter(late_parts, True)
        early_sum = scatter(early_parts, True)
        grad_out, grad_up, grad_down = (
            late_sum[0],
            join(late_sum[1 : 1 + chunks]),
            join(late_sum[1 + chunks : 1 + 2 * chunks]),
        )
        norms = lax.psum(from_slots(late_parts, True)[-1, :BAND].astype(F32), ("dp", "seq"))
        norms = lax.dynamic_slice(norms, (0, device * shard), (BAND, shard))
        row_grads = call(
            return_rows, row_outs, [SMEM] + [VMEM] * 8, [], (0, MIB), "return", 16
        )(ids, *row_ins)
    long_grad, short_grad, long_out, short_out = row_grads
    return (
        long_out,
        short_out,
        long_grad,
        short_grad,
        early_sum[0],
        early_sum[1],
        early_sum[2],
        grad_out,
        grad_up,
        grad_down.T,
        early_sum[3].T,
        norms[:2],
        norms[2:4],
    )


def solution(mesh):
    rows = P(("dp", "seq"), None)
    cols = P(None, ("dp", "seq"))
    acts = P("dp", "seq", None)
    return jax.shard_map(
        functools.partial(local, mesh.shape["dp"], mesh.shape["seq"]),
        mesh=mesh,
        in_specs=(acts,) * 4 + (P("dp"),) * 2 + (rows,) * 5 + (cols,) * 4,
        out_specs=(acts,) * 4 + (rows,) * 5 + (cols,) * 4,
        check_vma=False,
    )
```

```python
import functools
import math

import jax
import jax.numpy as jnp
from jax import lax
from jax.experimental import pallas as pl
from jax.experimental.pallas import tpu as pltpu
from jax.sharding import PartitionSpec as P

HEAD_DIM = 64
LANES = 128
BAND = 16
MIB = 1024 * 1024
BF = jnp.bfloat16
F32 = jnp.float32
VMEM = pl.BlockSpec(memory_space=pltpu.VMEM)
SMEM = pl.BlockSpec(memory_space=pltpu.SMEM)
HBM = pl.BlockSpec(memory_space=pltpu.HBM)
NN = (((1,), (0,)), ((), ()))
NT = (((1,), (1,)), ((), ()))
TN = (((0,), (0,)), ((), ()))


def mm(left, right, dims=NN, precision=None):
    return lax.dot_general(left, right, dims, precision, preferred_element_type=F32)


def call(body, outs, ins, scratch, cost, name, limit):
    flops, moved = cost
    return pl.pallas_call(
        body,
        out_shape=[jax.ShapeDtypeStruct(shape, dtype) for shape, dtype, _ in outs],
        out_specs=[spec for _, _, spec in outs],
        in_specs=ins,
        scratch_shapes=scratch,
        compiler_params=pltpu.CompilerParams(vmem_limit_bytes=limit * MIB),
        cost_estimate=pl.CostEstimate(flops=flops, bytes_accessed=moved, transcendentals=0),
        name=name,
    )


def own_place():
    seq = lax.axis_index("seq")
    return lax.axis_index("dp") * 4 + seq, seq


def slot_rows(core, layer, place, me):
    device = lax.bitwise_xor(jnp.int32((layer * 2 + core) * 4 + place), me)
    return pl.ds(pl.multiple_of(device * BAND, BAND), BAND)


def plain_layout(pieces):
    return [(core, layer, 0, pieces) for core in range(2) for layer in range(4)]


def split_layout(pieces):
    half = pieces // 2
    per_core = [(layer, 0, pieces) for layer in range(3)] + [(3, 0, half), (3, half, half)]
    return [(core,) + item for core in range(2) for item in per_core]


def fetch_weights(layout, parts, weights, sem, me):
    for (core, layer, first, count), part in zip(layout, parts):
        for place in range(4):
            rows = slot_rows(core, layer, place, me)
            target = weights.at[pl.ds(first, count), rows, :]
            pltpu.make_async_copy(part.at[place], target, sem).start()


def store_slots(grads, parts, sem, me):
    for core in range(2):
        for layer in range(4):
            for place in range(4):
                slot = parts[4].at[layer * 4 + place] if core else parts[layer].at[place]
                rows = slot_rows(core, layer, place, me)
                pltpu.make_async_copy(grads.at[:, rows, :], slot, sem).start()
    pltpu.make_async_copy(grads, grads, sem).wait()


def has_long(seq):
    return (seq == 1) | (seq == 2)


def pick(seq, *options):
    chosen = options[-1]
    for i in range(len(options) - 2, -1, -1):
        chosen = jnp.where(seq == i, options[i], chosen)
    return chosen


def pad_rows(part, rows):
    return jnp.concatenate([part, jnp.zeros((rows - part.shape[0], part.shape[1]), part.dtype)], 0)


def pack_body(with_weights, *refs):
    me, seq = own_place()
    count = 13 if with_weights else 4
    sources, refs = (refs[:count], refs[count:])
    outs = 5 if with_weights else 3
    targets, held, sem = (refs[:outs], refs[outs : outs + count], refs[-1])
    pay1, pay2, pay3 = targets[:3]
    ins = [
        pltpu.make_async_copy(source, there, sem.at[i])
        for i, (source, there) in enumerate(zip(sources, held))
    ]
    for item in ins:
        item.start()
    long_tok, short_tok, long_cot, short_cot = held[:4]
    n_long, n_short = (long_tok.shape[1], short_tok.shape[1])
    copies = []

    def copy(source, target):
        item = pltpu.make_async_copy(source, target, sem.at[len(copies)])
        item.start()
        copies.append(item)

    if with_weights:
        early, late = targets[3:]
        row = refs[outs + count]
        width = early.shape[2]
        gain, bias = held[11:]
        shard = gain.shape[1]
        col = lax.broadcasted_iota(jnp.int32, (shard, width), 1)
        at = lax.broadcasted_iota(jnp.int32, (shard, width), 0)
        spread = (col == at + me * shard).astype(BF)
    for item in ins:
        item.wait()
    if with_weights:
        wq, wk, wv, pos, wo, up, down = held[4:11]
        chunks = up.shape[1] // width
        vectors = jnp.concatenate([mm(gain[...], spread), mm(bias[...], spread)], 0)
        row[...] = pad_rows(vectors, BAND).astype(BF)
        for i, weight in enumerate((wq, wk, wv, pos)):
            copy(weight, early.at[i])
        copy(wo, late.at[0])
        for c in range(chunks):
            cols = pl.ds(c * width, width)
            copy(up.at[:, cols], late.at[1 + c])
            copy(down.at[:, cols], late.at[1 + chunks + c])
        copy(row, late.at[1 + 2 * chunks])
    last = len(copies)

    def rest(pairs):
        ends = [
            pltpu.make_async_copy(source, target, sem.at[last + i])
            for i, (source, target) in enumerate(pairs)
        ]
        for item in ends:
            item.start()
        for item in ends:
            item.wait()

    def halves(pay, one, two, rows):
        half = pay.shape[0] // 2
        return [(one, pay.at[pl.ds(0, rows), :]), (two, pay.at[pl.ds(half, rows), :])]

    longs = [long_tok.at[0], long_cot.at[0], n_long]
    zeros, ones = ([short_tok.at[i], short_cot.at[i], n_short] for i in range(2))
    plans = (
        halves(pay1, *longs) + [(long_tok.at[0], pay2)] + halves(pay3, *ones),
        halves(pay1, *zeros) + halves(pay2, *ones) + [(long_tok.at[0], pay3)],
        halves(pay1, *ones) + halves(pay2, *zeros),
        halves(pay1, *longs) + halves(pay3, *zeros),
    )
    for place, plan in enumerate(plans):

        @pl.when(seq == place)
        def _(plan=plan):
            rest(plan)

    for item in copies:
        item.wait()


def stack_heads(block, lane):
    zero = jnp.zeros_like(block)
    return jnp.concatenate([jnp.where(lane, block, zero), jnp.where(lane, zero, block)], 0)


def join_heads(stacked, lane):
    half = stacked.shape[0] // 2
    return jnp.where(lane, stacked[:half], stacked[half:])


def head_lanes():
    return lax.broadcasted_iota(jnp.int32, (1, LANES), 1) < HEAD_DIM


def block_base(seq, k, size):
    owner = lax.bitwise_xor(seq, jnp.int32(k))
    return pl.multiple_of(owner * jnp.where(has_long(seq), size, size // 2), size // 2)


def gather_queries(seq, source, target):
    size = source.shape[0] // 4
    half = size // 2

    @pl.when(seq == 1)
    def _():
        target[:size, :] = source[size : 2 * size, :]
        target[size:, :] = source[:size, :]

    @pl.when(seq == 2)
    def _():
        target[...] = source[: 2 * size, :]

    @pl.when((seq == 0) | (seq == 3))
    def _():
        for k in range(4):
            target[k * half : (k + 1) * half, :] = source[k * size : k * size + half, :]


def spread_queries(seq, value, target):
    size = target.shape[0] // 4
    half = size // 2

    @pl.when(seq == 1)
    def _():
        target[size : 2 * size, :] += value[:size]
        target[:size, :] += value[size:]

    @pl.when(seq == 2)
    def _():
        target[: 2 * size, :] += value

    @pl.when((seq == 0) | (seq == 3))
    def _():
        for k in range(4):
            target[k * size : k * size + half, :] += value[k * half : (k + 1) * half]


def row_blocks(seq, whole, shorts, one, two, three):
    rows, half = (whole.shape[1], shorts.shape[1])
    longs = has_long(seq)
    own_short = pad_rows(jnp.where(seq == 0, shorts[0], shorts[1]), rows)
    return (
        jnp.where(longs, whole[0], own_short),
        jnp.where(longs, one, pad_rows(one[:half], rows)),
        two,
        three,
    )


def attend_body(direct, layout, long_len, short_len, *refs):
    count = len(layout)
    long_tok, short_tok, got1, got2, got3 = refs[:5]
    parts, refs = (refs[5 : 5 + count], refs[5 + count :])
    first_o, low_o, lowq_o, q_o, k_o, v_o, probs_o, mix_o = refs[:8]
    weights, table, first, sem = refs[8:]
    me, seq = own_place()
    me = me if direct else jnp.int32(0)
    fetch_weights(layout, parts, weights, sem, me)
    n_long, n_short = (long_tok.shape[1], short_tok.shape[1])
    longs = has_long(seq)
    two, three = (
        jnp.where(longs, got[...], pad_rows(got[:n_short, :], n_long)) for got in (got2, got3)
    )
    blocks = row_blocks(seq, long_tok, short_tok, got1[:n_long, :], two, three)
    for k, block in enumerate(blocks):
        first[k * n_long : (k + 1) * n_long, :] = block.astype(F32)
    pltpu.make_async_copy(weights, weights, sem).wait()
    table[...] = weights[3].astype(F32).T
    for k in range(4):
        rows = slice(k * n_long, (k + 1) * n_long)
        first[rows, :] += table[pl.ds(block_base(seq, k, n_long), n_long), :]
    gather_queries(seq, first, first_o)
    lowq_o[...] = first_o[...].astype(BF)
    low_o[...] = first[...].astype(BF)
    k_o[...] = mm(low_o[...], weights[1]).astype(BF)
    v_o[...] = mm(low_o[...], weights[2]).astype(BF)
    q_o[...] = mm(lowq_o[...], weights[0]).astype(BF) * BF(HEAD_DIM**-0.5)
    rows, keys = (first_o.shape[0], first.shape[0])
    row = lax.broadcasted_iota(jnp.int32, (rows, 1), 0)
    row_pos = jnp.where(
        longs,
        row + (seq - 1) * rows,
        lax.bitwise_xor(row // n_short, jnp.full_like(row, seq)) * n_short + row % n_short,
    )
    row_pos = jnp.concatenate([row_pos, row_pos], 0)
    col = lax.broadcasted_iota(jnp.int32, (1, keys), 1)
    owner = lax.bitwise_xor(col // n_long, jnp.full_like(col, seq))
    inner = col % n_long
    col_pos = jnp.where(longs, owner * n_long + inner, owner * n_short + inner)
    length = pick(seq, short_len[0], long_len[0], long_len[0], short_len[1])
    seen = (col_pos < length) & (longs | (inner < n_short))
    col_pos = jnp.where(seen, col_pos, jnp.int32(1 << 20))
    allowed = col_pos <= row_pos
    lane = head_lanes()
    for g in range(first_o.shape[1] // LANES):
        cols = slice(g * LANES, (g + 1) * LANES)
        scores = mm(stack_heads(q_o[:, cols], lane), k_o[:, cols], NT)
        scores = jnp.where(allowed, scores, -1e30)
        shifted = jnp.exp(scores - jnp.max(scores, axis=-1, keepdims=True))
        probs_o[g] = (shifted / jnp.sum(shifted, axis=-1, keepdims=True)).astype(BF)
        mix_o[:, cols] = join_heads(mm(probs_o[g], v_o[:, cols]), lane).astype(BF)


def norm_parts(values):
    mean = jnp.mean(values, axis=-1, keepdims=True)
    centred = values - mean
    scale = lax.rsqrt(jnp.mean(centred * centred, axis=-1, keepdims=True) + 1e-05)
    return centred * scale, scale


def norm_back(cot, gain, xhat, scale):
    scaled = cot * gain
    mean = jnp.mean(scaled, axis=-1, keepdims=True)
    inner = jnp.mean(scaled * xhat, axis=-1, keepdims=True)
    return scale * (scaled - mean - xhat * inner)


def middle_body(direct, layout, first, mixed, long_cot, short_cot, *refs):
    count = len(layout)
    got1, got2, got3 = refs[:3]
    parts, refs = (refs[3 : 3 + count], refs[3 + count :])
    out_o, gsum_o, gmix_o = refs[:3]
    grad_parts = refs[3:8]
    weights, grads, act, slope, blocks, cots, sem = refs[8:]
    me, seq = own_place()
    me = me if direct else jnp.int32(0)
    fetch_weights(layout, parts, weights, sem, me)
    n_long, n_short = (long_cot.shape[1], short_cot.shape[1])
    two, three = (pad_rows(got[n_short:, :], n_long) for got in (got2, got3))
    found = row_blocks(seq, long_cot, short_cot, got1[n_long:, :], two, three)
    for k, block in enumerate(found):
        blocks[k * n_long : (k + 1) * n_long, :] = block.astype(F32)
    gather_queries(seq, blocks, cots)
    blocks[...] = jnp.zeros_like(blocks)
    pltpu.make_async_copy(weights, weights, sem).wait()
    width = first.shape[1]
    chunks = (weights.shape[0] - 2) // 2
    norm = weights.shape[0] - 1
    vectors = jnp.sum(weights[norm].astype(F32).reshape(-1, BAND, width), axis=0)
    gain0, gain1, bias0, bias1 = (vectors[i : i + 1] for i in range(4))
    mixed_low = mixed[...]
    xhat0, scale0 = norm_parts(first[...] + mm(mixed_low, weights[0]))
    normed = xhat0 * gain0 + bias0
    normed_low = normed.astype(BF)
    second = normed
    for c in range(chunks):
        hidden = mm(normed_low, weights[1 + c])
        cdf = 0.5 + 0.5 * lax.erf(hidden * (0.5**0.5))
        slope[c] = cdf + hidden * jnp.exp(-0.5 * hidden * hidden) * ((2 * math.pi) ** -0.5)
        act[c] = (hidden * cdf).astype(BF)
        second = second + mm(act[c], weights[1 + chunks + c], NT)
    xhat1, scale1 = norm_parts(second)
    spread_queries(seq, xhat1 * gain1 + bias1, blocks)
    out_o[...] = blocks[...].astype(BF)
    cot_wide = cots[...]
    grad_second = norm_back(cot_wide, gain1, xhat1, scale1)
    second_low = grad_second.astype(BF)
    grad_normed = grad_second
    for c in range(chunks):
        hidden_low = (mm(second_low, weights[1 + chunks + c]) * slope[c]).astype(BF)
        grads[1 + chunks + c] = mm(second_low, act[c], TN).astype(BF)
        grads[1 + c] = mm(normed_low, hidden_low, TN).astype(BF)
        grad_normed = grad_normed + mm(hidden_low, weights[1 + c], NT)
    grad_sum = norm_back(grad_normed, gain0, xhat0, scale0)
    gsum_o[...] = grad_sum
    sum_low = grad_sum.astype(BF)
    gmix_o[...] = mm(sum_low, weights[0], NT).astype(BF)
    grads[0] = mm(mixed_low, sum_low, TN).astype(BF)
    terms = jnp.concatenate(
        [
            jnp.sum(grad_normed * xhat0, axis=0, keepdims=True),
            jnp.sum(cot_wide * xhat1, axis=0, keepdims=True),
            jnp.sum(grad_normed, axis=0, keepdims=True),
            jnp.sum(cot_wide, axis=0, keepdims=True),
            jnp.zeros((BAND - 4, width), F32),
        ],
        0,
    ).astype(BF)
    for d in range(width // BAND):
        grads[norm, d * BAND : (d + 1) * BAND, :] = terms
    store_slots(grads, grad_parts, sem, me)


def attend_back_body(gmix, q, k, v, probs_i, dq_o, dk_o, dv_o):
    lane = head_lanes()
    scale = HEAD_DIM**-0.5
    for g in range(gmix.shape[1] // LANES):
        cols = slice(g * LANES, (g + 1) * LANES)
        grads = stack_heads(gmix[:, cols], lane)
        queries = stack_heads(q[:, cols], lane)
        probs = probs_i[g]
        grad_probs = mm(grads, v[:, cols], NT)
        wide = probs.astype(F32)
        inner = jnp.sum(wide * grad_probs, axis=-1, keepdims=True)
        grad_scores = (wide * (grad_probs - inner)).astype(BF)
        grad_q = mm(grad_scores, k[:, cols])
        dq_o[:, cols] = (join_heads(grad_q, lane) * scale).astype(BF)
        dk_o[:, cols] = mm(grad_scores, queries, TN).astype(BF)
        dv_o[:, cols] = mm(probs, grads, TN).astype(BF)


def leave_body(direct, layout, low, lowq, dq, dk, dv, gsum, outs, *refs):
    count = len(layout)
    parts, refs = (refs[:count], refs[count:])
    own_o, sent1_o, sent2_o, sent3_o = refs[:4]
    grad_parts = refs[4:9]
    weights, grads, table, back, sem = refs[9:]
    me, seq = own_place()
    me = me if direct else jnp.int32(0)
    fetch_weights(layout, parts, weights, sem, me)
    grads[0] = mm(lowq[...], dq[...], TN).astype(BF)
    grads[1] = mm(low[...], dk[...], TN).astype(BF)
    grads[2] = mm(low[...], dv[...], TN).astype(BF)
    pltpu.make_async_copy(weights, weights, sem).wait()
    back[...] = mm(dk[...], weights[1], NT) + mm(dv[...], weights[2], NT)
    spread_queries(seq, gsum[...] + mm(dq[...], weights[0], NT), back)
    size = own_o.shape[0]
    table[...] = jnp.zeros_like(table)
    for k, target in enumerate((own_o, sent1_o, sent2_o, sent3_o)):
        piece = back[k * size : (k + 1) * size, :]
        target[:size, :] = piece.astype(target.dtype)
        if k == 1:
            target[size:, :] = outs[size : 2 * size, :]
        elif k > 1:
            both = jnp.concatenate([piece[: size // 2].astype(BF), outs[k * size : k * size + size // 2, :]], 0)
            target[...] = jnp.where(has_long(seq), piece.astype(BF), both)
        table[pl.ds(block_base(seq, k, size), size), :] += piece
    grads[3] = table[...].T.astype(BF)
    store_slots(grads, grad_parts, sem, me)


def return_rows(own, outs, got1, got2, got3, long_grad, short_grad, long_out, short_out):
    seq = own_place()[1]
    size, half = (long_grad.shape[1], short_grad.shape[1])
    for i, (mine, long_o, short_o) in enumerate(((own, long_grad, short_grad), (outs, long_out, short_out))):
        mine = mine[:size, :].astype(F32)
        one = got1[i * size : (i + 1) * size, :].astype(F32)
        if i == 0:
            two, three = (got[...].astype(F32) for got in (got2, got3))
            long_o[0] = pick(seq, one + two, mine + three, mine, one).astype(BF)
        else:
            long_o[0] = pick(seq, one, mine, mine, one).astype(BF)
        two, three = (got[i * half : (i + 1) * half, :].astype(F32) for got in (got2, got3))
        mine, one = (mine[:half], one[:half])
        short_o[0] = pick(seq, mine, one, two, three).astype(BF)
        short_o[1] = pick(seq, three, two, one, mine).astype(BF)


def wide(ref, *index):
    return ref[index].astype(F32)


def sum_call(body, outs, ins, blocks_in, steps, name):
    def spec(shape, axis):
        block = tuple(1 if i == axis else size for i, size in enumerate(shape))
        return pl.BlockSpec(block, lambda i: tuple(i if a == axis else 0 for a in range(len(shape))))

    return pl.pallas_call(
        body,
        grid=(steps,),
        out_shape=[jax.ShapeDtypeStruct(shape, dtype) for shape, dtype, _ in outs],
        in_specs=blocks_in,
        out_specs=[spec(shape, axis) for shape, _, axis in outs],
        compiler_params=pltpu.CompilerParams(vmem_limit_bytes=16 * MIB),
        name=name,
    )(*ins)


def one_place(part, layer=0):
    shape = part.shape
    return pl.BlockSpec((1,) + shape[1:], lambda i: (layer * 4 + i,) + (0,) * (len(shape) - 1))


def first_sums_body(half, near1, near2, near3, far1, far2, far3, to_x, to_y):
    to_y[0, 0] = (wide(near2, 0)[:half] + wide(far2, 0)[:half]).astype(BF)
    to_y[1, 0] = (wide(near3, 0)[:half] + wide(far3, 0)[:half]).astype(BF)
    to_x[0, 0] = (wide(near1, 0)[half:] + wide(far1, 0)[half:]).astype(BF)
    to_x[1, 0] = (wide(near3, 0)[half:] + wide(far3, 0)[half:]).astype(BF)


def second_sums_body(half, near1, near2, far1, far2, from_x, from_y, to_x, to_y):
    to_x[0] = (wide(near1, 0)[:half] + wide(far1, 0)[:half] + wide(from_y, 0, 0)).astype(BF)
    to_y[0] = (wide(near2, 0)[half:] + wide(far2, 0)[half:] + wide(from_x, 0, 0)).astype(BF)


def last_sums_body(half, near0, far0, from_x, from_y, then_x, then_y, *outs):
    for place, out in enumerate(outs):
        low = wide(near0, place)[:half] + wide(far0, place)[:half]
        low = low + (wide(from_y, 0, place) + wide(then_x, place))
        out[:half] = low.astype(out.dtype)
        high = wide(near0, place)[half:] + wide(far0, place)[half:]
        high = high + (wide(from_x, 0, place) + wide(then_y, place))
        out[half:] = high.astype(out.dtype)


def four_sums_body(*refs):
    ins, outs = (refs[:-4], refs[-4:])
    for place, out in enumerate(outs):
        total = wide(ins[0], place)
        for item in ins[1:]:
            total = total + wide(item, place)
        out[...] = total.astype(out.dtype)


def cut_sums(body, parts, pieces, name):
    _, _, band, width = parts[0].shape

    def whole(part):
        shape = part.shape
        shape = (1,) + shape[1:] if len(shape) == 5 else (4,) + shape[1:]
        return pl.BlockSpec(shape, lambda i: (0,) * len(shape))

    out = pl.BlockSpec((pieces, band, width), lambda i: (0, 0, 0))
    return pl.pallas_call(
        body,
        grid=(1,),
        out_shape=[
            jax.ShapeDtypeStruct((pieces, band, width), F32 if place == 0 else BF)
            for place in range(4)
        ],
        in_specs=[whole(part) for part in parts],
        out_specs=[out] * 4,
        compiler_params=pltpu.CompilerParams(vmem_limit_bytes=24 * MIB),
        name=name,
    )(*parts)


def finish_body(*refs):
    late, early, rows = (refs[:4], refs[4:8], refs[8:13])
    row_outs, early_outs = (refs[13:17], refs[17:21])
    out_o, up_o, down_o, norm_o = refs[21:]
    width = out_o.shape[1]
    chunks = up_o.shape[1] // width

    def total(parts, i):
        own, one, two, three = parts
        return own[i] + (one[i].astype(F32) + two[i].astype(F32) + three[i].astype(F32))

    return_rows(*rows, *row_outs)
    out_o[...] = total(late, 0)
    for c in range(chunks):
        up_o[:, c * width : (c + 1) * width] = total(late, 1 + c)
        down_o[:, c * width : (c + 1) * width] = total(late, 1 + chunks + c)
    shard = norm_o.shape[1]
    row = lax.broadcasted_iota(jnp.int32, (width, shard), 0)
    col = lax.broadcasted_iota(jnp.int32, (width, shard), 1)
    chosen = (row == col + own_place()[0] * shard).astype(F32)
    norm_o[...] = mm(total(late, 1 + 2 * chunks), chosen, NN, lax.Precision.HIGHEST)
    for i, out in enumerate(early_outs):
        out[...] = total(early, i)


def after(value, *others):
    return lax.optimization_barrier((value,) + others)[0]


def local(
    dp_count,
    seq_count,
    long_tokens,
    short_tokens,
    long_cot,
    short_cot,
    long_lengths,
    short_lengths,
    w_query,
    w_key,
    w_value,
    w_out,
    w_up,
    w_down,
    pos_table,
    norm_gain,
    norm_bias,
):
    width = w_key.shape[1]
    hidden = w_up.shape[1]
    chunks = hidden // width
    shard = w_key.shape[0]
    direct = shard == BAND and dp_count == 8
    layers = 4
    device = lax.axis_index("dp") * seq_count + lax.axis_index("seq")
    n_long, n_short = (long_tokens.shape[1], short_tokens.shape[1])
    rows, keys = (2 * n_long, 4 * n_long)
    square = width * width
    early_pieces, late_pieces = (4, 2 + 2 * chunks)

    def swap_seq(value, mask, keep=lambda source, target: True):
        pairs = [(i, i ^ mask) for i in range(seq_count) if keep(i, i ^ mask)]
        return lax.ppermute(value, "seq", pairs)

    def swap_dp(value, mask):
        return lax.ppermute(value, "dp", [(i, i ^ mask) for i in range(dp_count)])

    acts = [long_tokens, short_tokens, long_cot, short_cot]
    packed = [
        ((2 * n_long, width), BF, HBM),
        ((n_long, width), BF, HBM),
        ((n_long, width), BF, HBM),
    ]
    own, specs, scratch = ([], [HBM] * 4, [])
    held = list(acts)
    if direct:
        own = [w_query, w_key, w_value, pos_table.T, w_out, w_up, w_down.T]
        own += [norm_gain, norm_bias]
        held += own
        packed += [((count, BAND, width), BF, HBM) for count in (early_pieces, late_pieces)]
        specs += [HBM] * 9
        scratch = [pltpu.VMEM((BAND, width), BF)]
    pays = call(
        functools.partial(pack_body, direct),
        packed,
        specs,
        [pltpu.VMEM(item.shape, BF) for item in held] + scratch + [pltpu.SemaphoreType.DMA((32,))],
        (0, 4 * MIB),
        "pack",
        60,
    )(*acts, *own)
    pay1, pay2, pay3 = pays[:3]

    def to_slots(whole):
        count = whole.shape[0]
        cut = whole.reshape(count, 4, 2, 4, BAND, width).transpose(2, 1, 3, 0, 4, 5)
        return [cut[core, outer] for core in range(2) for outer in range(4)]

    def slot_outs(pieces):
        near = ((4, pieces, BAND, width), BF, HBM)
        return [near] * layers + [((4 * layers, pieces, BAND, width), BF, HBM)]

    def from_slots(parts):
        count = parts[0].shape[1]
        cut = jnp.concatenate(parts, 0).reshape(2, 4, 4, count, BAND, width)
        return cut.transpose(3, 1, 0, 2, 4, 5).reshape(count, width, width)

    def places(piece):
        return [piece] + [swap_seq(piece, k) for k in range(1, 4)]

    def spread(column):
        near = [column] + [swap_dp(column, 2 * k) for k in range(1, layers)]
        return near

    def cross(near):
        return list(near) + [swap_dp(part, 1) for part in near]

    early_layout = plain_layout(early_pieces)
    late_layout = split_layout(late_pieces) if direct else plain_layout(late_pieces)
    if direct:
        early, late = pays[3:]
        early_places = places(early)
        late = after(late, *early_places)
        late_places = places(late)
        early_near = spread(jnp.stack(early_places))
        column = jnp.stack(late_places)
        column = after(column, *early_near)
        pay1, pay2, pay3 = lax.optimization_barrier((pay1, pay2, pay3, *late_places))[:3]
        got1, got2, got3 = (
            swap_seq(pay1, 1),
            swap_seq(pay2, 2, lambda source, target: target != 1),
            swap_seq(pay3, 3, lambda source, target: target != 1),
        )
        early_full = early_near + cross(lax.optimization_barrier((early_near, got1, got2, got3))[0])[4:]
        half = late_pieces // 2
        near1, near2 = (swap_dp(column, 2), swap_dp(column, 4))
        near3 = [swap_dp(near1[:, :half], 4), swap_dp(near2[:, half:], 2)]
        late_full = cross([column, near1, near2] + near3)
    if not direct:
        got1, got2, got3 = (
            swap_seq(pay1, 1),
            swap_seq(pay2, 2, lambda source, target: target != 1),
            swap_seq(pay3, 3, lambda source, target: target != 1),
        )

        def columns(weight):
            return weight.reshape(weight.shape[0], chunks, width).transpose(1, 0, 2)

        def whole(pieces):
            return lax.all_gather(pieces, ("dp", "seq"), axis=1, tiled=True)

        early_full = to_slots(whole(jnp.stack([w_query, w_key, w_value, pos_table.T])))
        vectors = jnp.concatenate([norm_gain, norm_bias], 0)
        vectors = lax.all_gather(vectors, ("dp", "seq"), axis=1, tiled=True)
        vectors = jnp.pad(vectors, ((0, width - 4), (0, 0)))
        late_whole = whole(jnp.concatenate([w_out[None], columns(w_up), columns(w_down.T)], 0))
        late_full = to_slots(jnp.concatenate([late_whole, vectors[None]], 0))

    groups = width // LANES
    first, low, low_queries, queries, key_rows, values, probs, mixed = call(
        functools.partial(attend_body, direct, early_layout),
        [
            ((rows, width), F32, VMEM),
            ((keys, width), BF, VMEM),
            ((rows, width), BF, VMEM),
            ((rows, width), BF, VMEM),
            ((keys, width), BF, VMEM),
            ((keys, width), BF, VMEM),
            ((groups, 2 * rows, keys), BF, VMEM),
            ((rows, width), BF, VMEM),
        ],
        [SMEM] * 2 + [VMEM] * 5 + [HBM] * len(early_layout),
        [
            pltpu.VMEM((early_pieces, width, width), BF),
            pltpu.VMEM((width, width), F32),
            pltpu.VMEM((keys, width), F32),
            pltpu.SemaphoreType.DMA,
        ],
        (8 * keys * square, 10 * MIB),
        "attend",
        24,
    )(long_lengths, short_lengths, long_tokens, short_tokens, got1, got2, got3, *early_full)

    block = (n_long, width)
    middle_outs = call(
        functools.partial(middle_body, direct, late_layout),
        [((keys, width), BF, VMEM)]
        + [((rows, width), F32, VMEM), ((rows, width), BF, VMEM)]
        + slot_outs(late_pieces),
        [VMEM] * 7 + [HBM] * len(late_layout),
        [
            pltpu.VMEM((late_pieces, width, width), BF),
            pltpu.VMEM((late_pieces, width, width), BF),
            pltpu.VMEM((chunks, rows, width), BF),
            pltpu.VMEM((chunks, rows, width), F32),
            pltpu.VMEM((keys, width), F32),
            pltpu.VMEM((rows, width), F32),
            pltpu.SemaphoreType.DMA,
        ],
        (16 * rows * square * chunks, 20 * MIB),
        "middle",
        32,
    )(first, mixed, long_cot, short_cot, got1, got2, got3, *late_full)
    out_blocks, grad_sum, grad_mixed = middle_outs[:3]
    late_parts = middle_outs[3:]

    def core_sums(parts, arrived):
        return [
            (parts[k].astype(F32) + arrived[4 * k : 4 * k + 4].astype(F32)).astype(BF)
            for k in range(1, layers)
        ]

    if direct:
        late_arrived = swap_dp(late_parts[-1], 1)

    grad_q, grad_k, grad_v = call(
        attend_back_body,
        [
            ((rows, width), BF, VMEM),
            ((keys, width), BF, VMEM),
            ((keys, width), BF, VMEM),
        ],
        [VMEM] * 5,
        [],
        (8 * keys * square, 8 * MIB),
        "attend_back",
        24,
    )(grad_mixed, queries, key_rows, values, probs)
    leave_outs = call(
        functools.partial(leave_body, direct, early_layout),
        [(block, F32, VMEM), ((2 * n_long, width), BF, VMEM)] + [(block, BF, VMEM)] * 2 + slot_outs(early_pieces),
        [VMEM] * 7 + [HBM] * len(early_layout),
        [
            pltpu.VMEM((early_pieces, width, width), BF),
            pltpu.VMEM((early_pieces, width, width), BF),
            pltpu.VMEM((width, width), F32),
            pltpu.VMEM((keys, width), F32),
            pltpu.SemaphoreType.DMA,
        ],
        (10 * keys * square, 8 * MIB),
        "leave",
        24,
    )(low, low_queries, grad_q, grad_k, grad_v, grad_sum, out_blocks, *early_full)
    grad_blocks, early_parts = (leave_outs[:4], leave_outs[4:])

    back = lambda source, target: source != 1
    got = [swap_seq(grad_blocks[1], 1)] + [swap_seq(grad_blocks[k], k, back) for k in (2, 3)]
    row_outs = [(item.shape, BF, VMEM) for item in (long_tokens, short_tokens)] * 2
    if direct:
        half = late_pieces // 2
        near0, near1, near2, near3 = late_parts[:4]
        far = late_arrived
        pair = ((2, 4, half, BAND, width), BF, 1)
        single = ((4, half, BAND, width), BF, 0)
        to_x, to_y = sum_call(
            functools.partial(first_sums_body, half),
            [pair, pair],
            [near1, near2, near3, far, far, far],
            [one_place(item) for item in (near1, near2, near3)] + [one_place(far, k) for k in (1, 2, 3)],
            4,
            "late_sums_1",
        )
        from_x, from_y = (swap_dp(to_x, 2), swap_dp(to_y, 4))
        second = pl.BlockSpec((1, 1, half, BAND, width), lambda i: (1, i, 0, 0, 0))
        then_x, then_y = sum_call(
            functools.partial(second_sums_body, half),
            [single, single],
            [near1, near2, far, far, from_x, from_y],
            [one_place(near1), one_place(near2), one_place(far, 1), one_place(far, 2), second, second],
            4,
            "late_sums_2",
        )
        early_far = after(early_parts[-1], to_x)
        early_arrived = swap_dp(early_far, 1)
        early_sums = core_sums(early_parts, early_arrived)
        then_x, then_y, early_sums = lax.optimization_barrier((then_x, then_y, early_sums))
        then_x, then_y = (swap_dp(then_x, 2), swap_dp(then_y, 4))
        early_layers = [swap_dp(part, 2 * k) for k, part in enumerate(early_sums, 1)]
        then_x, then_y, got = lax.optimization_barrier((then_x, then_y, got))
        late_cut = cut_sums(
            functools.partial(last_sums_body, half),
            [near0, far, from_x, from_y, then_x, then_y],
            late_pieces,
            "late_sums_3",
        )
        late_ends = [late_cut[0]] + [swap_seq(late_cut[k], k) for k in range(1, 4)]
        early_cut = cut_sums(
            four_sums_body, [early_parts[0], early_arrived] + early_layers, early_pieces, "early_sums"
        )
        early_ends = [early_cut[0]] + [swap_seq(early_cut[k], k) for k in range(1, 4)]
        row_ins = [grad_blocks[0], out_blocks, *got]
        ends = call(
            finish_body,
            row_outs
            + [((shard, width), F32, VMEM)] * 5
            + [((shard, hidden), F32, VMEM)] * 2
            + [((BAND, shard), F32, VMEM)],
            [VMEM] * 13,
            [],
            (0, MIB),
            "finish",
            16,
        )(*late_ends, *early_ends, *row_ins)
        row_grads, early_sum, (grad_out, grad_up, grad_down, norms) = (ends[:4], ends[4:8], ends[8:])
    else:

        def scatter(parts):
            whole_sum = from_slots(parts).astype(F32)
            return lax.psum_scatter(whole_sum, ("dp", "seq"), scatter_dimension=1, tiled=True)

        def join(pieces):
            return pieces.transpose(1, 0, 2).reshape(shard, hidden)

        late_sum = scatter(late_parts)
        early_sum = scatter(early_parts)
        grad_out, grad_up, grad_down = (
            late_sum[0],
            join(late_sum[1 : 1 + chunks]),
            join(late_sum[1 + chunks : 1 + 2 * chunks]),
        )
        norms = lax.psum(from_slots(late_parts)[-1, :BAND].astype(F32), ("dp", "seq"))
        norms = lax.dynamic_slice(norms, (0, device * shard), (BAND, shard))
        row_grads = call(
            return_rows, row_outs, [VMEM] * 5, [], (0, MIB), "return", 16
        )(grad_blocks[0], out_blocks, *got)
    long_grad, short_grad, long_out, short_out = row_grads
    return (
        long_out,
        short_out,
        long_grad,
        short_grad,
        early_sum[0],
        early_sum[1],
        early_sum[2],
        grad_out,
        grad_up,
        grad_down.T,
        early_sum[3].T,
        norms[:2],
        norms[2:4],
    )


def solution(mesh):
    rows = P(("dp", "seq"), None)
    cols = P(None, ("dp", "seq"))
    acts = P("dp", "seq", None)
    return jax.shard_map(
        functools.partial(local, mesh.shape["dp"], mesh.shape["seq"]),
        mesh=mesh,
        in_specs=(acts,) * 4 + (P("dp"),) * 2 + (rows,) * 5 + (cols,) * 4,
        out_specs=(acts,) * 4 + (rows,) * 5 + (cols,) * 4,
        check_vma=False,
    )
```

```python
import functools
import math

import jax
import jax.numpy as jnp
from jax import lax
from jax.experimental import pallas as pl
from jax.experimental.pallas import tpu as pltpu
from jax.sharding import PartitionSpec as P

HEAD_DIM = 64
LANES = 128
BAND = 16
MIB = 1024 * 1024
BF = jnp.bfloat16
F32 = jnp.float32
VMEM = pl.BlockSpec(memory_space=pltpu.VMEM)
SMEM = pl.BlockSpec(memory_space=pltpu.SMEM)
HBM = pl.BlockSpec(memory_space=pltpu.HBM)
NN = (((1,), (0,)), ((), ()))
NT = (((1,), (1,)), ((), ()))
TN = (((0,), (0,)), ((), ()))


def mm(left, right, dims=NN, precision=None):
    return lax.dot_general(left, right, dims, precision, preferred_element_type=F32)


def call(body, outs, ins, scratch, cost, name, limit):
    flops, moved = cost
    return pl.pallas_call(
        body,
        out_shape=[jax.ShapeDtypeStruct(shape, dtype) for shape, dtype, _ in outs],
        out_specs=[spec for _, _, spec in outs],
        in_specs=ins,
        scratch_shapes=scratch,
        compiler_params=pltpu.CompilerParams(vmem_limit_bytes=limit * MIB),
        cost_estimate=pl.CostEstimate(flops=flops, bytes_accessed=moved, transcendentals=0),
        name=name,
    )


def own_place():
    seq = lax.axis_index("seq")
    return lax.axis_index("dp") * 4 + seq, seq


def slot_rows(core, layer, place, me):
    device = lax.bitwise_xor(jnp.int32((layer * 2 + core) * 4 + place), me)
    return pl.ds(pl.multiple_of(device * BAND, BAND), BAND)


def plain_layout(pieces):
    return [(core, layer, 0, pieces) for core in range(2) for layer in range(4)]


def split_layout(pieces):
    half = pieces // 2
    per_core = [(layer, 0, pieces) for layer in range(3)] + [(3, 0, half), (3, half, half)]
    return [(core,) + item for core in range(2) for item in per_core]


def fetch_weights(layout, parts, weights, sem, me):
    for (core, layer, first, count), part in zip(layout, parts):
        for place in range(4):
            rows = slot_rows(core, layer, place, me)
            target = weights.at[pl.ds(first, count), rows, :]
            pltpu.make_async_copy(part.at[place], target, sem).start()


def store_slots(grads, parts, sem, me):
    for core in range(2):
        for layer in range(4):
            for place in range(4):
                slot = parts[4].at[layer * 4 + place] if core else parts[layer].at[place]
                rows = slot_rows(core, layer, place, me)
                pltpu.make_async_copy(grads.at[:, rows, :], slot, sem).start()
    pltpu.make_async_copy(grads, grads, sem).wait()


def has_long(seq):
    return (seq == 1) | (seq == 2)


def pick(seq, *options):
    chosen = options[-1]
    for i in range(len(options) - 2, -1, -1):
        chosen = jnp.where(seq == i, options[i], chosen)
    return chosen


def pad_rows(part, rows):
    return jnp.concatenate([part, jnp.zeros((rows - part.shape[0], part.shape[1]), part.dtype)], 0)


def pack_body(with_weights, *refs):
    me, seq = own_place()
    count = 13 if with_weights else 4
    sources, refs = (refs[:count], refs[count:])
    outs = 5 if with_weights else 3
    targets, held, sem = (refs[:outs], refs[outs : outs + count], refs[-1])
    pay1, pay2, pay3 = targets[:3]
    ins = [
        pltpu.make_async_copy(source, there, sem.at[i])
        for i, (source, there) in enumerate(zip(sources, held))
    ]
    for item in ins:
        item.start()
    long_tok, short_tok, long_cot, short_cot = held[:4]
    n_long, n_short = (long_tok.shape[1], short_tok.shape[1])
    copies = []

    def copy(source, target):
        item = pltpu.make_async_copy(source, target, sem.at[len(copies)])
        item.start()
        copies.append(item)

    if with_weights:
        early, late = targets[3:]
        row = refs[outs + count]
        width = early.shape[2]
        gain, bias = held[11:]
        shard = gain.shape[1]
        col = lax.broadcasted_iota(jnp.int32, (shard, width), 1)
        at = lax.broadcasted_iota(jnp.int32, (shard, width), 0)
        spread = (col == at + me * shard).astype(BF)
    for item in ins:
        item.wait()
    if with_weights:
        wq, wk, wv, pos, wo, up, down = held[4:11]
        chunks = up.shape[1] // width
        vectors = jnp.concatenate([mm(gain[...], spread), mm(bias[...], spread)], 0)
        row[...] = pad_rows(vectors, BAND).astype(BF)
        for i, weight in enumerate((wq, wk, wv, pos)):
            copy(weight, early.at[i])
        copy(wo, late.at[0])
        for c in range(chunks):
            cols = pl.ds(c * width, width)
            copy(up.at[:, cols], late.at[1 + c])
            copy(down.at[:, cols], late.at[1 + chunks + c])
        copy(row, late.at[1 + 2 * chunks])
    last = len(copies)

    def rest(pairs):
        ends = [
            pltpu.make_async_copy(source, target, sem.at[last + i])
            for i, (source, target) in enumerate(pairs)
        ]
        for item in ends:
            item.start()
        for item in ends:
            item.wait()

    def halves(pay, one, two, rows):
        half = pay.shape[0] // 2
        return [(one, pay.at[pl.ds(0, rows), :]), (two, pay.at[pl.ds(half, rows), :])]

    longs = [long_tok.at[0], long_cot.at[0], n_long]
    zeros, ones = ([short_tok.at[i], short_cot.at[i], n_short] for i in range(2))
    plans = (
        halves(pay1, *longs) + [(long_tok.at[0], pay2)] + halves(pay3, *ones),
        halves(pay1, *zeros) + halves(pay2, *ones) + [(long_tok.at[0], pay3)],
        halves(pay1, *ones) + halves(pay2, *zeros),
        halves(pay1, *longs) + halves(pay3, *zeros),
    )
    for place, plan in enumerate(plans):

        @pl.when(seq == place)
        def _(plan=plan):
            rest(plan)

    for item in copies:
        item.wait()


def stack_heads(block, lane):
    zero = jnp.zeros_like(block)
    return jnp.concatenate([jnp.where(lane, block, zero), jnp.where(lane, zero, block)], 0)


def join_heads(stacked, lane):
    half = stacked.shape[0] // 2
    return jnp.where(lane, stacked[:half], stacked[half:])


def head_lanes():
    return lax.broadcasted_iota(jnp.int32, (1, LANES), 1) < HEAD_DIM


def block_base(seq, k, size):
    owner = lax.bitwise_xor(seq, jnp.int32(k))
    return pl.multiple_of(owner * jnp.where(has_long(seq), size, size // 2), size // 2)


def gather_queries(seq, source, target):
    size = source.shape[0] // 4
    half = size // 2

    @pl.when(seq == 1)
    def _():
        target[:size, :] = source[size : 2 * size, :]
        target[size:, :] = source[:size, :]

    @pl.when(seq == 2)
    def _():
        target[...] = source[: 2 * size, :]

    @pl.when((seq == 0) | (seq == 3))
    def _():
        for k in range(4):
            target[k * half : (k + 1) * half, :] = source[k * size : k * size + half, :]


def spread_queries(seq, value, target):
    size = target.shape[0] // 4
    half = size // 2

    @pl.when(seq == 1)
    def _():
        target[size : 2 * size, :] += value[:size]
        target[:size, :] += value[size:]

    @pl.when(seq == 2)
    def _():
        target[: 2 * size, :] += value

    @pl.when((seq == 0) | (seq == 3))
    def _():
        for k in range(4):
            target[k * size : k * size + half, :] += value[k * half : (k + 1) * half]


def row_blocks(seq, whole, shorts, one, two, three):
    rows, half = (whole.shape[1], shorts.shape[1])
    longs = has_long(seq)
    own_short = pad_rows(jnp.where(seq == 0, shorts[0], shorts[1]), rows)
    return (
        jnp.where(longs, whole[0], own_short),
        jnp.where(longs, one, pad_rows(one[:half], rows)),
        two,
        three,
    )


def attend_body(direct, layout, long_len, short_len, *refs):
    count = len(layout)
    long_tok, short_tok, got1, got2, got3 = refs[:5]
    parts, refs = (refs[5 : 5 + count], refs[5 + count :])
    first_o, low_o, lowq_o, q_o, k_o, v_o, probs_o, mix_o = refs[:8]
    weights, table, first, sem = refs[8:]
    me, seq = own_place()
    me = me if direct else jnp.int32(0)
    fetch_weights(layout, parts, weights, sem, me)
    n_long, n_short = (long_tok.shape[1], short_tok.shape[1])
    longs = has_long(seq)
    two, three = (
        jnp.where(longs, got[...], pad_rows(got[:n_short, :], n_long)) for got in (got2, got3)
    )
    blocks = row_blocks(seq, long_tok, short_tok, got1[:n_long, :], two, three)
    for k, block in enumerate(blocks):
        first[k * n_long : (k + 1) * n_long, :] = block.astype(F32)
    pltpu.make_async_copy(weights, weights, sem).wait()
    table[...] = weights[3].astype(F32).T
    for k in range(4):
        rows = slice(k * n_long, (k + 1) * n_long)
        first[rows, :] += table[pl.ds(block_base(seq, k, n_long), n_long), :]
    gather_queries(seq, first, first_o)
    lowq_o[...] = first_o[...].astype(BF)
    low_o[...] = first[...].astype(BF)
    k_o[...] = mm(low_o[...], weights[1]).astype(BF)
    v_o[...] = mm(low_o[...], weights[2]).astype(BF)
    q_o[...] = mm(lowq_o[...], weights[0]).astype(BF) * BF(HEAD_DIM**-0.5)
    rows, keys = (first_o.shape[0], first.shape[0])
    row = lax.broadcasted_iota(jnp.int32, (rows, 1), 0)
    row_pos = jnp.where(
        longs,
        row + (seq - 1) * rows,
        lax.bitwise_xor(row // n_short, jnp.full_like(row, seq)) * n_short + row % n_short,
    )
    row_pos = jnp.concatenate([row_pos, row_pos], 0)
    col = lax.broadcasted_iota(jnp.int32, (1, keys), 1)
    owner = lax.bitwise_xor(col // n_long, jnp.full_like(col, seq))
    inner = col % n_long
    col_pos = jnp.where(longs, owner * n_long + inner, owner * n_short + inner)
    length = pick(seq, short_len[0], long_len[0], long_len[0], short_len[1])
    seen = (col_pos < length) & (longs | (inner < n_short))
    col_pos = jnp.where(seen, col_pos, jnp.int32(1 << 20))
    allowed = col_pos <= row_pos
    lane = head_lanes()
    for g in range(first_o.shape[1] // LANES):
        cols = slice(g * LANES, (g + 1) * LANES)
        scores = mm(stack_heads(q_o[:, cols], lane), k_o[:, cols], NT)
        scores = jnp.where(allowed, scores, -1e30)
        shifted = jnp.exp(scores - jnp.max(scores, axis=-1, keepdims=True))
        probs_o[g] = (shifted / jnp.sum(shifted, axis=-1, keepdims=True)).astype(BF)
        mix_o[:, cols] = join_heads(mm(probs_o[g], v_o[:, cols]), lane).astype(BF)


def norm_parts(values):
    mean = jnp.mean(values, axis=-1, keepdims=True)
    centred = values - mean
    scale = lax.rsqrt(jnp.mean(centred * centred, axis=-1, keepdims=True) + 1e-05)
    return centred * scale, scale


def norm_back(cot, gain, xhat, scale):
    scaled = cot * gain
    mean = jnp.mean(scaled, axis=-1, keepdims=True)
    inner = jnp.mean(scaled * xhat, axis=-1, keepdims=True)
    return scale * (scaled - mean - xhat * inner)


def middle_body(direct, layout, first, mixed, long_cot, short_cot, *refs):
    count = len(layout)
    got1, got2, got3 = refs[:3]
    parts, refs = (refs[3 : 3 + count], refs[3 + count :])
    out_o, gsum_o, gmix_o = refs[:3]
    grad_parts = refs[3:8]
    weights, grads, act, slope, blocks, cots, sem = refs[8:]
    me, seq = own_place()
    me = me if direct else jnp.int32(0)
    fetch_weights(layout, parts, weights, sem, me)
    n_long, n_short = (long_cot.shape[1], short_cot.shape[1])
    two, three = (pad_rows(got[n_short:, :], n_long) for got in (got2, got3))
    found = row_blocks(seq, long_cot, short_cot, got1[n_long:, :], two, three)
    for k, block in enumerate(found):
        blocks[k * n_long : (k + 1) * n_long, :] = block.astype(F32)
    gather_queries(seq, blocks, cots)
    blocks[...] = jnp.zeros_like(blocks)
    pltpu.make_async_copy(weights, weights, sem).wait()
    width = first.shape[1]
    chunks = (weights.shape[0] - 2) // 2
    norm = weights.shape[0] - 1
    vectors = jnp.sum(weights[norm].astype(F32).reshape(-1, BAND, width), axis=0)
    gain0, gain1, bias0, bias1 = (vectors[i : i + 1] for i in range(4))
    mixed_low = mixed[...]
    xhat0, scale0 = norm_parts(first[...] + mm(mixed_low, weights[0]))
    normed = xhat0 * gain0 + bias0
    normed_low = normed.astype(BF)
    second = normed
    for c in range(chunks):
        hidden = mm(normed_low, weights[1 + c])
        cdf = 0.5 + 0.5 * lax.erf(hidden * (0.5**0.5))
        slope[c] = cdf + hidden * jnp.exp(-0.5 * hidden * hidden) * ((2 * math.pi) ** -0.5)
        act[c] = (hidden * cdf).astype(BF)
        second = second + mm(act[c], weights[1 + chunks + c], NT)
    xhat1, scale1 = norm_parts(second)
    spread_queries(seq, xhat1 * gain1 + bias1, blocks)
    out_o[...] = blocks[...].astype(BF)
    cot_wide = cots[...]
    grad_second = norm_back(cot_wide, gain1, xhat1, scale1)
    second_low = grad_second.astype(BF)
    grad_normed = grad_second
    for c in range(chunks):
        hidden_low = (mm(second_low, weights[1 + chunks + c]) * slope[c]).astype(BF)
        grads[1 + chunks + c] = mm(second_low, act[c], TN).astype(BF)
        grads[1 + c] = mm(normed_low, hidden_low, TN).astype(BF)
        grad_normed = grad_normed + mm(hidden_low, weights[1 + c], NT)
    grad_sum = norm_back(grad_normed, gain0, xhat0, scale0)
    gsum_o[...] = grad_sum
    sum_low = grad_sum.astype(BF)
    gmix_o[...] = mm(sum_low, weights[0], NT).astype(BF)
    grads[0] = mm(mixed_low, sum_low, TN).astype(BF)
    terms = jnp.concatenate(
        [
            jnp.sum(grad_normed * xhat0, axis=0, keepdims=True),
            jnp.sum(cot_wide * xhat1, axis=0, keepdims=True),
            jnp.sum(grad_normed, axis=0, keepdims=True),
            jnp.sum(cot_wide, axis=0, keepdims=True),
            jnp.zeros((BAND - 4, width), F32),
        ],
        0,
    ).astype(BF)
    for d in range(width // BAND):
        grads[norm, d * BAND : (d + 1) * BAND, :] = terms
    store_slots(grads, grad_parts, sem, me)


def attend_back_body(gmix, q, k, v, probs_i, dq_o, dk_o, dv_o):
    lane = head_lanes()
    scale = HEAD_DIM**-0.5
    for g in range(gmix.shape[1] // LANES):
        cols = slice(g * LANES, (g + 1) * LANES)
        grads = stack_heads(gmix[:, cols], lane)
        queries = stack_heads(q[:, cols], lane)
        probs = probs_i[g]
        grad_probs = mm(grads, v[:, cols], NT)
        wide = probs.astype(F32)
        inner = jnp.sum(wide * grad_probs, axis=-1, keepdims=True)
        grad_scores = (wide * (grad_probs - inner)).astype(BF)
        grad_q = mm(grad_scores, k[:, cols])
        dq_o[:, cols] = (join_heads(grad_q, lane) * scale).astype(BF)
        dk_o[:, cols] = mm(grad_scores, queries, TN).astype(BF)
        dv_o[:, cols] = mm(probs, grads, TN).astype(BF)


def leave_body(direct, layout, low, lowq, dq, dk, dv, gsum, outs, *refs):
    count = len(layout)
    parts, refs = (refs[:count], refs[count:])
    own_o, sent1_o, sent2_o, sent3_o = refs[:4]
    grad_parts = refs[4:9]
    weights, grads, table, back, sem = refs[9:]
    me, seq = own_place()
    me = me if direct else jnp.int32(0)
    fetch_weights(layout, parts, weights, sem, me)
    grads[0] = mm(lowq[...], dq[...], TN).astype(BF)
    grads[1] = mm(low[...], dk[...], TN).astype(BF)
    grads[2] = mm(low[...], dv[...], TN).astype(BF)
    pltpu.make_async_copy(weights, weights, sem).wait()
    back[...] = mm(dk[...], weights[1], NT) + mm(dv[...], weights[2], NT)
    spread_queries(seq, gsum[...] + mm(dq[...], weights[0], NT), back)
    size = own_o.shape[0]
    table[...] = jnp.zeros_like(table)
    for k, target in enumerate((own_o, sent1_o, sent2_o, sent3_o)):
        piece = back[k * size : (k + 1) * size, :]
        target[:size, :] = piece.astype(target.dtype)
        if k == 1:
            target[size:, :] = outs[size : 2 * size, :]
        elif k > 1:
            both = jnp.concatenate([piece[: size // 2].astype(BF), outs[k * size : k * size + size // 2, :]], 0)
            target[...] = jnp.where(has_long(seq), piece.astype(BF), both)
        table[pl.ds(block_base(seq, k, size), size), :] += piece
    grads[3] = table[...].T.astype(BF)
    store_slots(grads, grad_parts, sem, me)


def return_rows(own, outs, got1, got2, got3, long_grad, short_grad, long_out, short_out):
    seq = own_place()[1]
    size, half = (long_grad.shape[1], short_grad.shape[1])
    for i, (mine, long_o, short_o) in enumerate(((own, long_grad, short_grad), (outs, long_out, short_out))):
        mine = mine[:size, :].astype(F32)
        one = got1[i * size : (i + 1) * size, :].astype(F32)
        if i == 0:
            two, three = (got[...].astype(F32) for got in (got2, got3))
            long_o[0] = pick(seq, one + two, mine + three, mine, one).astype(BF)
        else:
            long_o[0] = pick(seq, one, mine, mine, one).astype(BF)
        two, three = (got[i * half : (i + 1) * half, :].astype(F32) for got in (got2, got3))
        mine, one = (mine[:half], one[:half])
        short_o[0] = pick(seq, mine, one, two, three).astype(BF)
        short_o[1] = pick(seq, three, two, one, mine).astype(BF)


def wide(ref, *index):
    return ref[index].astype(F32)


def sum_call(body, outs, ins, blocks_in, steps, name):
    def spec(shape, axis):
        block = tuple(1 if i == axis else size for i, size in enumerate(shape))
        return pl.BlockSpec(block, lambda i: tuple(i if a == axis else 0 for a in range(len(shape))))

    return pl.pallas_call(
        body,
        grid=(steps,),
        out_shape=[jax.ShapeDtypeStruct(shape, dtype) for shape, dtype, _ in outs],
        in_specs=blocks_in,
        out_specs=[spec(shape, axis) for shape, _, axis in outs],
        compiler_params=pltpu.CompilerParams(vmem_limit_bytes=16 * MIB),
        name=name,
    )(*ins)


def one_place(part, layer=0):
    shape = part.shape
    return pl.BlockSpec((1,) + shape[1:], lambda i: (layer * 4 + i,) + (0,) * (len(shape) - 1))


def first_sums_body(half, near1, near2, near3, far1, far2, far3, to_x, to_y):
    to_y[0, 0] = (wide(near2, 0)[:half] + wide(far2, 0)[:half]).astype(BF)
    to_y[1, 0] = (wide(near3, 0)[:half] + wide(far3, 0)[:half]).astype(BF)
    to_x[0, 0] = (wide(near1, 0)[half:] + wide(far1, 0)[half:]).astype(BF)
    to_x[1, 0] = (wide(near3, 0)[half:] + wide(far3, 0)[half:]).astype(BF)


def second_sums_body(half, near1, near2, far1, far2, from_x, from_y, to_x, to_y):
    to_x[0] = (wide(near1, 0)[:half] + wide(far1, 0)[:half] + wide(from_y, 0, 0)).astype(BF)
    to_y[0] = (wide(near2, 0)[half:] + wide(far2, 0)[half:] + wide(from_x, 0, 0)).astype(BF)


def last_sums_body(half, near0, far0, from_x, from_y, then_x, then_y, *outs):
    for place, out in enumerate(outs):
        low = wide(near0, place)[:half] + wide(far0, place)[:half]
        low = low + (wide(from_y, 0, place) + wide(then_x, place))
        out[:half] = low.astype(out.dtype)
        high = wide(near0, place)[half:] + wide(far0, place)[half:]
        high = high + (wide(from_x, 0, place) + wide(then_y, place))
        out[half:] = high.astype(out.dtype)


def four_sums_body(*refs):
    ins, outs = (refs[:-4], refs[-4:])
    for place, out in enumerate(outs):
        total = wide(ins[0], place)
        for item in ins[1:]:
            total = total + wide(item, place)
        out[...] = total.astype(out.dtype)


def cut_sums(body, parts, pieces, name):
    _, _, band, width = parts[0].shape

    def whole(part):
        shape = part.shape
        shape = (1,) + shape[1:] if len(shape) == 5 else (4,) + shape[1:]
        return pl.BlockSpec(shape, lambda i: (0,) * len(shape))

    out = pl.BlockSpec((pieces, band, width), lambda i: (0, 0, 0))
    return pl.pallas_call(
        body,
        grid=(1,),
        out_shape=[
            jax.ShapeDtypeStruct((pieces, band, width), F32 if place == 0 else BF)
            for place in range(4)
        ],
        in_specs=[whole(part) for part in parts],
        out_specs=[out] * 4,
        compiler_params=pltpu.CompilerParams(vmem_limit_bytes=24 * MIB),
        name=name,
    )(*parts)


def finish_body(*refs):
    late, early, rows = (refs[:4], refs[4:8], refs[8:13])
    row_outs, early_outs = (refs[13:17], refs[17:21])
    out_o, up_o, down_o, gain_o, bias_o = refs[21:]
    width = out_o.shape[1]
    chunks = up_o.shape[1] // width

    def total(parts, i):
        own, one, two, three = parts
        return own[i] + (one[i].astype(F32) + two[i].astype(F32) + three[i].astype(F32))

    return_rows(*rows, *row_outs)
    out_o[...] = total(late, 0)
    for c in range(chunks):
        up_o[:, c * width : (c + 1) * width] = total(late, 1 + c)
        down_o[:, c * width : (c + 1) * width] = total(late, 1 + chunks + c)
    shard = gain_o.shape[1]
    row = lax.broadcasted_iota(jnp.int32, (width, shard), 0)
    col = lax.broadcasted_iota(jnp.int32, (width, shard), 1)
    chosen = (row == col + own_place()[0] * shard).astype(F32)
    norms = mm(total(late, 1 + 2 * chunks), chosen, NN, lax.Precision.HIGHEST)
    gain_o[...] = norms[:2]
    bias_o[...] = norms[2:4]
    for i, out in enumerate(early_outs):
        out[...] = total(early, i)


def after(value, *others):
    return lax.optimization_barrier((value,) + others)[0]


def local(
    dp_count,
    seq_count,
    long_tokens,
    short_tokens,
    long_cot,
    short_cot,
    long_lengths,
    short_lengths,
    w_query,
    w_key,
    w_value,
    w_out,
    w_up,
    w_down,
    pos_table,
    norm_gain,
    norm_bias,
):
    width = w_key.shape[1]
    hidden = w_up.shape[1]
    chunks = hidden // width
    shard = w_key.shape[0]
    direct = shard == BAND and dp_count == 8
    layers = 4
    device = lax.axis_index("dp") * seq_count + lax.axis_index("seq")
    n_long, n_short = (long_tokens.shape[1], short_tokens.shape[1])
    rows, keys = (2 * n_long, 4 * n_long)
    square = width * width
    early_pieces, late_pieces = (4, 2 + 2 * chunks)

    def swap_seq(value, mask, keep=lambda source, target: True):
        pairs = [(i, i ^ mask) for i in range(seq_count) if keep(i, i ^ mask)]
        return lax.ppermute(value, "seq", pairs)

    def swap_dp(value, mask):
        return lax.ppermute(value, "dp", [(i, i ^ mask) for i in range(dp_count)])

    acts = [long_tokens, short_tokens, long_cot, short_cot]
    packed = [
        ((2 * n_long, width), BF, HBM),
        ((n_long, width), BF, HBM),
        ((n_long, width), BF, HBM),
    ]
    own, specs, scratch = ([], [HBM] * 4, [])
    held = list(acts)
    if direct:
        own = [w_query, w_key, w_value, pos_table.T, w_out, w_up, w_down.T]
        own += [norm_gain, norm_bias]
        held += own
        packed += [((count, BAND, width), BF, HBM) for count in (early_pieces, late_pieces)]
        specs += [HBM] * 9
        scratch = [pltpu.VMEM((BAND, width), BF)]
    pays = call(
        functools.partial(pack_body, direct),
        packed,
        specs,
        [pltpu.VMEM(item.shape, BF) for item in held] + scratch + [pltpu.SemaphoreType.DMA((32,))],
        (0, 4 * MIB),
        "pack",
        60,
    )(*acts, *own)
    pay1, pay2, pay3 = pays[:3]

    def to_slots(whole):
        count = whole.shape[0]
        cut = whole.reshape(count, 4, 2, 4, BAND, width).transpose(2, 1, 3, 0, 4, 5)
        return [cut[core, outer] for core in range(2) for outer in range(4)]

    def slot_outs(pieces):
        near = ((4, pieces, BAND, width), BF, HBM)
        return [near] * layers + [((4 * layers, pieces, BAND, width), BF, HBM)]

    def from_slots(parts):
        count = parts[0].shape[1]
        cut = jnp.concatenate(parts, 0).reshape(2, 4, 4, count, BAND, width)
        return cut.transpose(3, 1, 0, 2, 4, 5).reshape(count, width, width)

    def places(piece):
        return [piece] + [swap_seq(piece, k) for k in range(1, 4)]

    def spread(column):
        near = [column] + [swap_dp(column, 2 * k) for k in range(1, layers)]
        return near

    def cross(near):
        return list(near) + [swap_dp(part, 1) for part in near]

    early_layout = plain_layout(early_pieces)
    late_layout = split_layout(late_pieces) if direct else plain_layout(late_pieces)
    if direct:
        early, late = pays[3:]
        early_places = places(early)
        late = after(late, early_places[1], early_places[2])
        late_places = places(late)
        early_near = spread(jnp.stack(early_places))
        column = jnp.stack(late_places)
        column = after(column, *early_near)
        pay1, pay2, pay3 = lax.optimization_barrier((pay1, pay2, pay3, *late_places))[:3]
        got1, got2, got3 = (
            swap_seq(pay1, 1),
            swap_seq(pay2, 2, lambda source, target: target != 1),
            swap_seq(pay3, 3, lambda source, target: target != 1),
        )
        early_full = early_near + cross(lax.optimization_barrier((early_near, got1, got2, got3))[0])[4:]
        half = late_pieces // 2
        near1, near2 = (swap_dp(column, 2), swap_dp(column, 4))
        near3 = [swap_dp(near1[:, :half], 4), swap_dp(near2[:, half:], 2)]
    if not direct:
        got1, got2, got3 = (
            swap_seq(pay1, 1),
            swap_seq(pay2, 2, lambda source, target: target != 1),
            swap_seq(pay3, 3, lambda source, target: target != 1),
        )

        def columns(weight):
            return weight.reshape(weight.shape[0], chunks, width).transpose(1, 0, 2)

        def whole(pieces):
            return lax.all_gather(pieces, ("dp", "seq"), axis=1, tiled=True)

        early_full = to_slots(whole(jnp.stack([w_query, w_key, w_value, pos_table.T])))
        vectors = jnp.concatenate([norm_gain, norm_bias], 0)
        vectors = lax.all_gather(vectors, ("dp", "seq"), axis=1, tiled=True)
        vectors = jnp.pad(vectors, ((0, width - 4), (0, 0)))
        late_whole = whole(jnp.concatenate([w_out[None], columns(w_up), columns(w_down.T)], 0))
        late_full = to_slots(jnp.concatenate([late_whole, vectors[None]], 0))

    groups = width // LANES
    first, low, low_queries, queries, key_rows, values, probs, mixed = call(
        functools.partial(attend_body, direct, early_layout),
        [
            ((rows, width), F32, VMEM),
            ((keys, width), BF, VMEM),
            ((rows, width), BF, VMEM),
            ((rows, width), BF, VMEM),
            ((keys, width), BF, VMEM),
            ((keys, width), BF, VMEM),
            ((groups, 2 * rows, keys), BF, VMEM),
            ((rows, width), BF, VMEM),
        ],
        [SMEM] * 2 + [VMEM] * 5 + [HBM] * len(early_layout),
        [
            pltpu.VMEM((early_pieces, width, width), BF),
            pltpu.VMEM((width, width), F32),
            pltpu.VMEM((keys, width), F32),
            pltpu.SemaphoreType.DMA,
        ],
        (8 * keys * square, 10 * MIB),
        "attend",
        24,
    )(long_lengths, short_lengths, long_tokens, short_tokens, got1, got2, got3, *early_full)

    if direct:
        near3, first = lax.optimization_barrier((near3, first))
        late_near = [column, near1, near2]
        late_far = [swap_dp(part, 1) for part in late_near + list(near3)]
        late_full = late_near + list(near3) + late_far
    block = (n_long, width)
    middle_outs = call(
        functools.partial(middle_body, direct, late_layout),
        [((keys, width), BF, VMEM)]
        + [((rows, width), F32, VMEM), ((rows, width), BF, VMEM)]
        + slot_outs(late_pieces),
        [VMEM] * 7 + [HBM] * len(late_layout),
        [
            pltpu.VMEM((late_pieces, width, width), BF),
            pltpu.VMEM((late_pieces, width, width), BF),
            pltpu.VMEM((chunks, rows, width), BF),
            pltpu.VMEM((chunks, rows, width), F32),
            pltpu.VMEM((keys, width), F32),
            pltpu.VMEM((rows, width), F32),
            pltpu.SemaphoreType.DMA,
        ],
        (16 * rows * square * chunks, 20 * MIB),
        "middle",
        32,
    )(first, mixed, long_cot, short_cot, got1, got2, got3, *late_full)
    out_blocks, grad_sum, grad_mixed = middle_outs[:3]
    late_parts = middle_outs[3:]

    def core_sums(parts, arrived):
        return [
            (parts[k].astype(F32) + arrived[4 * k : 4 * k + 4].astype(F32)).astype(BF)
            for k in range(1, layers)
        ]

    if direct:
        late_arrived = swap_dp(late_parts[-1], 1)

    grad_q, grad_k, grad_v = call(
        attend_back_body,
        [
            ((rows, width), BF, VMEM),
            ((keys, width), BF, VMEM),
            ((keys, width), BF, VMEM),
        ],
        [VMEM] * 5,
        [],
        (8 * keys * square, 8 * MIB),
        "attend_back",
        24,
    )(grad_mixed, queries, key_rows, values, probs)
    leave_outs = call(
        functools.partial(leave_body, direct, early_layout),
        [(block, F32, VMEM), ((2 * n_long, width), BF, VMEM)] + [(block, BF, VMEM)] * 2 + slot_outs(early_pieces),
        [VMEM] * 7 + [HBM] * len(early_layout),
        [
            pltpu.VMEM((early_pieces, width, width), BF),
            pltpu.VMEM((early_pieces, width, width), BF),
            pltpu.VMEM((width, width), F32),
            pltpu.VMEM((keys, width), F32),
            pltpu.SemaphoreType.DMA,
        ],
        (10 * keys * square, 8 * MIB),
        "leave",
        24,
    )(low, low_queries, grad_q, grad_k, grad_v, grad_sum, out_blocks, *early_full)
    grad_blocks, early_parts = (leave_outs[:4], leave_outs[4:])

    back = lambda source, target: source != 1
    got = [swap_seq(grad_blocks[1], 1)] + [swap_seq(grad_blocks[k], k, back) for k in (2, 3)]
    row_outs = [(item.shape, BF, VMEM) for item in (long_tokens, short_tokens)] * 2
    if direct:
        half = late_pieces // 2
        near0, near1, near2, near3 = late_parts[:4]
        far = late_arrived
        pair = ((2, 4, half, BAND, width), BF, 1)
        single = ((4, half, BAND, width), BF, 0)
        to_x, to_y = sum_call(
            functools.partial(first_sums_body, half),
            [pair, pair],
            [near1, near2, near3, far, far, far],
            [one_place(item) for item in (near1, near2, near3)] + [one_place(far, k) for k in (1, 2, 3)],
            4,
            "late_sums_1",
        )
        from_x, from_y = (swap_dp(to_x, 2), swap_dp(to_y, 4))
        second = pl.BlockSpec((1, 1, half, BAND, width), lambda i: (1, i, 0, 0, 0))
        then_x, then_y = sum_call(
            functools.partial(second_sums_body, half),
            [single, single],
            [near1, near2, far, far, from_x, from_y],
            [one_place(near1), one_place(near2), one_place(far, 1), one_place(far, 2), second, second],
            4,
            "late_sums_2",
        )
        early_far = after(early_parts[-1], to_x)
        early_arrived = swap_dp(early_far, 1)
        early_sums = core_sums(early_parts, early_arrived)
        then_x, then_y, early_sums = lax.optimization_barrier((then_x, then_y, early_sums))
        then_x, then_y = (swap_dp(then_x, 2), swap_dp(then_y, 4))
        early_layers = [swap_dp(part, 2 * k) for k, part in enumerate(early_sums, 1)]
        then_x, then_y, got = lax.optimization_barrier((then_x, then_y, got))
        late_cut = cut_sums(
            functools.partial(last_sums_body, half),
            [near0, far, from_x, from_y, then_x, then_y],
            late_pieces,
            "late_sums_3",
        )
        late_ends = [late_cut[0]] + [swap_seq(late_cut[k], k) for k in range(1, 4)]
        early_cut = cut_sums(
            four_sums_body, [early_parts[0], early_arrived] + early_layers, early_pieces, "early_sums"
        )
        early_ends = [early_cut[0]] + [swap_seq(early_cut[k], k) for k in range(1, 4)]
        row_ins = [grad_blocks[0], out_blocks, *got]
        ends = call(
            finish_body,
            row_outs
            + [((shard, width), F32, VMEM)] * 5
            + [((shard, hidden), F32, VMEM)] * 2
            + [((2, shard), F32, VMEM)] * 2,
            [VMEM] * 13,
            [],
            (0, MIB),
            "finish",
            16,
        )(*late_ends, *early_ends, *row_ins)
        row_grads, early_sum = (ends[:4], ends[4:8])
        grad_out, grad_up, grad_down, grad_gain, grad_bias = ends[8:]
    else:

        def scatter(parts):
            whole_sum = from_slots(parts).astype(F32)
            return lax.psum_scatter(whole_sum, ("dp", "seq"), scatter_dimension=1, tiled=True)

        def join(pieces):
            return pieces.transpose(1, 0, 2).reshape(shard, hidden)

        late_sum = scatter(late_parts)
        early_sum = scatter(early_parts)
        grad_out, grad_up, grad_down = (
            late_sum[0],
            join(late_sum[1 : 1 + chunks]),
            join(late_sum[1 + chunks : 1 + 2 * chunks]),
        )
        norms = lax.psum(from_slots(late_parts)[-1, :BAND].astype(F32), ("dp", "seq"))
        norms = lax.dynamic_slice(norms, (0, device * shard), (BAND, shard))
        grad_gain, grad_bias = (norms[:2], norms[2:4])
        row_grads = call(
            return_rows, row_outs, [VMEM] * 5, [], (0, MIB), "return", 16
        )(grad_blocks[0], out_blocks, *got)
    long_grad, short_grad, long_out, short_out = row_grads
    return (
        long_out,
        short_out,
        long_grad,
        short_grad,
        early_sum[0],
        early_sum[1],
        early_sum[2],
        grad_out,
        grad_up,
        grad_down.T,
        early_sum[3].T,
        grad_gain,
        grad_bias,
    )


def solution(mesh):
    rows = P(("dp", "seq"), None)
    cols = P(None, ("dp", "seq"))
    acts = P("dp", "seq", None)
    return jax.shard_map(
        functools.partial(local, mesh.shape["dp"], mesh.shape["seq"]),
        mesh=mesh,
        in_specs=(acts,) * 4 + (P("dp"),) * 2 + (rows,) * 5 + (cols,) * 4,
        out_specs=(acts,) * 4 + (rows,) * 5 + (cols,) * 4,
        check_vma=False,
    )
```

```python
import functools
import math

import jax
import jax.numpy as jnp
from jax import lax
from jax.experimental import pallas as pl
from jax.experimental.pallas import tpu as pltpu
from jax.sharding import PartitionSpec as P

HEAD_DIM = 64
LANES = 128
BAND = 16
MIB = 1024 * 1024
BF = jnp.bfloat16
F32 = jnp.float32
VMEM = pl.BlockSpec(memory_space=pltpu.VMEM)
SMEM = pl.BlockSpec(memory_space=pltpu.SMEM)
HBM = pl.BlockSpec(memory_space=pltpu.HBM)
NN = (((1,), (0,)), ((), ()))
NT = (((1,), (1,)), ((), ()))
TN = (((0,), (0,)), ((), ()))


def mm(left, right, dims=NN, precision=None):
    return lax.dot_general(left, right, dims, precision, preferred_element_type=F32)


def call(body, outs, ins, scratch, cost, name, limit):
    flops, moved = cost
    return pl.pallas_call(
        body,
        out_shape=[jax.ShapeDtypeStruct(shape, dtype) for shape, dtype, _ in outs],
        out_specs=[spec for _, _, spec in outs],
        in_specs=ins,
        scratch_shapes=scratch,
        compiler_params=pltpu.CompilerParams(vmem_limit_bytes=limit * MIB),
        cost_estimate=pl.CostEstimate(flops=flops, bytes_accessed=moved, transcendentals=0),
        name=name,
    )


def own_place():
    seq = lax.axis_index("seq")
    return lax.axis_index("dp") * 4 + seq, seq


def slot_rows(core, layer, place, me):
    device = lax.bitwise_xor(jnp.int32((layer * 2 + core) * 4 + place), me)
    return pl.ds(pl.multiple_of(device * BAND, BAND), BAND)


def plain_layout(pieces):
    return [(core, layer, 0, pieces) for core in range(2) for layer in range(4)]


def split_layout(pieces):
    half = pieces // 2
    per_core = [(layer, 0, pieces) for layer in range(3)] + [(3, 0, half), (3, half, half)]
    return [(core,) + item for core in range(2) for item in per_core]


def fetch_weights(layout, parts, weights, sem, me):
    for (core, layer, first, count), part in zip(layout, parts):
        for place in range(4):
            rows = slot_rows(core, layer, place, me)
            target = weights.at[pl.ds(first, count), rows, :]
            pltpu.make_async_copy(part.at[place], target, sem).start()


def store_slots(grads, parts, sem, me):
    for core in range(2):
        for layer in range(4):
            for place in range(4):
                slot = parts[4].at[layer * 4 + place] if core else parts[layer].at[place]
                rows = slot_rows(core, layer, place, me)
                pltpu.make_async_copy(grads.at[:, rows, :], slot, sem).start()
    pltpu.make_async_copy(grads, grads, sem).wait()


def has_long(seq):
    return (seq == 1) | (seq == 2)


def pick(seq, *options):
    chosen = options[-1]
    for i in range(len(options) - 2, -1, -1):
        chosen = jnp.where(seq == i, options[i], chosen)
    return chosen


def pad_rows(part, rows):
    return jnp.concatenate([part, jnp.zeros((rows - part.shape[0], part.shape[1]), part.dtype)], 0)


def pack_body(with_weights, *refs):
    me, seq = own_place()
    count = 13 if with_weights else 4
    sources, refs = (refs[:count], refs[count:])
    outs = 5 if with_weights else 3
    targets, held, sem = (refs[:outs], refs[outs : outs + count], refs[-1])
    pay1, pay2, pay3 = targets[:3]
    ins = [
        pltpu.make_async_copy(source, there, sem.at[i])
        for i, (source, there) in enumerate(zip(sources, held))
    ]
    for item in ins:
        item.start()
    long_tok, short_tok, long_cot, short_cot = held[:4]
    n_long, n_short = (long_tok.shape[1], short_tok.shape[1])
    copies = []

    def copy(source, target):
        item = pltpu.make_async_copy(source, target, sem.at[len(copies)])
        item.start()
        copies.append(item)

    if with_weights:
        early, late = targets[3:]
        row = refs[outs + count]
        width = early.shape[2]
        gain, bias = held[11:]
        shard = gain.shape[1]
        col = lax.broadcasted_iota(jnp.int32, (shard, width), 1)
        at = lax.broadcasted_iota(jnp.int32, (shard, width), 0)
        spread = (col == at + me * shard).astype(BF)
    for item in ins:
        item.wait()
    if with_weights:
        wq, wk, wv, pos, wo, up, down = held[4:11]
        chunks = up.shape[1] // width
        vectors = jnp.concatenate([mm(gain[...], spread), mm(bias[...], spread)], 0)
        row[...] = pad_rows(vectors, BAND).astype(BF)
        for i, weight in enumerate((wq, wk, wv, pos)):
            copy(weight, early.at[i])
        copy(wo, late.at[0])
        for c in range(chunks):
            cols = pl.ds(c * width, width)
            copy(up.at[:, cols], late.at[1 + c])
            copy(down.at[:, cols], late.at[1 + chunks + c])
        copy(row, late.at[1 + 2 * chunks])
    last = len(copies)

    def rest(pairs):
        ends = [
            pltpu.make_async_copy(source, target, sem.at[last + i])
            for i, (source, target) in enumerate(pairs)
        ]
        for item in ends:
            item.start()
        for item in ends:
            item.wait()

    def halves(pay, one, two, rows):
        half = pay.shape[0] // 2
        return [(one, pay.at[pl.ds(0, rows), :]), (two, pay.at[pl.ds(half, rows), :])]

    longs = [long_tok.at[0], long_cot.at[0], n_long]
    zeros, ones = ([short_tok.at[i], short_cot.at[i], n_short] for i in range(2))
    plans = (
        halves(pay1, *longs) + [(long_tok.at[0], pay2)] + halves(pay3, *ones),
        halves(pay1, *zeros) + halves(pay2, *ones) + [(long_tok.at[0], pay3)],
        halves(pay1, *ones) + halves(pay2, *zeros),
        halves(pay1, *longs) + halves(pay3, *zeros),
    )
    for place, plan in enumerate(plans):

        @pl.when(seq == place)
        def _(plan=plan):
            rest(plan)

    for item in copies:
        item.wait()


def stack_heads(block, lane):
    zero = jnp.zeros_like(block)
    return jnp.concatenate([jnp.where(lane, block, zero), jnp.where(lane, zero, block)], 0)


def join_heads(stacked, lane):
    half = stacked.shape[0] // 2
    return jnp.where(lane, stacked[:half], stacked[half:])


def head_lanes():
    return lax.broadcasted_iota(jnp.int32, (1, LANES), 1) < HEAD_DIM


def block_base(seq, k, size):
    owner = lax.bitwise_xor(seq, jnp.int32(k))
    return pl.multiple_of(owner * jnp.where(has_long(seq), size, size // 2), size // 2)


def gather_queries(seq, source, target):
    size = source.shape[0] // 4
    half = size // 2

    @pl.when(seq == 1)
    def _():
        target[:size, :] = source[size : 2 * size, :]
        target[size:, :] = source[:size, :]

    @pl.when(seq == 2)
    def _():
        target[...] = source[: 2 * size, :]

    @pl.when((seq == 0) | (seq == 3))
    def _():
        for k in range(4):
            target[k * half : (k + 1) * half, :] = source[k * size : k * size + half, :]


def spread_queries(seq, value, target):
    size = target.shape[0] // 4
    half = size // 2

    @pl.when(seq == 1)
    def _():
        target[size : 2 * size, :] += value[:size]
        target[:size, :] += value[size:]

    @pl.when(seq == 2)
    def _():
        target[: 2 * size, :] += value

    @pl.when((seq == 0) | (seq == 3))
    def _():
        for k in range(4):
            target[k * size : k * size + half, :] += value[k * half : (k + 1) * half]


def row_blocks(seq, whole, shorts, one, two, three):
    rows, half = (whole.shape[1], shorts.shape[1])
    longs = has_long(seq)
    own_short = pad_rows(jnp.where(seq == 0, shorts[0], shorts[1]), rows)
    return (
        jnp.where(longs, whole[0], own_short),
        jnp.where(longs, one, pad_rows(one[:half], rows)),
        two,
        three,
    )


def attend_body(direct, layout, long_len, short_len, *refs):
    count = len(layout)
    long_tok, short_tok, got1, got2, got3 = refs[:5]
    parts, refs = (refs[5 : 5 + count], refs[5 + count :])
    first_o, low_o, lowq_o, q_o, k_o, v_o, probs_o, mix_o = refs[:8]
    weights, table, first, sem = refs[8:]
    me, seq = own_place()
    me = me if direct else jnp.int32(0)
    fetch_weights(layout, parts, weights, sem, me)
    n_long, n_short = (long_tok.shape[1], short_tok.shape[1])
    longs = has_long(seq)
    two, three = (
        jnp.where(longs, got[...], pad_rows(got[:n_short, :], n_long)) for got in (got2, got3)
    )
    blocks = row_blocks(seq, long_tok, short_tok, got1[:n_long, :], two, three)
    for k, block in enumerate(blocks):
        first[k * n_long : (k + 1) * n_long, :] = block.astype(F32)
    pltpu.make_async_copy(weights, weights, sem).wait()
    table[...] = weights[3].astype(F32).T
    for k in range(4):
        rows = slice(k * n_long, (k + 1) * n_long)
        first[rows, :] += table[pl.ds(block_base(seq, k, n_long), n_long), :]
    gather_queries(seq, first, first_o)
    lowq_o[...] = first_o[...].astype(BF)
    low_o[...] = first[...].astype(BF)
    k_o[...] = mm(low_o[...], weights[1]).astype(BF)
    v_o[...] = mm(low_o[...], weights[2]).astype(BF)
    q_o[...] = mm(lowq_o[...], weights[0]).astype(BF) * BF(HEAD_DIM**-0.5)
    rows, keys = (first_o.shape[0], first.shape[0])
    row = lax.broadcasted_iota(jnp.int32, (rows, 1), 0)
    row_pos = jnp.where(
        longs,
        row + (seq - 1) * rows,
        lax.bitwise_xor(row // n_short, jnp.full_like(row, seq)) * n_short + row % n_short,
    )
    row_pos = jnp.concatenate([row_pos, row_pos], 0)
    col = lax.broadcasted_iota(jnp.int32, (1, keys), 1)
    owner = lax.bitwise_xor(col // n_long, jnp.full_like(col, seq))
    inner = col % n_long
    col_pos = jnp.where(longs, owner * n_long + inner, owner * n_short + inner)
    length = pick(seq, short_len[0], long_len[0], long_len[0], short_len[1])
    seen = (col_pos < length) & (longs | (inner < n_short))
    col_pos = jnp.where(seen, col_pos, jnp.int32(1 << 20))
    allowed = col_pos <= row_pos
    lane = head_lanes()
    for g in range(first_o.shape[1] // LANES):
        cols = slice(g * LANES, (g + 1) * LANES)
        scores = mm(stack_heads(q_o[:, cols], lane), k_o[:, cols], NT)
        scores = jnp.where(allowed, scores, -1e30)
        shifted = jnp.exp(scores - jnp.max(scores, axis=-1, keepdims=True))
        probs_o[g] = (shifted / jnp.sum(shifted, axis=-1, keepdims=True)).astype(BF)
        mix_o[:, cols] = join_heads(mm(probs_o[g], v_o[:, cols]), lane).astype(BF)


def norm_parts(values):
    mean = jnp.mean(values, axis=-1, keepdims=True)
    centred = values - mean
    scale = lax.rsqrt(jnp.mean(centred * centred, axis=-1, keepdims=True) + 1e-05)
    return centred * scale, scale


def norm_back(cot, gain, xhat, scale):
    scaled = cot * gain
    mean = jnp.mean(scaled, axis=-1, keepdims=True)
    inner = jnp.mean(scaled * xhat, axis=-1, keepdims=True)
    return scale * (scaled - mean - xhat * inner)


def middle_body(direct, layout, first, mixed, long_cot, short_cot, *refs):
    count = len(layout)
    got1, got2, got3 = refs[:3]
    parts, refs = (refs[3 : 3 + count], refs[3 + count :])
    out_o, gsum_o, gmix_o = refs[:3]
    grad_parts = refs[3:8]
    weights, grads, act, slope, blocks, cots, sem = refs[8:]
    me, seq = own_place()
    me = me if direct else jnp.int32(0)
    fetch_weights(layout, parts, weights, sem, me)
    n_long, n_short = (long_cot.shape[1], short_cot.shape[1])
    two, three = (pad_rows(got[n_short:, :], n_long) for got in (got2, got3))
    found = row_blocks(seq, long_cot, short_cot, got1[n_long:, :], two, three)
    for k, block in enumerate(found):
        blocks[k * n_long : (k + 1) * n_long, :] = block.astype(F32)
    gather_queries(seq, blocks, cots)
    blocks[...] = jnp.zeros_like(blocks)
    pltpu.make_async_copy(weights, weights, sem).wait()
    width = first.shape[1]
    chunks = (weights.shape[0] - 2) // 2
    norm = weights.shape[0] - 1
    vectors = jnp.sum(weights[norm].astype(F32).reshape(-1, BAND, width), axis=0)
    gain0, gain1, bias0, bias1 = (vectors[i : i + 1] for i in range(4))
    mixed_low = mixed[...]
    xhat0, scale0 = norm_parts(first[...] + mm(mixed_low, weights[0]))
    normed = xhat0 * gain0 + bias0
    normed_low = normed.astype(BF)
    second = normed
    for c in range(chunks):
        hidden = mm(normed_low, weights[1 + c])
        cdf = 0.5 + 0.5 * lax.erf(hidden * (0.5**0.5))
        slope[c] = cdf + hidden * jnp.exp(-0.5 * hidden * hidden) * ((2 * math.pi) ** -0.5)
        act[c] = (hidden * cdf).astype(BF)
        second = second + mm(act[c], weights[1 + chunks + c], NT)
    xhat1, scale1 = norm_parts(second)
    spread_queries(seq, xhat1 * gain1 + bias1, blocks)
    out_o[...] = blocks[...].astype(BF)
    cot_wide = cots[...]
    grad_second = norm_back(cot_wide, gain1, xhat1, scale1)
    second_low = grad_second.astype(BF)
    grad_normed = grad_second
    for c in range(chunks):
        hidden_low = (mm(second_low, weights[1 + chunks + c]) * slope[c]).astype(BF)
        grads[1 + chunks + c] = mm(second_low, act[c], TN).astype(BF)
        grads[1 + c] = mm(normed_low, hidden_low, TN).astype(BF)
        grad_normed = grad_normed + mm(hidden_low, weights[1 + c], NT)
    grad_sum = norm_back(grad_normed, gain0, xhat0, scale0)
    gsum_o[...] = grad_sum
    sum_low = grad_sum.astype(BF)
    gmix_o[...] = mm(sum_low, weights[0], NT).astype(BF)
    grads[0] = mm(mixed_low, sum_low, TN).astype(BF)
    terms = jnp.concatenate(
        [
            jnp.sum(grad_normed * xhat0, axis=0, keepdims=True),
            jnp.sum(cot_wide * xhat1, axis=0, keepdims=True),
            jnp.sum(grad_normed, axis=0, keepdims=True),
            jnp.sum(cot_wide, axis=0, keepdims=True),
            jnp.zeros((BAND - 4, width), F32),
        ],
        0,
    ).astype(BF)
    for d in range(width // BAND):
        grads[norm, d * BAND : (d + 1) * BAND, :] = terms
    store_slots(grads, grad_parts, sem, me)


def attend_back_body(direct, layout, gmix, q, k, v, probs_i, gsum, outs, *refs):
    count = len(layout)
    parts, refs = (refs[:count], refs[count:])
    dq_o, dk_o, dv_o, back_o, own_o, sent1_o, sent2_o, sent3_o, weights, sem = refs
    me, seq = own_place()
    fetch_weights(layout, parts, weights, sem, me if direct else jnp.int32(0))
    lane = head_lanes()
    scale = HEAD_DIM**-0.5
    for g in range(gmix.shape[1] // LANES):
        cols = slice(g * LANES, (g + 1) * LANES)
        grads = stack_heads(gmix[:, cols], lane)
        queries = stack_heads(q[:, cols], lane)
        probs = probs_i[g]
        grad_probs = mm(grads, v[:, cols], NT)
        spread = probs.astype(F32)
        inner = jnp.sum(spread * grad_probs, axis=-1, keepdims=True)
        grad_scores = (spread * (grad_probs - inner)).astype(BF)
        grad_q = mm(grad_scores, k[:, cols])
        dq_o[:, cols] = (join_heads(grad_q, lane) * scale).astype(BF)
        dk_o[:, cols] = mm(grad_scores, queries, TN).astype(BF)
        dv_o[:, cols] = mm(probs, grads, TN).astype(BF)
    pltpu.make_async_copy(weights, weights, sem).wait()
    back_o[...] = mm(dk_o[...], weights[1], NT) + mm(dv_o[...], weights[2], NT)
    spread_queries(seq, gsum[...] + mm(dq_o[...], weights[0], NT), back_o)
    size = own_o.shape[0]
    for k, target in enumerate((own_o, sent1_o, sent2_o, sent3_o)):
        piece = back_o[k * size : (k + 1) * size, :]
        target[:size, :] = piece.astype(target.dtype)
        if k == 1:
            target[size:, :] = outs[size : 2 * size, :]
        elif k > 1:
            half = size // 2
            both = jnp.concatenate(
                [piece[:half].astype(BF), outs[k * size : k * size + half, :]], 0
            )
            target[...] = jnp.where(has_long(seq), piece.astype(BF), both)


def leave_body(direct, low, lowq, dq, dk, dv, back, *refs):
    grad_parts, (grads, table, sem) = (refs[:5], refs[5:])
    me, seq = own_place()
    me = me if direct else jnp.int32(0)
    grads[0] = mm(lowq[...], dq[...], TN).astype(BF)
    grads[1] = mm(low[...], dk[...], TN).astype(BF)
    grads[2] = mm(low[...], dv[...], TN).astype(BF)
    size = back.shape[0] // 4
    table[...] = jnp.zeros_like(table)
    for k in range(4):
        table[pl.ds(block_base(seq, k, size), size), :] += back[k * size : (k + 1) * size, :]
    grads[3] = table[...].T.astype(BF)
    store_slots(grads, grad_parts, sem, me)


def return_rows(own, outs, got1, got2, got3, long_grad, short_grad, long_out, short_out):
    seq = own_place()[1]
    size, half = (long_grad.shape[1], short_grad.shape[1])
    for i, (mine, long_o, short_o) in enumerate(((own, long_grad, short_grad), (outs, long_out, short_out))):
        mine = mine[:size, :].astype(F32)
        one = got1[i * size : (i + 1) * size, :].astype(F32)
        if i == 0:
            two, three = (got[...].astype(F32) for got in (got2, got3))
            long_o[0] = pick(seq, one + two, mine + three, mine, one).astype(BF)
        else:
            long_o[0] = pick(seq, one, mine, mine, one).astype(BF)
        two, three = (got[i * half : (i + 1) * half, :].astype(F32) for got in (got2, got3))
        mine, one = (mine[:half], one[:half])
        short_o[0] = pick(seq, mine, one, two, three).astype(BF)
        short_o[1] = pick(seq, three, two, one, mine).astype(BF)


def wide(ref, *index):
    return ref[index].astype(F32)


def sum_call(body, outs, ins, blocks_in, steps, name):
    def spec(shape, axis):
        block = tuple(1 if i == axis else size for i, size in enumerate(shape))
        return pl.BlockSpec(block, lambda i: tuple(i if a == axis else 0 for a in range(len(shape))))

    return pl.pallas_call(
        body,
        grid=(steps,),
        out_shape=[jax.ShapeDtypeStruct(shape, dtype) for shape, dtype, _ in outs],
        in_specs=blocks_in,
        out_specs=[spec(shape, axis) for shape, _, axis in outs],
        compiler_params=pltpu.CompilerParams(vmem_limit_bytes=16 * MIB),
        name=name,
    )(*ins)


def one_place(part, layer=0):
    shape = part.shape
    return pl.BlockSpec((1,) + shape[1:], lambda i: (layer * 4 + i,) + (0,) * (len(shape) - 1))


def first_sums_body(half, near1, near2, near3, far1, far2, far3, to_x, to_y):
    to_y[0, 0] = (wide(near2, 0)[:half] + wide(far2, 0)[:half]).astype(BF)
    to_y[1, 0] = (wide(near3, 0)[:half] + wide(far3, 0)[:half]).astype(BF)
    to_x[0, 0] = (wide(near1, 0)[half:] + wide(far1, 0)[half:]).astype(BF)
    to_x[1, 0] = (wide(near3, 0)[half:] + wide(far3, 0)[half:]).astype(BF)


def second_sums_body(half, near1, near2, far1, far2, from_x, from_y, to_x, to_y):
    to_x[0] = (wide(near1, 0)[:half] + wide(far1, 0)[:half] + wide(from_y, 0, 0)).astype(BF)
    to_y[0] = (wide(near2, 0)[half:] + wide(far2, 0)[half:] + wide(from_x, 0, 0)).astype(BF)


def last_sums_body(half, near0, far0, from_x, from_y, then_x, then_y, *outs):
    for place, out in enumerate(outs):
        low = wide(near0, place)[:half] + wide(far0, place)[:half]
        low = low + (wide(from_y, 0, place) + wide(then_x, place))
        out[:half] = low.astype(out.dtype)
        high = wide(near0, place)[half:] + wide(far0, place)[half:]
        high = high + (wide(from_x, 0, place) + wide(then_y, place))
        out[half:] = high.astype(out.dtype)


def four_sums_body(*refs):
    ins, outs = (refs[:-4], refs[-4:])
    for place, out in enumerate(outs):
        total = wide(ins[0], place)
        for item in ins[1:]:
            total = total + wide(item, place)
        out[...] = total.astype(out.dtype)


def cut_sums(body, parts, pieces, name):
    _, _, band, width = parts[0].shape

    def whole(part):
        shape = part.shape
        shape = (1,) + shape[1:] if len(shape) == 5 else (4,) + shape[1:]
        return pl.BlockSpec(shape, lambda i: (0,) * len(shape))

    out = pl.BlockSpec((pieces, band, width), lambda i: (0, 0, 0))
    return pl.pallas_call(
        body,
        grid=(1,),
        out_shape=[
            jax.ShapeDtypeStruct((pieces, band, width), F32 if place == 0 else BF)
            for place in range(4)
        ],
        in_specs=[whole(part) for part in parts],
        out_specs=[out] * 4,
        compiler_params=pltpu.CompilerParams(vmem_limit_bytes=24 * MIB),
        name=name,
    )(*parts)


def finish_body(*refs):
    late, early, rows = (refs[:4], refs[4:8], refs[8:13])
    row_outs, early_outs = (refs[13:17], refs[17:21])
    out_o, up_o, down_o, gain_o, bias_o = refs[21:]
    width = out_o.shape[1]
    chunks = up_o.shape[1] // width

    def total(parts, i):
        own, one, two, three = parts
        return own[i] + (one[i].astype(F32) + two[i].astype(F32) + three[i].astype(F32))

    return_rows(*rows, *row_outs)
    out_o[...] = total(late, 0)
    for c in range(chunks):
        up_o[:, c * width : (c + 1) * width] = total(late, 1 + c)
        down_o[:, c * width : (c + 1) * width] = total(late, 1 + chunks + c)
    shard = gain_o.shape[1]
    row = lax.broadcasted_iota(jnp.int32, (width, shard), 0)
    col = lax.broadcasted_iota(jnp.int32, (width, shard), 1)
    chosen = (row == col + own_place()[0] * shard).astype(F32)
    norms = mm(total(late, 1 + 2 * chunks), chosen, NN, lax.Precision.HIGHEST)
    gain_o[...] = norms[:2]
    bias_o[...] = norms[2:4]
    for i, out in enumerate(early_outs):
        out[...] = total(early, i)


def after(value, *others):
    return lax.optimization_barrier((value,) + others)[0]


def local(
    dp_count,
    seq_count,
    long_tokens,
    short_tokens,
    long_cot,
    short_cot,
    long_lengths,
    short_lengths,
    w_query,
    w_key,
    w_value,
    w_out,
    w_up,
    w_down,
    pos_table,
    norm_gain,
    norm_bias,
):
    width = w_key.shape[1]
    hidden = w_up.shape[1]
    chunks = hidden // width
    shard = w_key.shape[0]
    direct = shard == BAND and dp_count == 8
    layers = 4
    device = lax.axis_index("dp") * seq_count + lax.axis_index("seq")
    n_long, n_short = (long_tokens.shape[1], short_tokens.shape[1])
    rows, keys = (2 * n_long, 4 * n_long)
    square = width * width
    early_pieces, late_pieces = (4, 2 + 2 * chunks)

    def swap_seq(value, mask, keep=lambda source, target: True):
        pairs = [(i, i ^ mask) for i in range(seq_count) if keep(i, i ^ mask)]
        return lax.ppermute(value, "seq", pairs)

    def swap_dp(value, mask):
        return lax.ppermute(value, "dp", [(i, i ^ mask) for i in range(dp_count)])

    acts = [long_tokens, short_tokens, long_cot, short_cot]
    packed = [
        ((2 * n_long, width), BF, HBM),
        ((n_long, width), BF, HBM),
        ((n_long, width), BF, HBM),
    ]
    own, specs, scratch = ([], [HBM] * 4, [])
    held = list(acts)
    if direct:
        own = [w_query, w_key, w_value, pos_table.T, w_out, w_up, w_down.T]
        own += [norm_gain, norm_bias]
        held += own
        packed += [((count, BAND, width), BF, HBM) for count in (early_pieces, late_pieces)]
        specs += [HBM] * 9
        scratch = [pltpu.VMEM((BAND, width), BF)]
    pays = call(
        functools.partial(pack_body, direct),
        packed,
        specs,
        [pltpu.VMEM(item.shape, BF) for item in held] + scratch + [pltpu.SemaphoreType.DMA((32,))],
        (0, 4 * MIB),
        "pack",
        60,
    )(*acts, *own)
    pay1, pay2, pay3 = pays[:3]

    def to_slots(whole):
        count = whole.shape[0]
        cut = whole.reshape(count, 4, 2, 4, BAND, width).transpose(2, 1, 3, 0, 4, 5)
        return [cut[core, outer] for core in range(2) for outer in range(4)]

    def slot_outs(pieces):
        near = ((4, pieces, BAND, width), BF, HBM)
        return [near] * layers + [((4 * layers, pieces, BAND, width), BF, HBM)]

    def from_slots(parts):
        count = parts[0].shape[1]
        cut = jnp.concatenate(parts, 0).reshape(2, 4, 4, count, BAND, width)
        return cut.transpose(3, 1, 0, 2, 4, 5).reshape(count, width, width)

    def places(piece):
        return [piece] + [swap_seq(piece, k) for k in range(1, 4)]

    def spread(column):
        near = [column] + [swap_dp(column, 2 * k) for k in range(1, layers)]
        return near

    def cross(near):
        return list(near) + [swap_dp(part, 1) for part in near]

    early_layout = plain_layout(early_pieces)
    late_layout = split_layout(late_pieces) if direct else plain_layout(late_pieces)
    if direct:
        early, late = pays[3:]
        early_places = places(early)
        late = after(late, early_places[1], early_places[2])
        late_places = places(late)
        early_near = spread(jnp.stack(early_places))
        column = jnp.stack(late_places)
        column = after(column, *early_near)
        pay1, pay2, pay3 = lax.optimization_barrier((pay1, pay2, pay3, *late_places))[:3]
        got1, got2, got3 = (
            swap_seq(pay1, 1),
            swap_seq(pay2, 2, lambda source, target: target != 1),
            swap_seq(pay3, 3, lambda source, target: target != 1),
        )
        early_full = early_near + cross(lax.optimization_barrier((early_near, got1, got2, got3))[0])[4:]
        half = late_pieces // 2
        near1, near2 = (swap_dp(column, 2), swap_dp(column, 4))
        near3 = [swap_dp(near1[:, :half], 4), swap_dp(near2[:, half:], 2)]
    if not direct:
        got1, got2, got3 = (
            swap_seq(pay1, 1),
            swap_seq(pay2, 2, lambda source, target: target != 1),
            swap_seq(pay3, 3, lambda source, target: target != 1),
        )

        def columns(weight):
            return weight.reshape(weight.shape[0], chunks, width).transpose(1, 0, 2)

        def whole(pieces):
            return lax.all_gather(pieces, ("dp", "seq"), axis=1, tiled=True)

        early_full = to_slots(whole(jnp.stack([w_query, w_key, w_value, pos_table.T])))
        vectors = jnp.concatenate([norm_gain, norm_bias], 0)
        vectors = lax.all_gather(vectors, ("dp", "seq"), axis=1, tiled=True)
        vectors = jnp.pad(vectors, ((0, width - 4), (0, 0)))
        late_whole = whole(jnp.concatenate([w_out[None], columns(w_up), columns(w_down.T)], 0))
        late_full = to_slots(jnp.concatenate([late_whole, vectors[None]], 0))

    groups = width // LANES
    first, low, low_queries, queries, key_rows, values, probs, mixed = call(
        functools.partial(attend_body, direct, early_layout),
        [
            ((rows, width), F32, VMEM),
            ((keys, width), BF, VMEM),
            ((rows, width), BF, VMEM),
            ((rows, width), BF, VMEM),
            ((keys, width), BF, VMEM),
            ((keys, width), BF, VMEM),
            ((groups, 2 * rows, keys), BF, VMEM),
            ((rows, width), BF, VMEM),
        ],
        [SMEM] * 2 + [VMEM] * 5 + [HBM] * len(early_layout),
        [
            pltpu.VMEM((early_pieces, width, width), BF),
            pltpu.VMEM((width, width), F32),
            pltpu.VMEM((keys, width), F32),
            pltpu.SemaphoreType.DMA,
        ],
        (8 * keys * square, 10 * MIB),
        "attend",
        24,
    )(long_lengths, short_lengths, long_tokens, short_tokens, got1, got2, got3, *early_full)

    if direct:
        near3, first = lax.optimization_barrier((near3, first))
        late_near = [column, near1, near2]
        late_far = [swap_dp(part, 1) for part in late_near + list(near3)]
        late_full = late_near + list(near3) + late_far
    block = (n_long, width)
    middle_outs = call(
        functools.partial(middle_body, direct, late_layout),
        [((keys, width), BF, VMEM)]
        + [((rows, width), F32, VMEM), ((rows, width), BF, VMEM)]
        + slot_outs(late_pieces),
        [VMEM] * 7 + [HBM] * len(late_layout),
        [
            pltpu.VMEM((late_pieces, width, width), BF),
            pltpu.VMEM((late_pieces, width, width), BF),
            pltpu.VMEM((chunks, rows, width), BF),
            pltpu.VMEM((chunks, rows, width), F32),
            pltpu.VMEM((keys, width), F32),
            pltpu.VMEM((rows, width), F32),
            pltpu.SemaphoreType.DMA,
        ],
        (16 * rows * square * chunks, 20 * MIB),
        "middle",
        32,
    )(first, mixed, long_cot, short_cot, got1, got2, got3, *late_full)
    out_blocks, grad_sum, grad_mixed = middle_outs[:3]
    late_parts = middle_outs[3:]

    def core_sums(parts, arrived):
        return [
            (parts[k].astype(F32) + arrived[4 * k : 4 * k + 4].astype(F32)).astype(BF)
            for k in range(1, layers)
        ]

    if direct:
        late_arrived = swap_dp(late_parts[-1], 1)

    grad_q, grad_k, grad_v, back_rows, *grad_blocks = call(
        functools.partial(attend_back_body, direct, early_layout),
        [
            ((rows, width), BF, VMEM),
            ((keys, width), BF, VMEM),
            ((keys, width), BF, VMEM),
            ((keys, width), F32, VMEM),
            (block, F32, VMEM),
            ((2 * n_long, width), BF, VMEM),
            (block, BF, VMEM),
            (block, BF, VMEM),
        ],
        [VMEM] * 7 + [HBM] * len(early_layout),
        [pltpu.VMEM((early_pieces, width, width), BF), pltpu.SemaphoreType.DMA],
        (16 * keys * square, 12 * MIB),
        "attend_back",
        24,
    )(grad_mixed, queries, key_rows, values, probs, grad_sum, out_blocks, *early_full)
    early_parts = call(
        functools.partial(leave_body, direct),
        slot_outs(early_pieces),
        [VMEM] * 6,
        [
            pltpu.VMEM((early_pieces, width, width), BF),
            pltpu.VMEM((width, width), F32),
            pltpu.SemaphoreType.DMA,
        ],
        (6 * keys * square, 8 * MIB),
        "leave",
        24,
    )(low, low_queries, grad_q, grad_k, grad_v, back_rows)

    back = lambda source, target: source != 1
    got = [swap_seq(grad_blocks[1], 1)] + [swap_seq(grad_blocks[k], k, back) for k in (2, 3)]
    row_outs = [(item.shape, BF, VMEM) for item in (long_tokens, short_tokens)] * 2
    if direct:
        half = late_pieces // 2
        near0, near1, near2, near3 = late_parts[:4]
        far = late_arrived
        pair = ((2, 4, half, BAND, width), BF, 1)
        single = ((4, half, BAND, width), BF, 0)
        to_x, to_y = sum_call(
            functools.partial(first_sums_body, half),
            [pair, pair],
            [near1, near2, near3, far, far, far],
            [one_place(item) for item in (near1, near2, near3)] + [one_place(far, k) for k in (1, 2, 3)],
            4,
            "late_sums_1",
        )
        from_x, from_y = (swap_dp(to_x, 2), swap_dp(to_y, 4))
        early_far = early_parts[-1]
        early_arrived = swap_dp(early_far, 1)
        early_sums = core_sums(early_parts, early_arrived)
        from_x, from_y, early_sums = lax.optimization_barrier((from_x, from_y, early_sums))
        second = pl.BlockSpec((1, 1, half, BAND, width), lambda i: (1, i, 0, 0, 0))
        then_x, then_y = sum_call(
            functools.partial(second_sums_body, half),
            [single, single],
            [near1, near2, far, far, from_x, from_y],
            [one_place(near1), one_place(near2), one_place(far, 1), one_place(far, 2), second, second],
            4,
            "late_sums_2",
        )
        then_x, then_y = (swap_dp(then_x, 2), swap_dp(then_y, 4))
        early_layers = [swap_dp(part, 2 * k) for k, part in enumerate(early_sums, 1)]
        then_x, then_y, got = lax.optimization_barrier((then_x, then_y, got))
        late_cut = cut_sums(
            functools.partial(last_sums_body, half),
            [near0, far, from_x, from_y, then_x, then_y],
            late_pieces,
            "late_sums_3",
        )
        late_ends = [late_cut[0]] + [swap_seq(late_cut[k], k) for k in range(1, 4)]
        early_cut = cut_sums(
            four_sums_body, [early_parts[0], early_arrived] + early_layers, early_pieces, "early_sums"
        )
        early_ends = [early_cut[0]] + [swap_seq(early_cut[k], k) for k in range(1, 4)]
        row_ins = [grad_blocks[0], out_blocks, *got]
        ends = call(
            finish_body,
            row_outs
            + [((shard, width), F32, VMEM)] * 5
            + [((shard, hidden), F32, VMEM)] * 2
            + [((2, shard), F32, VMEM)] * 2,
            [VMEM] * 13,
            [],
            (0, MIB),
            "finish",
            16,
        )(*late_ends, *early_ends, *row_ins)
        row_grads, early_sum = (ends[:4], ends[4:8])
        grad_out, grad_up, grad_down, grad_gain, grad_bias = ends[8:]
    else:

        def scatter(parts):
            whole_sum = from_slots(parts).astype(F32)
            return lax.psum_scatter(whole_sum, ("dp", "seq"), scatter_dimension=1, tiled=True)

        def join(pieces):
            return pieces.transpose(1, 0, 2).reshape(shard, hidden)

        late_sum = scatter(late_parts)
        early_sum = scatter(early_parts)
        grad_out, grad_up, grad_down = (
            late_sum[0],
            join(late_sum[1 : 1 + chunks]),
            join(late_sum[1 + chunks : 1 + 2 * chunks]),
        )
        norms = lax.psum(from_slots(late_parts)[-1, :BAND].astype(F32), ("dp", "seq"))
        norms = lax.dynamic_slice(norms, (0, device * shard), (BAND, shard))
        grad_gain, grad_bias = (norms[:2], norms[2:4])
        row_grads = call(
            return_rows, row_outs, [VMEM] * 5, [], (0, MIB), "return", 16
        )(grad_blocks[0], out_blocks, *got)
    long_grad, short_grad, long_out, short_out = row_grads
    return (
        long_out,
        short_out,
        long_grad,
        short_grad,
        early_sum[0],
        early_sum[1],
        early_sum[2],
        grad_out,
        grad_up,
        grad_down.T,
        early_sum[3].T,
        grad_gain,
        grad_bias,
    )


def solution(mesh):
    rows = P(("dp", "seq"), None)
    cols = P(None, ("dp", "seq"))
    acts = P("dp", "seq", None)
    return jax.shard_map(
        functools.partial(local, mesh.shape["dp"], mesh.shape["seq"]),
        mesh=mesh,
        in_specs=(acts,) * 4 + (P("dp"),) * 2 + (rows,) * 5 + (cols,) * 4,
        out_specs=(acts,) * 4 + (rows,) * 5 + (cols,) * 4,
        check_vma=False,
    )
```

```python
import functools
import math

import jax
import jax.numpy as jnp
from jax import lax
from jax.experimental import pallas as pl
from jax.experimental.pallas import tpu as pltpu
from jax.sharding import PartitionSpec as P

HEAD_DIM = 64
LANES = 128
BAND = 16
MIB = 1024 * 1024
BF = jnp.bfloat16
F32 = jnp.float32
VMEM = pl.BlockSpec(memory_space=pltpu.VMEM)
SMEM = pl.BlockSpec(memory_space=pltpu.SMEM)
HBM = pl.BlockSpec(memory_space=pltpu.HBM)
NN = (((1,), (0,)), ((), ()))
NT = (((1,), (1,)), ((), ()))
TN = (((0,), (0,)), ((), ()))


def mm(left, right, dims=NN, precision=None):
    return lax.dot_general(left, right, dims, precision, preferred_element_type=F32)


def call(body, outs, ins, scratch, cost, name, limit):
    flops, moved = cost
    return pl.pallas_call(
        body,
        out_shape=[jax.ShapeDtypeStruct(shape, dtype) for shape, dtype, _ in outs],
        out_specs=[spec for _, _, spec in outs],
        in_specs=ins,
        scratch_shapes=scratch,
        compiler_params=pltpu.CompilerParams(vmem_limit_bytes=limit * MIB),
        cost_estimate=pl.CostEstimate(flops=flops, bytes_accessed=moved, transcendentals=0),
        name=name,
    )


def own_place():
    seq = lax.axis_index("seq")
    return lax.axis_index("dp") * 4 + seq, seq


def slot_rows(core, layer, place, me):
    device = lax.bitwise_xor(jnp.int32((layer * 2 + core) * 4 + place), me)
    return pl.ds(pl.multiple_of(device * BAND, BAND), BAND)


def plain_layout(pieces):
    return [(core, layer, 0, pieces) for core in range(2) for layer in range(4)]


def split_layout(pieces):
    half = pieces // 2
    per_core = [(layer, 0, pieces) for layer in range(3)] + [(3, 0, half), (3, half, half)]
    return [(core,) + item for core in range(2) for item in per_core]


def fetch_weights(layout, parts, weights, sem, me):
    for (core, layer, first, count), part in zip(layout, parts):
        for place in range(4):
            rows = slot_rows(core, layer, place, me)
            target = weights.at[pl.ds(first, count), rows, :]
            pltpu.make_async_copy(part.at[place], target, sem).start()


def store_slots(grads, parts, sem, me):
    for core in range(2):
        for layer in range(4):
            for place in range(4):
                slot = parts[4].at[layer * 4 + place] if core else parts[layer].at[place]
                rows = slot_rows(core, layer, place, me)
                pltpu.make_async_copy(grads.at[:, rows, :], slot, sem).start()
    pltpu.make_async_copy(grads, grads, sem).wait()


def has_long(seq):
    return (seq == 1) | (seq == 2)


def pick(seq, *options):
    chosen = options[-1]
    for i in range(len(options) - 2, -1, -1):
        chosen = jnp.where(seq == i, options[i], chosen)
    return chosen


def pad_rows(part, rows):
    return jnp.concatenate([part, jnp.zeros((rows - part.shape[0], part.shape[1]), part.dtype)], 0)


def pack_body(with_weights, *refs):
    me, seq = own_place()
    count = 9 if with_weights else 4
    sources, refs = (refs[:count], refs[count:])
    outs = 4 if with_weights else 3
    targets, held, sem = (refs[:outs], refs[outs : outs + count], refs[-1])
    pay1, pay2, pay3 = targets[:3]
    ins = [
        pltpu.make_async_copy(source, there, sem.at[i])
        for i, (source, there) in enumerate(zip(sources, held))
    ]
    for item in ins:
        item.start()
    long_tok, short_tok, long_cot, short_cot = held[:4]
    n_long, n_short = (long_tok.shape[1], short_tok.shape[1])
    copies = []

    def copy(source, target):
        item = pltpu.make_async_copy(source, target, sem.at[len(copies)])
        item.start()
        copies.append(item)

    if with_weights:
        late = targets[3]
        row = refs[outs + count]
        width = late.shape[2]
        gain, bias = held[7:]
        shard = gain.shape[1]
        col = lax.broadcasted_iota(jnp.int32, (shard, width), 1)
        at = lax.broadcasted_iota(jnp.int32, (shard, width), 0)
        spread = (col == at + me * shard).astype(BF)
    for item in ins:
        item.wait()
    if with_weights:
        wo, up, down = held[4:7]
        chunks = up.shape[1] // width
        vectors = jnp.concatenate([mm(gain[...], spread), mm(bias[...], spread)], 0)
        row[...] = pad_rows(vectors, BAND).astype(BF)
        copy(wo, late.at[0])
        for c in range(chunks):
            cols = pl.ds(c * width, width)
            copy(up.at[:, cols], late.at[1 + c])
            copy(down.at[:, cols], late.at[1 + chunks + c])
        copy(row, late.at[1 + 2 * chunks])
    last = len(copies)

    def rest(pairs):
        ends = [
            pltpu.make_async_copy(source, target, sem.at[last + i])
            for i, (source, target) in enumerate(pairs)
        ]
        for item in ends:
            item.start()
        for item in ends:
            item.wait()

    def halves(pay, one, two, rows):
        half = pay.shape[0] // 2
        return [(one, pay.at[pl.ds(0, rows), :]), (two, pay.at[pl.ds(half, rows), :])]

    longs = [long_tok.at[0], long_cot.at[0], n_long]
    zeros, ones = ([short_tok.at[i], short_cot.at[i], n_short] for i in range(2))
    plans = (
        halves(pay1, *longs) + [(long_tok.at[0], pay2)] + halves(pay3, *ones),
        halves(pay1, *zeros) + halves(pay2, *ones) + [(long_tok.at[0], pay3)],
        halves(pay1, *ones) + halves(pay2, *zeros),
        halves(pay1, *longs) + halves(pay3, *zeros),
    )
    for place, plan in enumerate(plans):

        @pl.when(seq == place)
        def _(plan=plan):
            rest(plan)

    for item in copies:
        item.wait()


def early_pack_body(*refs):
    sources, early, held, sem = (refs[:4], refs[4], refs[5], refs[6])
    for i, source in enumerate(sources):
        pltpu.make_async_copy(source, held.at[i], sem.at[i]).start()
    for i, source in enumerate(sources):
        pltpu.make_async_copy(source, held.at[i], sem.at[i]).wait()
    pltpu.make_async_copy(held, early, sem.at[0]).start()
    pltpu.make_async_copy(held, early, sem.at[0]).wait()


def stack_heads(block, lane):
    zero = jnp.zeros_like(block)
    return jnp.concatenate([jnp.where(lane, block, zero), jnp.where(lane, zero, block)], 0)


def join_heads(stacked, lane):
    half = stacked.shape[0] // 2
    return jnp.where(lane, stacked[:half], stacked[half:])


def head_lanes():
    return lax.broadcasted_iota(jnp.int32, (1, LANES), 1) < HEAD_DIM


def block_base(seq, k, size):
    owner = lax.bitwise_xor(seq, jnp.int32(k))
    return pl.multiple_of(owner * jnp.where(has_long(seq), size, size // 2), size // 2)


def gather_queries(seq, source, target):
    size = source.shape[0] // 4
    half = size // 2

    @pl.when(seq == 1)
    def _():
        target[:size, :] = source[size : 2 * size, :]
        target[size:, :] = source[:size, :]

    @pl.when(seq == 2)
    def _():
        target[...] = source[: 2 * size, :]

    @pl.when((seq == 0) | (seq == 3))
    def _():
        for k in range(4):
            target[k * half : (k + 1) * half, :] = source[k * size : k * size + half, :]


def spread_queries(seq, value, target):
    size = target.shape[0] // 4
    half = size // 2

    @pl.when(seq == 1)
    def _():
        target[size : 2 * size, :] += value[:size]
        target[:size, :] += value[size:]

    @pl.when(seq == 2)
    def _():
        target[: 2 * size, :] += value

    @pl.when((seq == 0) | (seq == 3))
    def _():
        for k in range(4):
            target[k * size : k * size + half, :] += value[k * half : (k + 1) * half]


def row_blocks(seq, whole, shorts, one, two, three):
    rows, half = (whole.shape[1], shorts.shape[1])
    longs = has_long(seq)
    own_short = pad_rows(jnp.where(seq == 0, shorts[0], shorts[1]), rows)
    return (
        jnp.where(longs, whole[0], own_short),
        jnp.where(longs, one, pad_rows(one[:half], rows)),
        two,
        three,
    )


def attend_body(direct, layout, long_len, short_len, *refs):
    count = len(layout)
    long_tok, short_tok, got1, got2, got3 = refs[:5]
    parts, refs = (refs[5 : 5 + count], refs[5 + count :])
    first_o, low_o, lowq_o, q_o, k_o, v_o, probs_o, mix_o = refs[:8]
    weights, table, first, sem = refs[8:]
    me, seq = own_place()
    me = me if direct else jnp.int32(0)
    fetch_weights(layout, parts, weights, sem, me)
    n_long, n_short = (long_tok.shape[1], short_tok.shape[1])
    longs = has_long(seq)
    two, three = (
        jnp.where(longs, got[...], pad_rows(got[:n_short, :], n_long)) for got in (got2, got3)
    )
    blocks = row_blocks(seq, long_tok, short_tok, got1[:n_long, :], two, three)
    for k, block in enumerate(blocks):
        first[k * n_long : (k + 1) * n_long, :] = block.astype(F32)
    pltpu.make_async_copy(weights, weights, sem).wait()
    table[...] = weights[3].astype(F32).T
    for k in range(4):
        rows = slice(k * n_long, (k + 1) * n_long)
        first[rows, :] += table[pl.ds(block_base(seq, k, n_long), n_long), :]
    gather_queries(seq, first, first_o)
    lowq_o[...] = first_o[...].astype(BF)
    low_o[...] = first[...].astype(BF)
    k_o[...] = mm(low_o[...], weights[1]).astype(BF)
    v_o[...] = mm(low_o[...], weights[2]).astype(BF)
    q_o[...] = mm(lowq_o[...], weights[0]).astype(BF) * BF(HEAD_DIM**-0.5)
    rows, keys = (first_o.shape[0], first.shape[0])
    row = lax.broadcasted_iota(jnp.int32, (rows, 1), 0)
    row_pos = jnp.where(
        longs,
        row + (seq - 1) * rows,
        lax.bitwise_xor(row // n_short, jnp.full_like(row, seq)) * n_short + row % n_short,
    )
    row_pos = jnp.concatenate([row_pos, row_pos], 0)
    col = lax.broadcasted_iota(jnp.int32, (1, keys), 1)
    owner = lax.bitwise_xor(col // n_long, jnp.full_like(col, seq))
    inner = col % n_long
    col_pos = jnp.where(longs, owner * n_long + inner, owner * n_short + inner)
    length = pick(seq, short_len[0], long_len[0], long_len[0], short_len[1])
    seen = (col_pos < length) & (longs | (inner < n_short))
    col_pos = jnp.where(seen, col_pos, jnp.int32(1 << 20))
    allowed = col_pos <= row_pos
    lane = head_lanes()
    for g in range(first_o.shape[1] // LANES):
        cols = slice(g * LANES, (g + 1) * LANES)
        scores = mm(stack_heads(q_o[:, cols], lane), k_o[:, cols], NT)
        scores = jnp.where(allowed, scores, -1e30)
        shifted = jnp.exp(scores - jnp.max(scores, axis=-1, keepdims=True))
        probs_o[g] = (shifted / jnp.sum(shifted, axis=-1, keepdims=True)).astype(BF)
        mix_o[:, cols] = join_heads(mm(probs_o[g], v_o[:, cols]), lane).astype(BF)


def norm_parts(values):
    mean = jnp.mean(values, axis=-1, keepdims=True)
    centred = values - mean
    scale = lax.rsqrt(jnp.mean(centred * centred, axis=-1, keepdims=True) + 1e-05)
    return centred * scale, scale


def norm_back(cot, gain, xhat, scale):
    scaled = cot * gain
    mean = jnp.mean(scaled, axis=-1, keepdims=True)
    inner = jnp.mean(scaled * xhat, axis=-1, keepdims=True)
    return scale * (scaled - mean - xhat * inner)


def middle_body(direct, layout, first, mixed, long_cot, short_cot, *refs):
    count = len(layout)
    got1, got2, got3 = refs[:3]
    parts, refs = (refs[3 : 3 + count], refs[3 + count :])
    out_o, gsum_o, gmix_o = refs[:3]
    grad_parts = refs[3:8]
    weights, grads, act, slope, cots, sem = refs[8:]
    me, seq = own_place()
    me = me if direct else jnp.int32(0)
    fetch_weights(layout, parts, weights, sem, me)
    n_long, n_short = (long_cot.shape[1], short_cot.shape[1])

    @pl.when(has_long(seq))
    def _():
        own = pl.ds(jnp.where(seq == 1, n_long, 0), n_long)
        other = pl.ds(jnp.where(seq == 1, 0, n_long), n_long)
        cots[own, :] = long_cot[0].astype(F32)
        cots[other, :] = got1[n_long:, :].astype(F32)

    @pl.when((seq == 0) | (seq == 3))
    def _():
        own = jnp.where(seq == 0, short_cot[0], short_cot[1])
        others = (got1[n_long : n_long + n_short, :], got2[n_short:, :], got3[n_short:, :])
        for k, block in enumerate((own,) + others):
            cots[k * n_short : (k + 1) * n_short, :] = block.astype(F32)

    pltpu.make_async_copy(weights, weights, sem).wait()
    width = first.shape[1]
    chunks = (weights.shape[0] - 2) // 2
    norm = weights.shape[0] - 1
    vectors = jnp.sum(weights[norm].astype(F32).reshape(-1, BAND, width), axis=0)
    gain0, gain1, bias0, bias1 = (vectors[i : i + 1] for i in range(4))
    mixed_low = mixed[...]
    xhat0, scale0 = norm_parts(first[...] + mm(mixed_low, weights[0]))
    normed = xhat0 * gain0 + bias0
    normed_low = normed.astype(BF)
    second = normed
    for c in range(chunks):
        hidden = mm(normed_low, weights[1 + c])
        cdf = 0.5 + 0.5 * lax.erf(hidden * (0.5**0.5))
        slope[c] = cdf + hidden * jnp.exp(-0.5 * hidden * hidden) * ((2 * math.pi) ** -0.5)
        act[c] = (hidden * cdf).astype(BF)
        second = second + mm(act[c], weights[1 + chunks + c], NT)
    xhat1, scale1 = norm_parts(second)
    result = (xhat1 * gain1 + bias1).astype(BF)
    out_o[...] = jnp.zeros_like(out_o)
    spread_queries(seq, result, out_o)
    cot_wide = cots[...]
    grad_second = norm_back(cot_wide, gain1, xhat1, scale1)
    second_low = grad_second.astype(BF)
    grad_normed = grad_second
    for c in range(chunks):
        hidden_low = (mm(second_low, weights[1 + chunks + c]) * slope[c]).astype(BF)
        grads[1 + chunks + c] = mm(second_low, act[c], TN).astype(BF)
        grads[1 + c] = mm(normed_low, hidden_low, TN).astype(BF)
        grad_normed = grad_normed + mm(hidden_low, weights[1 + c], NT)
    grad_sum = norm_back(grad_normed, gain0, xhat0, scale0)
    gsum_o[...] = grad_sum
    sum_low = grad_sum.astype(BF)
    gmix_o[...] = mm(sum_low, weights[0], NT).astype(BF)
    grads[0] = mm(mixed_low, sum_low, TN).astype(BF)
    terms = jnp.concatenate(
        [
            jnp.sum(grad_normed * xhat0, axis=0, keepdims=True),
            jnp.sum(cot_wide * xhat1, axis=0, keepdims=True),
            jnp.sum(grad_normed, axis=0, keepdims=True),
            jnp.sum(cot_wide, axis=0, keepdims=True),
            jnp.zeros((BAND - 4, width), F32),
        ],
        0,
    ).astype(BF)
    for d in range(width // BAND):
        grads[norm, d * BAND : (d + 1) * BAND, :] = terms
    store_slots(grads, grad_parts, sem, me)


def attend_back_body(direct, layout, gmix, q, k, v, probs_i, gsum, outs, *refs):
    count = len(layout)
    parts, refs = (refs[:count], refs[count:])
    dq_o, dk_o, dv_o, back_o, own_o, sent1_o, sent2_o, sent3_o, weights, sem = refs
    me, seq = own_place()
    fetch_weights(layout, parts, weights, sem, me if direct else jnp.int32(0))
    lane = head_lanes()
    scale = HEAD_DIM**-0.5
    for g in range(gmix.shape[1] // LANES):
        cols = slice(g * LANES, (g + 1) * LANES)
        grads = stack_heads(gmix[:, cols], lane)
        queries = stack_heads(q[:, cols], lane)
        probs = probs_i[g]
        grad_probs = mm(grads, v[:, cols], NT)
        spread = probs.astype(F32)
        inner = jnp.sum(spread * grad_probs, axis=-1, keepdims=True)
        grad_scores = (spread * (grad_probs - inner)).astype(BF)
        grad_q = mm(grad_scores, k[:, cols])
        dq_o[:, cols] = (join_heads(grad_q, lane) * scale).astype(BF)
        dk_o[:, cols] = mm(grad_scores, queries, TN).astype(BF)
        dv_o[:, cols] = mm(probs, grads, TN).astype(BF)
    pltpu.make_async_copy(weights, weights, sem).wait()
    back_o[...] = mm(dk_o[...], weights[1], NT) + mm(dv_o[...], weights[2], NT)
    spread_queries(seq, gsum[...] + mm(dq_o[...], weights[0], NT), back_o)
    size = own_o.shape[0]
    for k, target in enumerate((own_o, sent1_o, sent2_o, sent3_o)):
        piece = back_o[k * size : (k + 1) * size, :]
        target[:size, :] = piece.astype(target.dtype)
        if k == 1:
            target[size:, :] = outs[size : 2 * size, :]
        elif k > 1:
            half = size // 2
            both = jnp.concatenate(
                [piece[:half].astype(BF), outs[k * size : k * size + half, :]], 0
            )
            target[...] = jnp.where(has_long(seq), piece.astype(BF), both)


def leave_body(direct, low, lowq, dq, dk, dv, back, *refs):
    grad_parts, (grads, table, sem) = (refs[:5], refs[5:])
    me, seq = own_place()
    me = me if direct else jnp.int32(0)
    grads[0] = mm(lowq[...], dq[...], TN).astype(BF)
    grads[1] = mm(low[...], dk[...], TN).astype(BF)
    grads[2] = mm(low[...], dv[...], TN).astype(BF)
    size = back.shape[0] // 4
    table[...] = jnp.zeros_like(table)
    for k in range(4):
        table[pl.ds(block_base(seq, k, size), size), :] += back[k * size : (k + 1) * size, :]
    grads[3] = table[...].T.astype(BF)
    store_slots(grads, grad_parts, sem, me)


def return_rows(own, outs, got1, got2, got3, long_grad, short_grad, long_out, short_out):
    seq = own_place()[1]
    size, half = (long_grad.shape[1], short_grad.shape[1])
    for i, (mine, long_o, short_o) in enumerate(((own, long_grad, short_grad), (outs, long_out, short_out))):
        mine = mine[:size, :].astype(F32)
        one = got1[i * size : (i + 1) * size, :].astype(F32)
        if i == 0:
            two, three = (got[...].astype(F32) for got in (got2, got3))
            long_o[0] = pick(seq, one + two, mine + three, mine, one).astype(BF)
        else:
            long_o[0] = pick(seq, one, mine, mine, one).astype(BF)
        two, three = (got[i * half : (i + 1) * half, :].astype(F32) for got in (got2, got3))
        mine, one = (mine[:half], one[:half])
        short_o[0] = pick(seq, mine, one, two, three).astype(BF)
        short_o[1] = pick(seq, three, two, one, mine).astype(BF)


def wide(ref, *index):
    return ref[index].astype(F32)


def sum_call(body, outs, ins, blocks_in, steps, name):
    def spec(shape, axis):
        block = tuple(1 if i == axis else size for i, size in enumerate(shape))
        return pl.BlockSpec(block, lambda i: tuple(i if a == axis else 0 for a in range(len(shape))))

    return pl.pallas_call(
        body,
        grid=(steps,),
        out_shape=[jax.ShapeDtypeStruct(shape, dtype) for shape, dtype, _ in outs],
        in_specs=blocks_in,
        out_specs=[spec(shape, axis) for shape, _, axis in outs],
        compiler_params=pltpu.CompilerParams(vmem_limit_bytes=16 * MIB),
        name=name,
    )(*ins)


def one_place(part, layer=0):
    shape = part.shape
    return pl.BlockSpec((1,) + shape[1:], lambda i: (layer * 4 + i,) + (0,) * (len(shape) - 1))


def first_sums_body(half, near1, near2, near3, far1, far2, far3, to_x, to_y, last_x, last_y):
    to_y[0] = (wide(near3, 0)[:half] + wide(far3, 0)[:half]).astype(BF)
    to_x[0] = (wide(near3, 0)[half:] + wide(far3, 0)[half:]).astype(BF)
    last_y[0] = (wide(near2, 0)[:half] + wide(far2, 0)[:half]).astype(BF)
    last_x[0] = (wide(near1, 0)[half:] + wide(far1, 0)[half:]).astype(BF)


def second_sums_body(half, near1, near2, far1, far2, from_x, from_y, to_x, to_y):
    to_x[0] = (wide(near1, 0)[:half] + wide(far1, 0)[:half] + wide(from_y, 0)).astype(BF)
    to_y[0] = (wide(near2, 0)[half:] + wide(far2, 0)[half:] + wide(from_x, 0)).astype(BF)


def last_sums_body(half, near0, far0, from_x, from_y, then_x, then_y, *outs):
    for place, out in enumerate(outs):
        low = wide(near0, place)[:half] + wide(far0, place)[:half]
        low = low + (wide(from_y, place) + wide(then_x, place))
        out[:half] = low.astype(out.dtype)
        high = wide(near0, place)[half:] + wide(far0, place)[half:]
        high = high + (wide(from_x, place) + wide(then_y, place))
        out[half:] = high.astype(out.dtype)


def four_sums_body(*refs):
    ins, outs = (refs[:-4], refs[-4:])
    for place, out in enumerate(outs):
        total = wide(ins[0], place)
        for item in ins[1:]:
            total = total + wide(item, place)
        out[...] = total.astype(out.dtype)


def cut_sums(body, parts, pieces, name):
    _, _, band, width = parts[0].shape

    def whole(part):
        shape = part.shape
        shape = (1,) + shape[1:] if len(shape) == 5 else (4,) + shape[1:]
        return pl.BlockSpec(shape, lambda i: (0,) * len(shape))

    out = pl.BlockSpec((pieces, band, width), lambda i: (0, 0, 0))
    return pl.pallas_call(
        body,
        grid=(1,),
        out_shape=[
            jax.ShapeDtypeStruct((pieces, band, width), F32 if place == 0 else BF)
            for place in range(4)
        ],
        in_specs=[whole(part) for part in parts],
        out_specs=[out] * 4,
        compiler_params=pltpu.CompilerParams(vmem_limit_bytes=24 * MIB),
        name=name,
    )(*parts)


def finish_body(*refs):
    late, early, rows = (refs[:4], refs[4:8], refs[8:13])
    row_outs, early_outs = (refs[13:17], refs[17:21])
    out_o, up_o, down_o, gain_o, bias_o = refs[21:]
    width = out_o.shape[1]
    chunks = up_o.shape[1] // width

    def total(parts, i):
        own, one, two, three = parts
        return own[i] + (one[i].astype(F32) + two[i].astype(F32) + three[i].astype(F32))

    return_rows(*rows, *row_outs)
    out_o[...] = total(late, 0)
    for c in range(chunks):
        up_o[:, c * width : (c + 1) * width] = total(late, 1 + c)
        down_o[:, c * width : (c + 1) * width] = total(late, 1 + chunks + c)
    shard = gain_o.shape[1]
    row = lax.broadcasted_iota(jnp.int32, (width, shard), 0)
    col = lax.broadcasted_iota(jnp.int32, (width, shard), 1)
    chosen = (row == col + own_place()[0] * shard).astype(F32)
    norms = mm(total(late, 1 + 2 * chunks), chosen, NN, lax.Precision.HIGHEST)
    gain_o[...] = norms[:2]
    bias_o[...] = norms[2:4]
    for i, out in enumerate(early_outs):
        out[...] = total(early, i)


def after(value, *others):
    return lax.optimization_barrier((value,) + others)[0]


def local(
    dp_count,
    seq_count,
    long_tokens,
    short_tokens,
    long_cot,
    short_cot,
    long_lengths,
    short_lengths,
    w_query,
    w_key,
    w_value,
    w_out,
    w_up,
    w_down,
    pos_table,
    norm_gain,
    norm_bias,
):
    width = w_key.shape[1]
    hidden = w_up.shape[1]
    chunks = hidden // width
    shard = w_key.shape[0]
    direct = shard == BAND and dp_count == 8
    layers = 4
    device = lax.axis_index("dp") * seq_count + lax.axis_index("seq")
    n_long, n_short = (long_tokens.shape[1], short_tokens.shape[1])
    rows, keys = (2 * n_long, 4 * n_long)
    square = width * width
    early_pieces, late_pieces = (4, 2 + 2 * chunks)

    def swap_seq(value, mask, keep=lambda source, target: True):
        pairs = [(i, i ^ mask) for i in range(seq_count) if keep(i, i ^ mask)]
        return lax.ppermute(value, "seq", pairs)

    def swap_dp(value, mask):
        return lax.ppermute(value, "dp", [(i, i ^ mask) for i in range(dp_count)])

    acts = [long_tokens, short_tokens, long_cot, short_cot]
    packed = [
        ((2 * n_long, width), BF, HBM),
        ((n_long, width), BF, HBM),
        ((n_long, width), BF, HBM),
    ]
    own, specs, scratch = ([], [HBM] * 4, [])
    held = list(acts)
    if direct:
        own = [w_out, w_up, w_down.T]
        own += [norm_gain, norm_bias]
        held += own
        packed += [((late_pieces, BAND, width), BF, HBM)]
        specs += [HBM] * 5
        scratch = [pltpu.VMEM((BAND, width), BF)]
    pays = call(
        functools.partial(pack_body, direct),
        packed,
        specs,
        [pltpu.VMEM(item.shape, BF) for item in held] + scratch + [pltpu.SemaphoreType.DMA((32,))],
        (0, 4 * MIB),
        "pack",
        60,
    )(*acts, *own)
    pay1, pay2, pay3 = pays[:3]

    def to_slots(whole):
        count = whole.shape[0]
        cut = whole.reshape(count, 4, 2, 4, BAND, width).transpose(2, 1, 3, 0, 4, 5)
        return [cut[core, outer] for core in range(2) for outer in range(4)]

    def slot_outs(pieces):
        near = ((4, pieces, BAND, width), BF, HBM)
        return [near] * layers + [((4 * layers, pieces, BAND, width), BF, HBM)]

    def from_slots(parts):
        count = parts[0].shape[1]
        cut = jnp.concatenate(parts, 0).reshape(2, 4, 4, count, BAND, width)
        return cut.transpose(3, 1, 0, 2, 4, 5).reshape(count, width, width)

    def places(piece):
        return [piece] + [swap_seq(piece, k) for k in range(1, 4)]

    def spread(column):
        near = [column] + [swap_dp(column, 2 * k) for k in range(1, layers)]
        return near

    def cross(near):
        return list(near) + [swap_dp(part, 1) for part in near]

    early_layout = plain_layout(early_pieces)
    late_layout = split_layout(late_pieces) if direct else plain_layout(late_pieces)
    if direct:
        late = pays[3]
        shape = (early_pieces, BAND, width)
        early = call(
            early_pack_body,
            [(shape, BF, HBM)],
            [HBM] * 4,
            [pltpu.VMEM(shape, BF), pltpu.SemaphoreType.DMA((4,))],
            (0, MIB),
            "early_pack",
            60,
        )(w_query, w_key, w_value, pos_table.T)[0]
        early_places = places(early)
        late = after(late, early_places[1], early_places[2])
        late_places = places(late)
        early_near = spread(jnp.stack(early_places))
        column = jnp.stack(late_places)
        column = after(column, *early_near)
        pay1, pay2, pay3 = lax.optimization_barrier((pay1, pay2, pay3, *late_places))[:3]
        got1, got2, got3 = (
            swap_seq(pay1, 1),
            swap_seq(pay2, 2, lambda source, target: target != 1),
            swap_seq(pay3, 3, lambda source, target: target != 1),
        )
        early_full = early_near + cross(lax.optimization_barrier((early_near, got1, got2, got3))[0])[4:]
        half = late_pieces // 2
        near1, near2 = (swap_dp(column, 2), swap_dp(column, 4))
        near3 = [swap_dp(near1[:, :half], 4), swap_dp(near2[:, half:], 2)]
    if not direct:
        got1, got2, got3 = (
            swap_seq(pay1, 1),
            swap_seq(pay2, 2, lambda source, target: target != 1),
            swap_seq(pay3, 3, lambda source, target: target != 1),
        )

        def columns(weight):
            return weight.reshape(weight.shape[0], chunks, width).transpose(1, 0, 2)

        def whole(pieces):
            return lax.all_gather(pieces, ("dp", "seq"), axis=1, tiled=True)

        early_full = to_slots(whole(jnp.stack([w_query, w_key, w_value, pos_table.T])))
        vectors = jnp.concatenate([norm_gain, norm_bias], 0)
        vectors = lax.all_gather(vectors, ("dp", "seq"), axis=1, tiled=True)
        vectors = jnp.pad(vectors, ((0, width - 4), (0, 0)))
        late_whole = whole(jnp.concatenate([w_out[None], columns(w_up), columns(w_down.T)], 0))
        late_full = to_slots(jnp.concatenate([late_whole, vectors[None]], 0))

    groups = width // LANES
    first, low, low_queries, queries, key_rows, values, probs, mixed = call(
        functools.partial(attend_body, direct, early_layout),
        [
            ((rows, width), F32, VMEM),
            ((keys, width), BF, VMEM),
            ((rows, width), BF, VMEM),
            ((rows, width), BF, VMEM),
            ((keys, width), BF, VMEM),
            ((keys, width), BF, VMEM),
            ((groups, 2 * rows, keys), BF, VMEM),
            ((rows, width), BF, VMEM),
        ],
        [SMEM] * 2 + [VMEM] * 5 + [HBM] * len(early_layout),
        [
            pltpu.VMEM((early_pieces, width, width), BF),
            pltpu.VMEM((width, width), F32),
            pltpu.VMEM((keys, width), F32),
            pltpu.SemaphoreType.DMA,
        ],
        (8 * keys * square, 10 * MIB),
        "attend",
        24,
    )(long_lengths, short_lengths, long_tokens, short_tokens, got1, got2, got3, *early_full)

    if direct:
        near3, first = lax.optimization_barrier((near3, first))
        late_near = [column, near1, near2]
        late_far = [swap_dp(part, 1) for part in late_near + list(near3)]
        late_full = late_near + list(near3) + late_far
    block = (n_long, width)
    middle_outs = call(
        functools.partial(middle_body, direct, late_layout),
        [((keys, width), BF, VMEM)]
        + [((rows, width), F32, VMEM), ((rows, width), BF, VMEM)]
        + slot_outs(late_pieces),
        [VMEM] * 7 + [HBM] * len(late_layout),
        [
            pltpu.VMEM((late_pieces, width, width), BF),
            pltpu.VMEM((late_pieces, width, width), BF),
            pltpu.VMEM((chunks, rows, width), BF),
            pltpu.VMEM((chunks, rows, width), F32),
            pltpu.VMEM((rows, width), F32),
            pltpu.SemaphoreType.DMA,
        ],
        (16 * rows * square * chunks, 20 * MIB),
        "middle",
        32,
    )(first, mixed, long_cot, short_cot, got1, got2, got3, *late_full)
    out_blocks, grad_sum, grad_mixed = middle_outs[:3]
    late_parts = middle_outs[3:]

    def core_sums(parts, arrived):
        return [
            (parts[k].astype(F32) + arrived[4 * k : 4 * k + 4].astype(F32)).astype(BF)
            for k in range(1, layers)
        ]

    if direct:
        late_arrived = swap_dp(late_parts[-1], 1)

    grad_q, grad_k, grad_v, back_rows, *grad_blocks = call(
        functools.partial(attend_back_body, direct, early_layout),
        [
            ((rows, width), BF, VMEM),
            ((keys, width), BF, VMEM),
            ((keys, width), BF, VMEM),
            ((keys, width), F32, VMEM),
            (block, F32, VMEM),
            ((2 * n_long, width), BF, VMEM),
            (block, BF, VMEM),
            (block, BF, VMEM),
        ],
        [VMEM] * 7 + [HBM] * len(early_layout),
        [pltpu.VMEM((early_pieces, width, width), BF), pltpu.SemaphoreType.DMA],
        (16 * keys * square, 12 * MIB),
        "attend_back",
        24,
    )(grad_mixed, queries, key_rows, values, probs, grad_sum, out_blocks, *early_full)
    early_parts = call(
        functools.partial(leave_body, direct),
        slot_outs(early_pieces),
        [VMEM] * 6,
        [
            pltpu.VMEM((early_pieces, width, width), BF),
            pltpu.VMEM((width, width), F32),
            pltpu.SemaphoreType.DMA,
        ],
        (6 * keys * square, 8 * MIB),
        "leave",
        24,
    )(low, low_queries, grad_q, grad_k, grad_v, back_rows)

    back = lambda source, target: source != 1
    got = [swap_seq(grad_blocks[1], 1)] + [swap_seq(grad_blocks[k], k, back) for k in (2, 3)]
    row_outs = [(item.shape, BF, VMEM) for item in (long_tokens, short_tokens)] * 2
    if direct:
        half = late_pieces // 2
        near0, near1, near2, near3 = late_parts[:4]
        far = late_arrived
        single = ((4, half, BAND, width), BF, 0)
        to_x, to_y, last_x, last_y = sum_call(
            functools.partial(first_sums_body, half),
            [single] * 4,
            [near1, near2, near3, far, far, far],
            [one_place(item) for item in (near1, near2, near3)] + [one_place(far, k) for k in (1, 2, 3)],
            4,
            "late_sums_1",
        )
        from_x, from_y = (swap_dp(to_x, 2), swap_dp(to_y, 4))
        last_x, last_y = (swap_dp(last_x, 2), swap_dp(last_y, 4))
        early_far = early_parts[-1]
        early_arrived = swap_dp(early_far, 1)
        early_sums = core_sums(early_parts, early_arrived)
        from_x, from_y, early_sums = lax.optimization_barrier((from_x, from_y, early_sums))
        then_x, then_y = sum_call(
            functools.partial(second_sums_body, half),
            [single, single],
            [near1, near2, far, far, from_x, from_y],
            [one_place(near1), one_place(near2), one_place(far, 1), one_place(far, 2), one_place(from_x), one_place(from_y)],
            4,
            "late_sums_2",
        )
        then_x, then_y = (swap_dp(then_x, 2), swap_dp(then_y, 4))
        early_sums = lax.optimization_barrier((early_sums, last_x, last_y))[0]
        early_layers = [swap_dp(part, 2 * k) for k, part in enumerate(early_sums, 1)]
        then_x, then_y, got = lax.optimization_barrier((then_x, then_y, got))
        late_cut = cut_sums(
            functools.partial(last_sums_body, half),
            [near0, far, last_x, last_y, then_x, then_y],
            late_pieces,
            "late_sums_3",
        )
        late_ends = [late_cut[0]] + [swap_seq(late_cut[k], k) for k in range(1, 4)]
        early_cut = cut_sums(
            four_sums_body, [early_parts[0], early_arrived] + early_layers, early_pieces, "early_sums"
        )
        early_ends = [early_cut[0]] + [swap_seq(early_cut[k], k) for k in range(1, 4)]
        row_ins = [grad_blocks[0], out_blocks, *got]
        ends = call(
            finish_body,
            row_outs
            + [((shard, width), F32, VMEM)] * 5
            + [((shard, hidden), F32, VMEM)] * 2
            + [((2, shard), F32, VMEM)] * 2,
            [VMEM] * 13,
            [],
            (0, MIB),
            "finish",
            16,
        )(*late_ends, *early_ends, *row_ins)
        row_grads, early_sum = (ends[:4], ends[4:8])
        grad_out, grad_up, grad_down, grad_gain, grad_bias = ends[8:]
    else:

        def scatter(parts):
            whole_sum = from_slots(parts).astype(F32)
            return lax.psum_scatter(whole_sum, ("dp", "seq"), scatter_dimension=1, tiled=True)

        def join(pieces):
            return pieces.transpose(1, 0, 2).reshape(shard, hidden)

        late_sum = scatter(late_parts)
        early_sum = scatter(early_parts)
        grad_out, grad_up, grad_down = (
            late_sum[0],
            join(late_sum[1 : 1 + chunks]),
            join(late_sum[1 + chunks : 1 + 2 * chunks]),
        )
        norms = lax.psum(from_slots(late_parts)[-1, :BAND].astype(F32), ("dp", "seq"))
        norms = lax.dynamic_slice(norms, (0, device * shard), (BAND, shard))
        grad_gain, grad_bias = (norms[:2], norms[2:4])
        row_grads = call(
            return_rows, row_outs, [VMEM] * 5, [], (0, MIB), "return", 16
        )(grad_blocks[0], out_blocks, *got)
    long_grad, short_grad, long_out, short_out = row_grads
    return (
        long_out,
        short_out,
        long_grad,
        short_grad,
        early_sum[0],
        early_sum[1],
        early_sum[2],
        grad_out,
        grad_up,
        grad_down.T,
        early_sum[3].T,
        grad_gain,
        grad_bias,
    )


def solution(mesh):
    rows = P(("dp", "seq"), None)
    cols = P(None, ("dp", "seq"))
    acts = P("dp", "seq", None)
    return jax.shard_map(
        functools.partial(local, mesh.shape["dp"], mesh.shape["seq"]),
        mesh=mesh,
        in_specs=(acts,) * 4 + (P("dp"),) * 2 + (rows,) * 5 + (cols,) * 4,
        out_specs=(acts,) * 4 + (rows,) * 5 + (cols,) * 4,
        check_vma=False,
    )
```

```python
import functools
import math

import jax
import jax.numpy as jnp
from jax import lax
from jax.experimental import pallas as pl
from jax.experimental.pallas import tpu as pltpu
from jax.sharding import PartitionSpec as P

HEAD_DIM = 64
LANES = 128
BAND = 16
MIB = 1024 * 1024
BF = jnp.bfloat16
F32 = jnp.float32
VMEM = pl.BlockSpec(memory_space=pltpu.VMEM)
SMEM = pl.BlockSpec(memory_space=pltpu.SMEM)
HBM = pl.BlockSpec(memory_space=pltpu.HBM)
NN = (((1,), (0,)), ((), ()))
NT = (((1,), (1,)), ((), ()))
TN = (((0,), (0,)), ((), ()))


def mm(left, right, dims=NN, precision=None):
    return lax.dot_general(left, right, dims, precision, preferred_element_type=F32)


def call(body, outs, ins, scratch, cost, name, limit):
    flops, moved = cost
    return pl.pallas_call(
        body,
        out_shape=[jax.ShapeDtypeStruct(shape, dtype) for shape, dtype, _ in outs],
        out_specs=[spec for _, _, spec in outs],
        in_specs=ins,
        scratch_shapes=scratch,
        compiler_params=pltpu.CompilerParams(vmem_limit_bytes=limit * MIB),
        cost_estimate=pl.CostEstimate(flops=flops, bytes_accessed=moved, transcendentals=0),
        name=name,
    )


def own_place():
    seq = lax.axis_index("seq")
    return lax.axis_index("dp") * 4 + seq, seq


def slot_rows(core, layer, place, me):
    device = lax.bitwise_xor(jnp.int32((layer * 2 + core) * 4 + place), me)
    return pl.ds(pl.multiple_of(device * BAND, BAND), BAND)


def plain_layout(pieces):
    return [(core, layer, 0, pieces) for core in range(2) for layer in range(4)]


def split_layout(pieces):
    half = pieces // 2
    per_core = [(layer, 0, pieces) for layer in range(3)] + [(3, 0, half), (3, half, half)]
    return [(core,) + item for core in range(2) for item in per_core]


def fetch_weights(layout, parts, weights, sem, me):
    for (core, layer, first, count), part in zip(layout, parts):
        for place in range(4):
            rows = slot_rows(core, layer, place, me)
            target = weights.at[pl.ds(first, count), rows, :]
            pltpu.make_async_copy(part.at[place], target, sem).start()


def store_slots(grads, parts, sem, me):
    for core in range(2):
        for layer in range(4):
            for place in range(4):
                slot = parts[4].at[layer * 4 + place] if core else parts[layer].at[place]
                rows = slot_rows(core, layer, place, me)
                pltpu.make_async_copy(grads.at[:, rows, :], slot, sem).start()
    pltpu.make_async_copy(grads, grads, sem).wait()


def has_long(seq):
    return (seq == 1) | (seq == 2)


def pick(seq, *options):
    chosen = options[-1]
    for i in range(len(options) - 2, -1, -1):
        chosen = jnp.where(seq == i, options[i], chosen)
    return chosen


def pad_rows(part, rows):
    return jnp.concatenate([part, jnp.zeros((rows - part.shape[0], part.shape[1]), part.dtype)], 0)


def pack_body(with_weights, *refs):
    me, seq = own_place()
    count = 9 if with_weights else 4
    sources, refs = (refs[:count], refs[count:])
    outs = 4 if with_weights else 3
    targets, held, sem = (refs[:outs], refs[outs : outs + count], refs[-1])
    pay1, pay2, pay3 = targets[:3]
    ins = [
        pltpu.make_async_copy(source, there, sem.at[i])
        for i, (source, there) in enumerate(zip(sources, held))
    ]
    for item in ins:
        item.start()
    long_tok, short_tok, long_cot, short_cot = held[:4]
    n_long, n_short = (long_tok.shape[1], short_tok.shape[1])
    copies = []

    def copy(source, target):
        item = pltpu.make_async_copy(source, target, sem.at[len(copies)])
        item.start()
        copies.append(item)

    if with_weights:
        late = targets[3]
        row = refs[outs + count]
        width = late.shape[2]
        gain, bias = held[7:]
        shard = gain.shape[1]
        col = lax.broadcasted_iota(jnp.int32, (shard, width), 1)
        at = lax.broadcasted_iota(jnp.int32, (shard, width), 0)
        spread = (col == at + me * shard).astype(BF)
    for item in ins:
        item.wait()
    if with_weights:
        wo, up, down = held[4:7]
        chunks = up.shape[1] // width
        vectors = jnp.concatenate([mm(gain[...], spread), mm(bias[...], spread)], 0)
        row[...] = pad_rows(vectors, BAND).astype(BF)
        copy(wo, late.at[0])
        for c in range(chunks):
            cols = pl.ds(c * width, width)
            copy(up.at[:, cols], late.at[1 + c])
            copy(down.at[:, cols], late.at[1 + chunks + c])
        copy(row, late.at[1 + 2 * chunks])
    last = len(copies)

    def rest(pairs):
        ends = [
            pltpu.make_async_copy(source, target, sem.at[last + i])
            for i, (source, target) in enumerate(pairs)
        ]
        for item in ends:
            item.start()
        for item in ends:
            item.wait()

    def halves(pay, one, two, rows):
        half = pay.shape[0] // 2
        return [(one, pay.at[pl.ds(0, rows), :]), (two, pay.at[pl.ds(half, rows), :])]

    longs = [long_tok.at[0], long_cot.at[0], n_long]
    zeros, ones = ([short_tok.at[i], short_cot.at[i], n_short] for i in range(2))
    plans = (
        halves(pay1, *longs) + [(long_tok.at[0], pay2)] + halves(pay3, *ones),
        halves(pay1, *zeros) + halves(pay2, *ones) + [(long_tok.at[0], pay3)],
        halves(pay1, *ones) + halves(pay2, *zeros),
        halves(pay1, *longs) + halves(pay3, *zeros),
    )
    for place, plan in enumerate(plans):

        @pl.when(seq == place)
        def _(plan=plan):
            rest(plan)

    for item in copies:
        item.wait()


def stack_heads(block, lane):
    zero = jnp.zeros_like(block)
    return jnp.concatenate([jnp.where(lane, block, zero), jnp.where(lane, zero, block)], 0)


def join_heads(stacked, lane):
    half = stacked.shape[0] // 2
    return jnp.where(lane, stacked[:half], stacked[half:])


def head_lanes():
    return lax.broadcasted_iota(jnp.int32, (1, LANES), 1) < HEAD_DIM


def block_base(seq, k, size):
    owner = lax.bitwise_xor(seq, jnp.int32(k))
    return pl.multiple_of(owner * jnp.where(has_long(seq), size, size // 2), size // 2)


def gather_queries(seq, source, target):
    size = source.shape[0] // 4
    half = size // 2

    @pl.when(seq == 1)
    def _():
        target[:size, :] = source[size : 2 * size, :]
        target[size:, :] = source[:size, :]

    @pl.when(seq == 2)
    def _():
        target[...] = source[: 2 * size, :]

    @pl.when((seq == 0) | (seq == 3))
    def _():
        for k in range(4):
            target[k * half : (k + 1) * half, :] = source[k * size : k * size + half, :]


def spread_queries(seq, value, target):
    size = target.shape[0] // 4
    half = size // 2

    @pl.when(seq == 1)
    def _():
        target[size : 2 * size, :] += value[:size]
        target[:size, :] += value[size:]

    @pl.when(seq == 2)
    def _():
        target[: 2 * size, :] += value

    @pl.when((seq == 0) | (seq == 3))
    def _():
        for k in range(4):
            target[k * size : k * size + half, :] += value[k * half : (k + 1) * half]


def row_blocks(seq, whole, shorts, one, two, three):
    rows, half = (whole.shape[1], shorts.shape[1])
    longs = has_long(seq)
    own_short = pad_rows(jnp.where(seq == 0, shorts[0], shorts[1]), rows)
    return (
        jnp.where(longs, whole[0], own_short),
        jnp.where(longs, one, pad_rows(one[:half], rows)),
        two,
        three,
    )


def attend_body(direct, layout, long_len, short_len, *refs):
    count = len(layout)
    long_tok, short_tok, got1, got2, got3 = refs[:5]
    parts, refs = (refs[5 : 5 + count], refs[5 + count :])
    first_o, low_o, lowq_o, q_o, k_o, v_o, probs_o, mix_o = refs[:8]
    weights, table, first, sem = refs[8:]
    me, seq = own_place()
    me = me if direct else jnp.int32(0)
    fetch_weights(layout, parts, weights, sem, me)
    n_long, n_short = (long_tok.shape[1], short_tok.shape[1])
    longs = has_long(seq)
    two, three = (
        jnp.where(longs, got[...], pad_rows(got[:n_short, :], n_long)) for got in (got2, got3)
    )
    blocks = row_blocks(seq, long_tok, short_tok, got1[:n_long, :], two, three)
    for k, block in enumerate(blocks):
        first[k * n_long : (k + 1) * n_long, :] = block.astype(F32)
    pltpu.make_async_copy(weights, weights, sem).wait()
    table[...] = weights[3].astype(F32).T
    for k in range(4):
        rows = slice(k * n_long, (k + 1) * n_long)
        first[rows, :] += table[pl.ds(block_base(seq, k, n_long), n_long), :]
    gather_queries(seq, first, first_o)
    lowq_o[...] = first_o[...].astype(BF)
    low_o[...] = first[...].astype(BF)
    k_o[...] = mm(low_o[...], weights[1]).astype(BF)
    v_o[...] = mm(low_o[...], weights[2]).astype(BF)
    q_o[...] = mm(lowq_o[...], weights[0]).astype(BF) * BF(HEAD_DIM**-0.5)
    rows, keys = (first_o.shape[0], first.shape[0])
    row = lax.broadcasted_iota(jnp.int32, (rows, 1), 0)
    row_pos = jnp.where(
        longs,
        row + (seq - 1) * rows,
        lax.bitwise_xor(row // n_short, jnp.full_like(row, seq)) * n_short + row % n_short,
    )
    row_pos = jnp.concatenate([row_pos, row_pos], 0)
    col = lax.broadcasted_iota(jnp.int32, (1, keys), 1)
    owner = lax.bitwise_xor(col // n_long, jnp.full_like(col, seq))
    inner = col % n_long
    col_pos = jnp.where(longs, owner * n_long + inner, owner * n_short + inner)
    length = pick(seq, short_len[0], long_len[0], long_len[0], short_len[1])
    seen = (col_pos < length) & (longs | (inner < n_short))
    col_pos = jnp.where(seen, col_pos, jnp.int32(1 << 20))
    allowed = col_pos <= row_pos
    lane = head_lanes()
    for g in range(first_o.shape[1] // LANES):
        cols = slice(g * LANES, (g + 1) * LANES)
        scores = mm(stack_heads(q_o[:, cols], lane), k_o[:, cols], NT)
        scores = jnp.where(allowed, scores, -1e30)
        shifted = jnp.exp(scores - jnp.max(scores, axis=-1, keepdims=True))
        probs_o[g] = (shifted / jnp.sum(shifted, axis=-1, keepdims=True)).astype(BF)
        mix_o[:, cols] = join_heads(mm(probs_o[g], v_o[:, cols]), lane).astype(BF)


def norm_parts(values):
    mean = jnp.mean(values, axis=-1, keepdims=True)
    centred = values - mean
    scale = lax.rsqrt(jnp.mean(centred * centred, axis=-1, keepdims=True) + 1e-05)
    return centred * scale, scale


def norm_back(cot, gain, xhat, scale):
    scaled = cot * gain
    mean = jnp.mean(scaled, axis=-1, keepdims=True)
    inner = jnp.mean(scaled * xhat, axis=-1, keepdims=True)
    return scale * (scaled - mean - xhat * inner)


def middle_body(direct, layout, first, mixed, long_cot, short_cot, *refs):
    count = len(layout)
    got1, got2, got3 = refs[:3]
    parts, refs = (refs[3 : 3 + count], refs[3 + count :])
    out_o, gsum_o, gmix_o = refs[:3]
    grad_parts = refs[3:8]
    weights, grads, act, slope, cots, sem = refs[8:]
    me, seq = own_place()
    me = me if direct else jnp.int32(0)
    fetch_weights(layout, parts, weights, sem, me)
    n_long, n_short = (long_cot.shape[1], short_cot.shape[1])

    @pl.when(has_long(seq))
    def _():
        own = pl.ds(jnp.where(seq == 1, n_long, 0), n_long)
        other = pl.ds(jnp.where(seq == 1, 0, n_long), n_long)
        cots[own, :] = long_cot[0].astype(F32)
        cots[other, :] = got1[n_long:, :].astype(F32)

    @pl.when((seq == 0) | (seq == 3))
    def _():
        own = jnp.where(seq == 0, short_cot[0], short_cot[1])
        others = (got1[n_long : n_long + n_short, :], got2[n_short:, :], got3[n_short:, :])
        for k, block in enumerate((own,) + others):
            cots[k * n_short : (k + 1) * n_short, :] = block.astype(F32)

    pltpu.make_async_copy(weights, weights, sem).wait()
    width = first.shape[1]
    chunks = (weights.shape[0] - 2) // 2
    norm = weights.shape[0] - 1
    vectors = jnp.sum(weights[norm].astype(F32).reshape(-1, BAND, width), axis=0)
    gain0, gain1, bias0, bias1 = (vectors[i : i + 1] for i in range(4))
    mixed_low = mixed[...]
    xhat0, scale0 = norm_parts(first[...] + mm(mixed_low, weights[0]))
    normed = xhat0 * gain0 + bias0
    normed_low = normed.astype(BF)
    second = normed
    for c in range(chunks):
        hidden = mm(normed_low, weights[1 + c])
        cdf = 0.5 + 0.5 * lax.erf(hidden * (0.5**0.5))
        slope[c] = cdf + hidden * jnp.exp(-0.5 * hidden * hidden) * ((2 * math.pi) ** -0.5)
        act[c] = (hidden * cdf).astype(BF)
        second = second + mm(act[c], weights[1 + chunks + c], NT)
    xhat1, scale1 = norm_parts(second)
    result = (xhat1 * gain1 + bias1).astype(BF)
    out_o[...] = jnp.zeros_like(out_o)
    spread_queries(seq, result, out_o)
    cot_wide = cots[...]
    grad_second = norm_back(cot_wide, gain1, xhat1, scale1)
    second_low = grad_second.astype(BF)
    grad_normed = grad_second
    for c in range(chunks):
        hidden_low = (mm(second_low, weights[1 + chunks + c]) * slope[c]).astype(BF)
        grads[1 + chunks + c] = mm(second_low, act[c], TN).astype(BF)
        grads[1 + c] = mm(normed_low, hidden_low, TN).astype(BF)
        grad_normed = grad_normed + mm(hidden_low, weights[1 + c], NT)
    grad_sum = norm_back(grad_normed, gain0, xhat0, scale0)
    gsum_o[...] = grad_sum
    sum_low = grad_sum.astype(BF)
    gmix_o[...] = mm(sum_low, weights[0], NT).astype(BF)
    grads[0] = mm(mixed_low, sum_low, TN).astype(BF)
    terms = jnp.concatenate(
        [
            jnp.sum(grad_normed * xhat0, axis=0, keepdims=True),
            jnp.sum(cot_wide * xhat1, axis=0, keepdims=True),
            jnp.sum(grad_normed, axis=0, keepdims=True),
            jnp.sum(cot_wide, axis=0, keepdims=True),
            jnp.zeros((BAND - 4, width), F32),
        ],
        0,
    ).astype(BF)
    for d in range(width // BAND):
        grads[norm, d * BAND : (d + 1) * BAND, :] = terms
    store_slots(grads, grad_parts, sem, me)


def attend_back_body(direct, layout, gmix, q, k, v, probs_i, gsum, outs, *refs):
    count = len(layout)
    parts, refs = (refs[:count], refs[count:])
    dq_o, dk_o, dv_o, back_o, own_o, sent1_o, sent2_o, sent3_o, weights, sem = refs
    me, seq = own_place()
    fetch_weights(layout, parts, weights, sem, me if direct else jnp.int32(0))
    lane = head_lanes()
    scale = HEAD_DIM**-0.5
    for g in range(gmix.shape[1] // LANES):
        cols = slice(g * LANES, (g + 1) * LANES)
        grads = stack_heads(gmix[:, cols], lane)
        queries = stack_heads(q[:, cols], lane)
        probs = probs_i[g]
        grad_probs = mm(grads, v[:, cols], NT)
        spread = probs.astype(F32)
        inner = jnp.sum(spread * grad_probs, axis=-1, keepdims=True)
        grad_scores = (spread * (grad_probs - inner)).astype(BF)
        grad_q = mm(grad_scores, k[:, cols])
        dq_o[:, cols] = (join_heads(grad_q, lane) * scale).astype(BF)
        dk_o[:, cols] = mm(grad_scores, queries, TN).astype(BF)
        dv_o[:, cols] = mm(probs, grads, TN).astype(BF)
    pltpu.make_async_copy(weights, weights, sem).wait()
    back_o[...] = mm(dk_o[...], weights[1], NT) + mm(dv_o[...], weights[2], NT)
    spread_queries(seq, gsum[...] + mm(dq_o[...], weights[0], NT), back_o)
    size = own_o.shape[0]
    for k, target in enumerate((own_o, sent1_o, sent2_o, sent3_o)):
        piece = back_o[k * size : (k + 1) * size, :]
        target[:size, :] = piece.astype(target.dtype)
        if k == 1:
            target[size:, :] = outs[size : 2 * size, :]
        elif k > 1:
            half = size // 2
            both = jnp.concatenate(
                [piece[:half].astype(BF), outs[k * size : k * size + half, :]], 0
            )
            target[...] = jnp.where(has_long(seq), piece.astype(BF), both)


def leave_body(direct, low, lowq, dq, dk, dv, back, *refs):
    grad_parts, (grads, table, sem) = (refs[:5], refs[5:])
    me, seq = own_place()
    me = me if direct else jnp.int32(0)
    grads[0] = mm(lowq[...], dq[...], TN).astype(BF)
    grads[1] = mm(low[...], dk[...], TN).astype(BF)
    grads[2] = mm(low[...], dv[...], TN).astype(BF)
    size = back.shape[0] // 4
    table[...] = jnp.zeros_like(table)
    for k in range(4):
        table[pl.ds(block_base(seq, k, size), size), :] += back[k * size : (k + 1) * size, :]
    grads[3] = table[...].T.astype(BF)
    store_slots(grads, grad_parts, sem, me)


def return_rows(own, outs, got1, got2, got3, long_grad, short_grad, long_out, short_out):
    seq = own_place()[1]
    size, half = (long_grad.shape[1], short_grad.shape[1])
    for i, (mine, long_o, short_o) in enumerate(((own, long_grad, short_grad), (outs, long_out, short_out))):
        mine = mine[:size, :].astype(F32)
        one = got1[i * size : (i + 1) * size, :].astype(F32)
        if i == 0:
            two, three = (got[...].astype(F32) for got in (got2, got3))
            long_o[0] = pick(seq, one + two, mine + three, mine, one).astype(BF)
        else:
            long_o[0] = pick(seq, one, mine, mine, one).astype(BF)
        two, three = (got[i * half : (i + 1) * half, :].astype(F32) for got in (got2, got3))
        mine, one = (mine[:half], one[:half])
        short_o[0] = pick(seq, mine, one, two, three).astype(BF)
        short_o[1] = pick(seq, three, two, one, mine).astype(BF)


def wide(ref, *index):
    return ref[index].astype(F32)


def sum_call(body, outs, ins, blocks_in, steps, name):
    def spec(shape, axis):
        block = tuple(1 if i == axis else size for i, size in enumerate(shape))
        return pl.BlockSpec(block, lambda i: tuple(i if a == axis else 0 for a in range(len(shape))))

    return pl.pallas_call(
        body,
        grid=(steps,),
        out_shape=[jax.ShapeDtypeStruct(shape, dtype) for shape, dtype, _ in outs],
        in_specs=blocks_in,
        out_specs=[spec(shape, axis) for shape, _, axis in outs],
        compiler_params=pltpu.CompilerParams(vmem_limit_bytes=16 * MIB),
        name=name,
    )(*ins)


def one_place(part, layer=0):
    shape = part.shape
    return pl.BlockSpec((1,) + shape[1:], lambda i: (layer * 4 + i,) + (0,) * (len(shape) - 1))


def first_sums_body(half, near1, near2, near3, far1, far2, far3, to_x, to_y, last_x, last_y):
    to_y[0] = (wide(near3, 0)[:half] + wide(far3, 0)[:half]).astype(BF)
    to_x[0] = (wide(near3, 0)[half:] + wide(far3, 0)[half:]).astype(BF)
    last_y[0] = (wide(near2, 0)[:half] + wide(far2, 0)[:half]).astype(BF)
    last_x[0] = (wide(near1, 0)[half:] + wide(far1, 0)[half:]).astype(BF)


def second_sums_body(half, near1, near2, far1, far2, from_x, from_y, to_x, to_y):
    to_x[0] = (wide(near1, 0)[:half] + wide(far1, 0)[:half] + wide(from_y, 0)).astype(BF)
    to_y[0] = (wide(near2, 0)[half:] + wide(far2, 0)[half:] + wide(from_x, 0)).astype(BF)


def last_sums_body(half, near0, far0, from_x, from_y, then_x, then_y, *outs):
    for place, out in enumerate(outs):
        low = wide(near0, place)[:half] + wide(far0, place)[:half]
        low = low + (wide(from_y, place) + wide(then_x, place))
        out[:half] = low.astype(out.dtype)
        high = wide(near0, place)[half:] + wide(far0, place)[half:]
        high = high + (wide(from_x, place) + wide(then_y, place))
        out[half:] = high.astype(out.dtype)


def four_sums_body(*refs):
    ins, outs = (refs[:-4], refs[-4:])
    for place, out in enumerate(outs):
        total = wide(ins[0], place)
        for item in ins[1:]:
            total = total + wide(item, place)
        out[...] = total.astype(out.dtype)


def cut_sums(body, parts, pieces, name):
    _, _, band, width = parts[0].shape

    def whole(part):
        shape = part.shape
        shape = (1,) + shape[1:] if len(shape) == 5 else (4,) + shape[1:]
        return pl.BlockSpec(shape, lambda i: (0,) * len(shape))

    out = pl.BlockSpec((pieces, band, width), lambda i: (0, 0, 0))
    return pl.pallas_call(
        body,
        grid=(1,),
        out_shape=[
            jax.ShapeDtypeStruct((pieces, band, width), F32 if place == 0 else BF)
            for place in range(4)
        ],
        in_specs=[whole(part) for part in parts],
        out_specs=[out] * 4,
        compiler_params=pltpu.CompilerParams(vmem_limit_bytes=24 * MIB),
        name=name,
    )(*parts)


def finish_body(*refs):
    late, early, rows = (refs[:4], refs[4:8], refs[8:13])
    row_outs, early_outs = (refs[13:17], refs[17:21])
    out_o, up_o, down_o, gain_o, bias_o = refs[21:]
    width = out_o.shape[1]
    chunks = up_o.shape[1] // width

    def total(parts, i):
        own, one, two, three = parts
        return own[i] + (one[i].astype(F32) + two[i].astype(F32) + three[i].astype(F32))

    return_rows(*rows, *row_outs)
    out_o[...] = total(late, 0)
    for c in range(chunks):
        up_o[:, c * width : (c + 1) * width] = total(late, 1 + c)
        down_o[:, c * width : (c + 1) * width] = total(late, 1 + chunks + c)
    shard = gain_o.shape[1]
    row = lax.broadcasted_iota(jnp.int32, (width, shard), 0)
    col = lax.broadcasted_iota(jnp.int32, (width, shard), 1)
    chosen = (row == col + own_place()[0] * shard).astype(F32)
    norms = mm(total(late, 1 + 2 * chunks), chosen, NN, lax.Precision.HIGHEST)
    gain_o[...] = norms[:2]
    bias_o[...] = norms[2:4]
    for i, out in enumerate(early_outs):
        out[...] = total(early, i)


def after(value, *others):
    return lax.optimization_barrier((value,) + others)[0]


def local(
    dp_count,
    seq_count,
    long_tokens,
    short_tokens,
    long_cot,
    short_cot,
    long_lengths,
    short_lengths,
    w_query,
    w_key,
    w_value,
    w_out,
    w_up,
    w_down,
    pos_table,
    norm_gain,
    norm_bias,
):
    width = w_key.shape[1]
    hidden = w_up.shape[1]
    chunks = hidden // width
    shard = w_key.shape[0]
    direct = shard == BAND and dp_count == 8
    layers = 4
    device = lax.axis_index("dp") * seq_count + lax.axis_index("seq")
    n_long, n_short = (long_tokens.shape[1], short_tokens.shape[1])
    rows, keys = (2 * n_long, 4 * n_long)
    square = width * width
    early_pieces, late_pieces = (4, 2 + 2 * chunks)

    def swap_seq(value, mask, keep=lambda source, target: True):
        pairs = [(i, i ^ mask) for i in range(seq_count) if keep(i, i ^ mask)]
        return lax.ppermute(value, "seq", pairs)

    def swap_dp(value, mask):
        return lax.ppermute(value, "dp", [(i, i ^ mask) for i in range(dp_count)])

    acts = [long_tokens, short_tokens, long_cot, short_cot]
    packed = [
        ((2 * n_long, width), BF, HBM),
        ((n_long, width), BF, HBM),
        ((n_long, width), BF, HBM),
    ]
    own, specs, scratch = ([], [HBM] * 4, [])
    held = list(acts)
    if direct:
        own = [w_out, w_up, w_down.T]
        own += [norm_gain, norm_bias]
        held += own
        packed += [((late_pieces, BAND, width), BF, HBM)]
        specs += [HBM] * 5
        scratch = [pltpu.VMEM((BAND, width), BF)]
    pays = call(
        functools.partial(pack_body, direct),
        packed,
        specs,
        [pltpu.VMEM(item.shape, BF) for item in held] + scratch + [pltpu.SemaphoreType.DMA((32,))],
        (0, 4 * MIB),
        "pack",
        60,
    )(*acts, *own)
    pay1, pay2, pay3 = pays[:3]

    def to_slots(whole):
        count = whole.shape[0]
        cut = whole.reshape(count, 4, 2, 4, BAND, width).transpose(2, 1, 3, 0, 4, 5)
        return [cut[core, outer] for core in range(2) for outer in range(4)]

    def slot_outs(pieces):
        near = ((4, pieces, BAND, width), BF, HBM)
        return [near] * layers + [((4 * layers, pieces, BAND, width), BF, HBM)]

    def from_slots(parts):
        count = parts[0].shape[1]
        cut = jnp.concatenate(parts, 0).reshape(2, 4, 4, count, BAND, width)
        return cut.transpose(3, 1, 0, 2, 4, 5).reshape(count, width, width)

    def places(piece):
        return [piece] + [swap_seq(piece, k) for k in range(1, 4)]

    def spread(column):
        near = [column] + [swap_dp(column, 2 * k) for k in range(1, layers)]
        return near

    def cross(near):
        return list(near) + [swap_dp(part, 1) for part in near]

    early_layout = plain_layout(early_pieces)
    late_layout = split_layout(late_pieces) if direct else plain_layout(late_pieces)
    if direct:
        late = pays[3]
        early = jnp.stack([w_query, w_key, w_value, pos_table.T])
        early_places = places(early)
        late = after(late, early_places[1], early_places[2])
        late_places = places(late)
        early_near = spread(jnp.stack(early_places))
        column = jnp.stack(late_places)
        column = after(column, *early_near)
        pay1, pay2, pay3 = lax.optimization_barrier((pay1, pay2, pay3, *late_places))[:3]
        got1, got2, got3 = (
            swap_seq(pay1, 1),
            swap_seq(pay2, 2, lambda source, target: target != 1),
            swap_seq(pay3, 3, lambda source, target: target != 1),
        )
        early_full = early_near + cross(lax.optimization_barrier((early_near, got1, got2, got3))[0])[4:]
        half = late_pieces // 2
        near1, near2 = (swap_dp(column, 2), swap_dp(column, 4))
        near3 = [swap_dp(near1[:, :half], 4), swap_dp(near2[:, half:], 2)]
    if not direct:
        got1, got2, got3 = (
            swap_seq(pay1, 1),
            swap_seq(pay2, 2, lambda source, target: target != 1),
            swap_seq(pay3, 3, lambda source, target: target != 1),
        )

        def columns(weight):
            return weight.reshape(weight.shape[0], chunks, width).transpose(1, 0, 2)

        def whole(pieces):
            return lax.all_gather(pieces, ("dp", "seq"), axis=1, tiled=True)

        early_full = to_slots(whole(jnp.stack([w_query, w_key, w_value, pos_table.T])))
        vectors = jnp.concatenate([norm_gain, norm_bias], 0)
        vectors = lax.all_gather(vectors, ("dp", "seq"), axis=1, tiled=True)
        vectors = jnp.pad(vectors, ((0, width - 4), (0, 0)))
        late_whole = whole(jnp.concatenate([w_out[None], columns(w_up), columns(w_down.T)], 0))
        late_full = to_slots(jnp.concatenate([late_whole, vectors[None]], 0))

    groups = width // LANES
    first, low, low_queries, queries, key_rows, values, probs, mixed = call(
        functools.partial(attend_body, direct, early_layout),
        [
            ((rows, width), F32, VMEM),
            ((keys, width), BF, VMEM),
            ((rows, width), BF, VMEM),
            ((rows, width), BF, VMEM),
            ((keys, width), BF, VMEM),
            ((keys, width), BF, VMEM),
            ((groups, 2 * rows, keys), BF, VMEM),
            ((rows, width), BF, VMEM),
        ],
        [SMEM] * 2 + [VMEM] * 5 + [HBM] * len(early_layout),
        [
            pltpu.VMEM((early_pieces, width, width), BF),
            pltpu.VMEM((width, width), F32),
            pltpu.VMEM((keys, width), F32),
            pltpu.SemaphoreType.DMA,
        ],
        (8 * keys * square, 10 * MIB),
        "attend",
        24,
    )(long_lengths, short_lengths, long_tokens, short_tokens, got1, got2, got3, *early_full)

    if direct:
        near3, first = lax.optimization_barrier((near3, first))
        late_near = [column, near1, near2]
        late_far = [swap_dp(part, 1) for part in late_near + list(near3)]
        late_full = late_near + list(near3) + late_far
    block = (n_long, width)
    middle_outs = call(
        functools.partial(middle_body, direct, late_layout),
        [((keys, width), BF, VMEM)]
        + [((rows, width), F32, VMEM), ((rows, width), BF, VMEM)]
        + slot_outs(late_pieces),
        [VMEM] * 7 + [HBM] * len(late_layout),
        [
            pltpu.VMEM((late_pieces, width, width), BF),
            pltpu.VMEM((late_pieces, width, width), BF),
            pltpu.VMEM((chunks, rows, width), BF),
            pltpu.VMEM((chunks, rows, width), F32),
            pltpu.VMEM((rows, width), F32),
            pltpu.SemaphoreType.DMA,
        ],
        (16 * rows * square * chunks, 20 * MIB),
        "middle",
        32,
    )(first, mixed, long_cot, short_cot, got1, got2, got3, *late_full)
    out_blocks, grad_sum, grad_mixed = middle_outs[:3]
    late_parts = middle_outs[3:]

    def core_sums(parts, arrived):
        return [
            (parts[k].astype(F32) + arrived[4 * k : 4 * k + 4].astype(F32)).astype(BF)
            for k in range(1, layers)
        ]

    if direct:
        late_arrived = swap_dp(late_parts[-1], 1)

    grad_q, grad_k, grad_v, back_rows, *grad_blocks = call(
        functools.partial(attend_back_body, direct, early_layout),
        [
            ((rows, width), BF, VMEM),
            ((keys, width), BF, VMEM),
            ((keys, width), BF, VMEM),
            ((keys, width), F32, VMEM),
            (block, F32, VMEM),
            ((2 * n_long, width), BF, VMEM),
            (block, BF, VMEM),
            (block, BF, VMEM),
        ],
        [VMEM] * 7 + [HBM] * len(early_layout),
        [pltpu.VMEM((early_pieces, width, width), BF), pltpu.SemaphoreType.DMA],
        (16 * keys * square, 12 * MIB),
        "attend_back",
        24,
    )(grad_mixed, queries, key_rows, values, probs, grad_sum, out_blocks, *early_full)
    early_parts = call(
        functools.partial(leave_body, direct),
        slot_outs(early_pieces),
        [VMEM] * 6,
        [
            pltpu.VMEM((early_pieces, width, width), BF),
            pltpu.VMEM((width, width), F32),
            pltpu.SemaphoreType.DMA,
        ],
        (6 * keys * square, 8 * MIB),
        "leave",
        24,
    )(low, low_queries, grad_q, grad_k, grad_v, back_rows)

    back = lambda source, target: source != 1
    got = [swap_seq(grad_blocks[1], 1)] + [swap_seq(grad_blocks[k], k, back) for k in (2, 3)]
    row_outs = [(item.shape, BF, VMEM) for item in (long_tokens, short_tokens)] * 2
    if direct:
        half = late_pieces // 2
        near0, near1, near2, near3 = late_parts[:4]
        far = late_arrived
        single = ((4, half, BAND, width), BF, 0)
        to_x, to_y, last_x, last_y = sum_call(
            functools.partial(first_sums_body, half),
            [single] * 4,
            [near1, near2, near3, far, far, far],
            [one_place(item) for item in (near1, near2, near3)] + [one_place(far, k) for k in (1, 2, 3)],
            4,
            "late_sums_1",
        )
        from_x, from_y = (swap_dp(to_x, 2), swap_dp(to_y, 4))
        last_x, last_y = (swap_dp(last_x, 2), swap_dp(last_y, 4))
        early_far = early_parts[-1]
        early_arrived = swap_dp(early_far, 1)
        early_sums = core_sums(early_parts, early_arrived)
        from_x, from_y, early_sums = lax.optimization_barrier((from_x, from_y, early_sums))
        then_x, then_y = sum_call(
            functools.partial(second_sums_body, half),
            [single, single],
            [near1, near2, far, far, from_x, from_y],
            [one_place(near1), one_place(near2), one_place(far, 1), one_place(far, 2), one_place(from_x), one_place(from_y)],
            4,
            "late_sums_2",
        )
        then_x, then_y = (swap_dp(then_x, 2), swap_dp(then_y, 4))
        early_sums = lax.optimization_barrier((early_sums, last_x, last_y))[0]
        early_layers = [swap_dp(part, 2 * k) for k, part in enumerate(early_sums, 1)]
        then_x, then_y, got = lax.optimization_barrier((then_x, then_y, got))
        late_cut = cut_sums(
            functools.partial(last_sums_body, half),
            [near0, far, last_x, last_y, then_x, then_y],
            late_pieces,
            "late_sums_3",
        )
        late_ends = [late_cut[0]] + [swap_seq(late_cut[k], k) for k in range(1, 4)]
        early_cut = cut_sums(
            four_sums_body, [early_parts[0], early_arrived] + early_layers, early_pieces, "early_sums"
        )
        early_ends = [early_cut[0]] + [swap_seq(early_cut[k], k) for k in range(1, 4)]
        row_ins = [grad_blocks[0], out_blocks, *got]
        ends = call(
            finish_body,
            row_outs
            + [((shard, width), F32, VMEM)] * 5
            + [((shard, hidden), F32, VMEM)] * 2
            + [((2, shard), F32, VMEM)] * 2,
            [VMEM] * 13,
            [],
            (0, MIB),
            "finish",
            16,
        )(*late_ends, *early_ends, *row_ins)
        row_grads, early_sum = (ends[:4], ends[4:8])
        grad_out, grad_up, grad_down, grad_gain, grad_bias = ends[8:]
    else:

        def scatter(parts):
            whole_sum = from_slots(parts).astype(F32)
            return lax.psum_scatter(whole_sum, ("dp", "seq"), scatter_dimension=1, tiled=True)

        def join(pieces):
            return pieces.transpose(1, 0, 2).reshape(shard, hidden)

        late_sum = scatter(late_parts)
        early_sum = scatter(early_parts)
        grad_out, grad_up, grad_down = (
            late_sum[0],
            join(late_sum[1 : 1 + chunks]),
            join(late_sum[1 + chunks : 1 + 2 * chunks]),
        )
        norms = lax.psum(from_slots(late_parts)[-1, :BAND].astype(F32), ("dp", "seq"))
        norms = lax.dynamic_slice(norms, (0, device * shard), (BAND, shard))
        grad_gain, grad_bias = (norms[:2], norms[2:4])
        row_grads = call(
            return_rows, row_outs, [VMEM] * 5, [], (0, MIB), "return", 16
        )(grad_blocks[0], out_blocks, *got)
    long_grad, short_grad, long_out, short_out = row_grads
    return (
        long_out,
        short_out,
        long_grad,
        short_grad,
        early_sum[0],
        early_sum[1],
        early_sum[2],
        grad_out,
        grad_up,
        grad_down.T,
        early_sum[3].T,
        grad_gain,
        grad_bias,
    )


def solution(mesh):
    rows = P(("dp", "seq"), None)
    cols = P(None, ("dp", "seq"))
    acts = P("dp", "seq", None)
    return jax.shard_map(
        functools.partial(local, mesh.shape["dp"], mesh.shape["seq"]),
        mesh=mesh,
        in_specs=(acts,) * 4 + (P("dp"),) * 2 + (rows,) * 5 + (cols,) * 4,
        out_specs=(acts,) * 4 + (rows,) * 5 + (cols,) * 4,
        check_vma=False,
    )
```

```python
import functools
import math

import jax
import jax.numpy as jnp
from jax import lax
from jax.experimental import pallas as pl
from jax.experimental.pallas import tpu as pltpu
from jax.sharding import PartitionSpec as P

HEAD_DIM = 64
LANES = 128
BAND = 16
MIB = 1024 * 1024
BF = jnp.bfloat16
F32 = jnp.float32
VMEM = pl.BlockSpec(memory_space=pltpu.VMEM)
SMEM = pl.BlockSpec(memory_space=pltpu.SMEM)
HBM = pl.BlockSpec(memory_space=pltpu.HBM)
NN = (((1,), (0,)), ((), ()))
NT = (((1,), (1,)), ((), ()))
TN = (((0,), (0,)), ((), ()))


def mm(left, right, dims=NN, precision=None):
    return lax.dot_general(left, right, dims, precision, preferred_element_type=F32)


def call(body, outs, ins, scratch, cost, name, limit):
    flops, moved = cost
    return pl.pallas_call(
        body,
        out_shape=[jax.ShapeDtypeStruct(shape, dtype) for shape, dtype, _ in outs],
        out_specs=[spec for _, _, spec in outs],
        in_specs=ins,
        scratch_shapes=scratch,
        compiler_params=pltpu.CompilerParams(vmem_limit_bytes=limit * MIB),
        cost_estimate=pl.CostEstimate(flops=flops, bytes_accessed=moved, transcendentals=0),
        name=name,
    )


def own_place():
    seq = lax.axis_index("seq")
    return lax.axis_index("dp") * 4 + seq, seq


def slot_rows(core, layer, place, me):
    device = lax.bitwise_xor(jnp.int32((layer * 2 + core) * 4 + place), me)
    return pl.ds(pl.multiple_of(device * BAND, BAND), BAND)


def plain_layout(pieces):
    return [(core, layer, 0, pieces) for core in range(2) for layer in range(4)]


def split_layout(pieces):
    half = pieces // 2
    per_core = [(layer, 0, pieces) for layer in range(3)] + [(3, 0, half), (3, half, half)]
    return [(core,) + item for core in range(2) for item in per_core]


def fetch_weights(layout, parts, weights, sem, me):
    for (core, layer, first, count), part in zip(layout, parts):
        for place in range(4):
            rows = slot_rows(core, layer, place, me)
            target = weights.at[pl.ds(first, count), rows, :]
            pltpu.make_async_copy(part.at[place], target, sem).start()


def store_slots(grads, parts, sem, me):
    for core in range(2):
        for layer in range(4):
            for place in range(4):
                slot = parts[4].at[layer * 4 + place] if core else parts[layer].at[place]
                rows = slot_rows(core, layer, place, me)
                pltpu.make_async_copy(grads.at[:, rows, :], slot, sem).start()
    pltpu.make_async_copy(grads, grads, sem).wait()


def has_long(seq):
    return (seq == 1) | (seq == 2)


def pick(seq, *options):
    chosen = options[-1]
    for i in range(len(options) - 2, -1, -1):
        chosen = jnp.where(seq == i, options[i], chosen)
    return chosen


def pad_rows(part, rows):
    return jnp.concatenate([part, jnp.zeros((rows - part.shape[0], part.shape[1]), part.dtype)], 0)


def pack_body(with_weights, *refs):
    me, seq = own_place()
    count = 9 if with_weights else 4
    sources, refs = (refs[:count], refs[count:])
    outs = 4 if with_weights else 3
    targets, held, sem = (refs[:outs], refs[outs : outs + count], refs[-1])
    pay1, pay2, pay3 = targets[:3]
    ins = [
        pltpu.make_async_copy(source, there, sem.at[i])
        for i, (source, there) in enumerate(zip(sources, held))
    ]
    for item in ins:
        item.start()
    long_tok, short_tok, long_cot, short_cot = held[:4]
    n_long, n_short = (long_tok.shape[1], short_tok.shape[1])
    copies = []

    def copy(source, target):
        item = pltpu.make_async_copy(source, target, sem.at[len(copies)])
        item.start()
        copies.append(item)

    if with_weights:
        late = targets[3]
        row = refs[outs + count]
        width = late.shape[2]
        gain, bias = held[7:]
        shard = gain.shape[1]
        col = lax.broadcasted_iota(jnp.int32, (shard, width), 1)
        at = lax.broadcasted_iota(jnp.int32, (shard, width), 0)
        spread = (col == at + me * shard).astype(BF)
    for item in ins:
        item.wait()
    if with_weights:
        wo, up, down = held[4:7]
        chunks = up.shape[1] // width
        vectors = jnp.concatenate([mm(gain[...], spread), mm(bias[...], spread)], 0)
        row[...] = pad_rows(vectors, BAND).astype(BF)
        copy(wo, late.at[0])
        for c in range(chunks):
            cols = pl.ds(c * width, width)
            copy(up.at[:, cols], late.at[1 + c])
            copy(down.at[:, cols], late.at[1 + chunks + c])
        copy(row, late.at[1 + 2 * chunks])
    last = len(copies)

    def rest(pairs):
        ends = [
            pltpu.make_async_copy(source, target, sem.at[last + i])
            for i, (source, target) in enumerate(pairs)
        ]
        for item in ends:
            item.start()
        for item in ends:
            item.wait()

    def halves(pay, one, two, rows):
        half = pay.shape[0] // 2
        return [(one, pay.at[pl.ds(0, rows), :]), (two, pay.at[pl.ds(half, rows), :])]

    longs = [long_tok.at[0], long_cot.at[0], n_long]
    zeros, ones = ([short_tok.at[i], short_cot.at[i], n_short] for i in range(2))
    plans = (
        halves(pay1, *longs) + [(long_tok.at[0], pay2)] + halves(pay3, *ones),
        halves(pay1, *zeros) + halves(pay2, *ones) + [(long_tok.at[0], pay3)],
        halves(pay1, *ones) + halves(pay2, *zeros),
        halves(pay1, *longs) + halves(pay3, *zeros),
    )
    for place, plan in enumerate(plans):

        @pl.when(seq == place)
        def _(plan=plan):
            rest(plan)

    for item in copies:
        item.wait()


def stack_heads(block, lane):
    zero = jnp.zeros_like(block)
    return jnp.concatenate([jnp.where(lane, block, zero), jnp.where(lane, zero, block)], 0)


def join_heads(stacked, lane):
    half = stacked.shape[0] // 2
    return jnp.where(lane, stacked[:half], stacked[half:])


def head_lanes():
    return lax.broadcasted_iota(jnp.int32, (1, LANES), 1) < HEAD_DIM


def block_base(seq, k, size):
    owner = lax.bitwise_xor(seq, jnp.int32(k))
    return pl.multiple_of(owner * jnp.where(has_long(seq), size, size // 2), size // 2)


def gather_queries(seq, source, target):
    size = source.shape[0] // 4
    half = size // 2

    @pl.when(seq == 1)
    def _():
        target[:size, :] = source[size : 2 * size, :]
        target[size:, :] = source[:size, :]

    @pl.when(seq == 2)
    def _():
        target[...] = source[: 2 * size, :]

    @pl.when((seq == 0) | (seq == 3))
    def _():
        for k in range(4):
            target[k * half : (k + 1) * half, :] = source[k * size : k * size + half, :]


def spread_queries(seq, value, target):
    size = target.shape[0] // 4
    half = size // 2

    @pl.when(seq == 1)
    def _():
        target[size : 2 * size, :] += value[:size]
        target[:size, :] += value[size:]

    @pl.when(seq == 2)
    def _():
        target[: 2 * size, :] += value

    @pl.when((seq == 0) | (seq == 3))
    def _():
        for k in range(4):
            target[k * size : k * size + half, :] += value[k * half : (k + 1) * half]


def row_blocks(seq, whole, shorts, one, two, three):
    rows, half = (whole.shape[1], shorts.shape[1])
    longs = has_long(seq)
    own_short = pad_rows(jnp.where(seq == 0, shorts[0], shorts[1]), rows)
    return (
        jnp.where(longs, whole[0], own_short),
        jnp.where(longs, one, pad_rows(one[:half], rows)),
        two,
        three,
    )


def attend_body(direct, layout, long_len, short_len, *refs):
    count = len(layout)
    long_tok, short_tok, got1, got2, got3 = refs[:5]
    parts, refs = (refs[5 : 5 + count], refs[5 + count :])
    first_o, low_o, lowq_o, q_o, k_o, v_o, probs_o, mix_o = refs[:8]
    weights, table, first, sem = refs[8:]
    me, seq = own_place()
    me = me if direct else jnp.int32(0)
    fetch_weights(layout, parts, weights, sem, me)
    n_long, n_short = (long_tok.shape[1], short_tok.shape[1])
    longs = has_long(seq)
    two, three = (
        jnp.where(longs, got[...], pad_rows(got[:n_short, :], n_long)) for got in (got2, got3)
    )
    blocks = row_blocks(seq, long_tok, short_tok, got1[:n_long, :], two, three)
    for k, block in enumerate(blocks):
        first[k * n_long : (k + 1) * n_long, :] = block.astype(F32)
    pltpu.make_async_copy(weights, weights, sem).wait()
    table[...] = weights[3].astype(F32).T
    for k in range(4):
        rows = slice(k * n_long, (k + 1) * n_long)
        first[rows, :] += table[pl.ds(block_base(seq, k, n_long), n_long), :]
    gather_queries(seq, first, first_o)
    lowq_o[...] = first_o[...].astype(BF)
    low_o[...] = first[...].astype(BF)
    k_o[...] = mm(low_o[...], weights[1]).astype(BF)
    v_o[...] = mm(low_o[...], weights[2]).astype(BF)
    q_o[...] = mm(lowq_o[...], weights[0]).astype(BF) * BF(HEAD_DIM**-0.5)
    rows, keys = (first_o.shape[0], first.shape[0])
    row = lax.broadcasted_iota(jnp.int32, (rows, 1), 0)
    row_pos = jnp.where(
        longs,
        row + (seq - 1) * rows,
        lax.bitwise_xor(row // n_short, jnp.full_like(row, seq)) * n_short + row % n_short,
    )
    row_pos = jnp.concatenate([row_pos, row_pos], 0)
    col = lax.broadcasted_iota(jnp.int32, (1, keys), 1)
    owner = lax.bitwise_xor(col // n_long, jnp.full_like(col, seq))
    inner = col % n_long
    col_pos = jnp.where(longs, owner * n_long + inner, owner * n_short + inner)
    length = pick(seq, short_len[0], long_len[0], long_len[0], short_len[1])
    seen = (col_pos < length) & (longs | (inner < n_short))
    col_pos = jnp.where(seen, col_pos, jnp.int32(1 << 20))
    allowed = col_pos <= row_pos
    lane = head_lanes()
    for g in range(first_o.shape[1] // LANES):
        cols = slice(g * LANES, (g + 1) * LANES)
        scores = mm(stack_heads(q_o[:, cols], lane), k_o[:, cols], NT)
        scores = jnp.where(allowed, scores, -1e30)
        shifted = jnp.exp(scores - jnp.max(scores, axis=-1, keepdims=True))
        probs_o[g] = (shifted / jnp.sum(shifted, axis=-1, keepdims=True)).astype(BF)
        mix_o[:, cols] = join_heads(mm(probs_o[g], v_o[:, cols]), lane).astype(BF)


def norm_parts(values):
    mean = jnp.mean(values, axis=-1, keepdims=True)
    centred = values - mean
    scale = lax.rsqrt(jnp.mean(centred * centred, axis=-1, keepdims=True) + 1e-05)
    return centred * scale, scale


def norm_back(cot, gain, xhat, scale):
    scaled = cot * gain
    mean = jnp.mean(scaled, axis=-1, keepdims=True)
    inner = jnp.mean(scaled * xhat, axis=-1, keepdims=True)
    return scale * (scaled - mean - xhat * inner)


def middle_body(direct, layout, first, mixed, long_cot, short_cot, *refs):
    count = len(layout)
    got1, got2, got3 = refs[:3]
    parts, refs = (refs[3 : 3 + count], refs[3 + count :])
    out_o, gsum_o, gmix_o = refs[:3]
    grad_parts = refs[3:8]
    weights, grads, act, slope, cots, sem = refs[8:]
    me, seq = own_place()
    me = me if direct else jnp.int32(0)
    fetch_weights(layout, parts, weights, sem, me)
    n_long, n_short = (long_cot.shape[1], short_cot.shape[1])

    @pl.when(has_long(seq))
    def _():
        own = pl.ds(jnp.where(seq == 1, n_long, 0), n_long)
        other = pl.ds(jnp.where(seq == 1, 0, n_long), n_long)
        cots[own, :] = long_cot[0].astype(F32)
        cots[other, :] = got1[n_long:, :].astype(F32)

    @pl.when((seq == 0) | (seq == 3))
    def _():
        own = jnp.where(seq == 0, short_cot[0], short_cot[1])
        others = (got1[n_long : n_long + n_short, :], got2[n_short:, :], got3[n_short:, :])
        for k, block in enumerate((own,) + others):
            cots[k * n_short : (k + 1) * n_short, :] = block.astype(F32)

    pltpu.make_async_copy(weights, weights, sem).wait()
    width = first.shape[1]
    chunks = (weights.shape[0] - 2) // 2
    norm = weights.shape[0] - 1
    vectors = jnp.sum(weights[norm].astype(F32).reshape(-1, BAND, width), axis=0)
    gain0, gain1, bias0, bias1 = (vectors[i : i + 1] for i in range(4))
    mixed_low = mixed[...]
    xhat0, scale0 = norm_parts(first[...] + mm(mixed_low, weights[0]))
    normed = xhat0 * gain0 + bias0
    normed_low = normed.astype(BF)
    second = normed
    for c in range(chunks):
        hidden = mm(normed_low, weights[1 + c])
        cdf = 0.5 + 0.5 * lax.erf(hidden * (0.5**0.5))
        slope[c] = cdf + hidden * jnp.exp(-0.5 * hidden * hidden) * ((2 * math.pi) ** -0.5)
        act[c] = (hidden * cdf).astype(BF)
        second = second + mm(act[c], weights[1 + chunks + c], NT)
    xhat1, scale1 = norm_parts(second)
    result = (xhat1 * gain1 + bias1).astype(BF)
    out_o[...] = jnp.zeros_like(out_o)
    spread_queries(seq, result, out_o)
    cot_wide = cots[...]
    grad_second = norm_back(cot_wide, gain1, xhat1, scale1)
    second_low = grad_second.astype(BF)
    grad_normed = grad_second
    for c in range(chunks):
        hidden_low = (mm(second_low, weights[1 + chunks + c]) * slope[c]).astype(BF)
        grads[1 + chunks + c] = mm(second_low, act[c], TN).astype(BF)
        grads[1 + c] = mm(normed_low, hidden_low, TN).astype(BF)
        grad_normed = grad_normed + mm(hidden_low, weights[1 + c], NT)
    grad_sum = norm_back(grad_normed, gain0, xhat0, scale0)
    gsum_o[...] = grad_sum
    sum_low = grad_sum.astype(BF)
    gmix_o[...] = mm(sum_low, weights[0], NT).astype(BF)
    grads[0] = mm(mixed_low, sum_low, TN).astype(BF)
    terms = jnp.concatenate(
        [
            jnp.sum(grad_normed * xhat0, axis=0, keepdims=True),
            jnp.sum(cot_wide * xhat1, axis=0, keepdims=True),
            jnp.sum(grad_normed, axis=0, keepdims=True),
            jnp.sum(cot_wide, axis=0, keepdims=True),
            jnp.zeros((BAND - 4, width), F32),
        ],
        0,
    ).astype(BF)
    for d in range(width // BAND):
        grads[norm, d * BAND : (d + 1) * BAND, :] = terms
    store_slots(grads, grad_parts, sem, me)


def attend_back_body(direct, layout, gmix, q, k, v, probs_i, gsum, outs, *refs):
    count = len(layout)
    parts, refs = (refs[:count], refs[count:])
    dq_o, dk_o, dv_o, back_o, own_o, sent1_o, sent2_o, sent3_o, weights, sem = refs
    me, seq = own_place()
    fetch_weights(layout, parts, weights, sem, me if direct else jnp.int32(0))
    lane = head_lanes()
    scale = HEAD_DIM**-0.5
    for g in range(gmix.shape[1] // LANES):
        cols = slice(g * LANES, (g + 1) * LANES)
        grads = stack_heads(gmix[:, cols], lane)
        queries = stack_heads(q[:, cols], lane)
        probs = probs_i[g]
        grad_probs = mm(grads, v[:, cols], NT)
        spread = probs.astype(F32)
        inner = jnp.sum(spread * grad_probs, axis=-1, keepdims=True)
        grad_scores = (spread * (grad_probs - inner)).astype(BF)
        grad_q = mm(grad_scores, k[:, cols])
        dq_o[:, cols] = (join_heads(grad_q, lane) * scale).astype(BF)
        dk_o[:, cols] = mm(grad_scores, queries, TN).astype(BF)
        dv_o[:, cols] = mm(probs, grads, TN).astype(BF)
    pltpu.make_async_copy(weights, weights, sem).wait()
    back_o[...] = mm(dk_o[...], weights[1], NT) + mm(dv_o[...], weights[2], NT)
    spread_queries(seq, gsum[...] + mm(dq_o[...], weights[0], NT), back_o)
    size = own_o.shape[0]
    for k, target in enumerate((own_o, sent1_o, sent2_o, sent3_o)):
        piece = back_o[k * size : (k + 1) * size, :]
        target[:size, :] = piece.astype(target.dtype)
        if k == 1:
            target[size:, :] = outs[size : 2 * size, :]
        elif k > 1:
            half = size // 2
            both = jnp.concatenate(
                [piece[:half].astype(BF), outs[k * size : k * size + half, :]], 0
            )
            target[...] = jnp.where(has_long(seq), piece.astype(BF), both)


def leave_body(direct, low, lowq, dq, dk, dv, back, *refs):
    grad_parts, (grads, table, sem) = (refs[:5], refs[5:])
    me, seq = own_place()
    me = me if direct else jnp.int32(0)
    grads[0] = mm(lowq[...], dq[...], TN).astype(BF)
    grads[1] = mm(low[...], dk[...], TN).astype(BF)
    grads[2] = mm(low[...], dv[...], TN).astype(BF)
    size = back.shape[0] // 4
    table[...] = jnp.zeros_like(table)
    for k in range(4):
        table[pl.ds(block_base(seq, k, size), size), :] += back[k * size : (k + 1) * size, :]
    grads[3] = table[...].T.astype(BF)
    store_slots(grads, grad_parts, sem, me)


def return_rows(own, outs, got1, got2, got3, long_grad, short_grad, long_out, short_out):
    seq = own_place()[1]
    size, half = (long_grad.shape[1], short_grad.shape[1])
    for i, (mine, long_o, short_o) in enumerate(((own, long_grad, short_grad), (outs, long_out, short_out))):
        mine = mine[:size, :].astype(F32)
        one = got1[i * size : (i + 1) * size, :].astype(F32)
        if i == 0:
            two, three = (got[...].astype(F32) for got in (got2, got3))
            long_o[0] = pick(seq, one + two, mine + three, mine, one).astype(BF)
        else:
            long_o[0] = pick(seq, one, mine, mine, one).astype(BF)
        two, three = (got[i * half : (i + 1) * half, :].astype(F32) for got in (got2, got3))
        mine, one = (mine[:half], one[:half])
        short_o[0] = pick(seq, mine, one, two, three).astype(BF)
        short_o[1] = pick(seq, three, two, one, mine).astype(BF)


def wide(ref, *index):
    return ref[index].astype(F32)


def sum_call(body, outs, ins, blocks_in, steps, name):
    def spec(shape, axis):
        block = tuple(1 if i == axis else size for i, size in enumerate(shape))
        return pl.BlockSpec(block, lambda i: tuple(i if a == axis else 0 for a in range(len(shape))))

    return pl.pallas_call(
        body,
        grid=(steps,),
        out_shape=[jax.ShapeDtypeStruct(shape, dtype) for shape, dtype, _ in outs],
        in_specs=blocks_in,
        out_specs=[spec(shape, axis) for shape, _, axis in outs],
        compiler_params=pltpu.CompilerParams(vmem_limit_bytes=16 * MIB),
        name=name,
    )(*ins)


def one_place(part, layer=0):
    shape = part.shape
    return pl.BlockSpec((1,) + shape[1:], lambda i: (layer * 4 + i,) + (0,) * (len(shape) - 1))


def first_sums_body(half, near1, near2, near3, far1, far2, far3, to_x, to_y, last_x, last_y):
    to_y[0] = (wide(near3, 0)[:half] + wide(far3, 0)[:half]).astype(BF)
    to_x[0] = (wide(near3, 0)[half:] + wide(far3, 0)[half:]).astype(BF)
    last_y[0] = (wide(near2, 0)[:half] + wide(far2, 0)[:half]).astype(BF)
    last_x[0] = (wide(near1, 0)[half:] + wide(far1, 0)[half:]).astype(BF)


def second_sums_body(half, near1, near2, far1, far2, from_x, from_y, to_x, to_y):
    to_x[0] = (wide(near1, 0)[:half] + wide(far1, 0)[:half] + wide(from_y, 0)).astype(BF)
    to_y[0] = (wide(near2, 0)[half:] + wide(far2, 0)[half:] + wide(from_x, 0)).astype(BF)


def last_sums_body(half, near0, far0, from_x, from_y, then_x, then_y, *outs):
    for place, out in enumerate(outs):
        low = wide(near0, place)[:half] + wide(far0, place)[:half]
        low = low + (wide(from_y, place) + wide(then_x, place))
        out[:half] = low.astype(out.dtype)
        high = wide(near0, place)[half:] + wide(far0, place)[half:]
        high = high + (wide(from_x, place) + wide(then_y, place))
        out[half:] = high.astype(out.dtype)


def four_sums_body(*refs):
    ins, outs = (refs[:-4], refs[-4:])
    for place, out in enumerate(outs):
        total = wide(ins[0], place)
        for item in ins[1:]:
            total = total + wide(item, place)
        out[...] = total.astype(out.dtype)


def cut_sums(body, parts, pieces, name):
    _, _, band, width = parts[0].shape

    def whole(part):
        shape = part.shape
        shape = (1,) + shape[1:] if len(shape) == 5 else (4,) + shape[1:]
        return pl.BlockSpec(shape, lambda i: (0,) * len(shape))

    out = pl.BlockSpec((pieces, band, width), lambda i: (0, 0, 0))
    return pl.pallas_call(
        body,
        grid=(1,),
        out_shape=[
            jax.ShapeDtypeStruct((pieces, band, width), F32 if place == 0 else BF)
            for place in range(4)
        ],
        in_specs=[whole(part) for part in parts],
        out_specs=[out] * 4,
        compiler_params=pltpu.CompilerParams(vmem_limit_bytes=24 * MIB),
        name=name,
    )(*parts)


def finish_body(*refs):
    late, early, rows = (refs[:4], refs[4:8], refs[8:13])
    row_outs, early_outs = (refs[13:17], refs[17:21])
    out_o, up_o, down_o, gain_o, bias_o = refs[21:]
    width = out_o.shape[1]
    chunks = up_o.shape[1] // width

    def total(parts, i):
        own, one, two, three = parts
        return own[i] + (one[i].astype(F32) + two[i].astype(F32) + three[i].astype(F32))

    return_rows(*rows, *row_outs)
    out_o[...] = total(late, 0)
    for c in range(chunks):
        up_o[:, c * width : (c + 1) * width] = total(late, 1 + c)
        down_o[:, c * width : (c + 1) * width] = total(late, 1 + chunks + c)
    shard = gain_o.shape[1]
    row = lax.broadcasted_iota(jnp.int32, (width, shard), 0)
    col = lax.broadcasted_iota(jnp.int32, (width, shard), 1)
    chosen = (row == col + own_place()[0] * shard).astype(F32)
    norms = mm(total(late, 1 + 2 * chunks), chosen, NN, lax.Precision.HIGHEST)
    gain_o[...] = norms[:2]
    bias_o[...] = norms[2:4]
    for i, out in enumerate(early_outs):
        out[...] = total(early, i)


def after(value, *others):
    return lax.optimization_barrier((value,) + others)[0]


def local(
    dp_count,
    seq_count,
    long_tokens,
    short_tokens,
    long_cot,
    short_cot,
    long_lengths,
    short_lengths,
    w_query,
    w_key,
    w_value,
    w_out,
    w_up,
    w_down,
    pos_table,
    norm_gain,
    norm_bias,
):
    width = w_key.shape[1]
    hidden = w_up.shape[1]
    chunks = hidden // width
    shard = w_key.shape[0]
    direct = shard == BAND and dp_count == 8
    layers = 4
    device = lax.axis_index("dp") * seq_count + lax.axis_index("seq")
    n_long, n_short = (long_tokens.shape[1], short_tokens.shape[1])
    rows, keys = (2 * n_long, 4 * n_long)
    square = width * width
    early_pieces, late_pieces = (4, 2 + 2 * chunks)

    def swap_seq(value, mask, keep=lambda source, target: True):
        pairs = [(i, i ^ mask) for i in range(seq_count) if keep(i, i ^ mask)]
        return lax.ppermute(value, "seq", pairs)

    def swap_dp(value, mask):
        return lax.ppermute(value, "dp", [(i, i ^ mask) for i in range(dp_count)])

    acts = [long_tokens, short_tokens, long_cot, short_cot]
    packed = [
        ((2 * n_long, width), BF, HBM),
        ((n_long, width), BF, HBM),
        ((n_long, width), BF, HBM),
    ]
    own, specs, scratch = ([], [HBM] * 4, [])
    held = list(acts)
    if direct:
        own = [w_out, w_up, w_down.T]
        own += [norm_gain, norm_bias]
        held += own
        packed += [((late_pieces, BAND, width), BF, HBM)]
        specs += [HBM] * 5
        scratch = [pltpu.VMEM((BAND, width), BF)]
    pays = call(
        functools.partial(pack_body, direct),
        packed,
        specs,
        [pltpu.VMEM(item.shape, BF) for item in held] + scratch + [pltpu.SemaphoreType.DMA((32,))],
        (0, 4 * MIB),
        "pack",
        60,
    )(*acts, *own)
    pay1, pay2, pay3 = pays[:3]

    def to_slots(whole):
        count = whole.shape[0]
        cut = whole.reshape(count, 4, 2, 4, BAND, width).transpose(2, 1, 3, 0, 4, 5)
        return [cut[core, outer] for core in range(2) for outer in range(4)]

    def slot_outs(pieces):
        near = ((4, pieces, BAND, width), BF, HBM)
        return [near] * layers + [((4 * layers, pieces, BAND, width), BF, HBM)]

    def from_slots(parts):
        count = parts[0].shape[1]
        cut = jnp.concatenate(parts, 0).reshape(2, 4, 4, count, BAND, width)
        return cut.transpose(3, 1, 0, 2, 4, 5).reshape(count, width, width)

    def places(piece):
        return [piece] + [swap_seq(piece, k) for k in range(1, 4)]

    def spread(column):
        near = [column] + [swap_dp(column, 2 * k) for k in range(1, layers)]
        return near

    def cross(near):
        return list(near) + [swap_dp(part, 1) for part in near]

    early_layout = plain_layout(early_pieces)
    late_layout = split_layout(late_pieces) if direct else plain_layout(late_pieces)
    if direct:
        late = pays[3]
        early = jnp.stack([w_query, w_key, w_value, pos_table.T])
        early_places = places(early)
        late_places = places(late)
        early_near = spread(jnp.stack(early_places))
        column = jnp.stack(late_places)
        column = after(column, *early_near)
        pay1, pay2, pay3 = lax.optimization_barrier((pay1, pay2, pay3, *late_places))[:3]
        got1, got2, got3 = (
            swap_seq(pay1, 1),
            swap_seq(pay2, 2, lambda source, target: target != 1),
            swap_seq(pay3, 3, lambda source, target: target != 1),
        )
        early_full = early_near + cross(lax.optimization_barrier((early_near, got1, got2, got3))[0])[4:]
        half = late_pieces // 2
        near1, near2 = (swap_dp(column, 2), swap_dp(column, 4))
        near3 = [swap_dp(near1[:, :half], 4), swap_dp(near2[:, half:], 2)]
    if not direct:
        got1, got2, got3 = (
            swap_seq(pay1, 1),
            swap_seq(pay2, 2, lambda source, target: target != 1),
            swap_seq(pay3, 3, lambda source, target: target != 1),
        )

        def columns(weight):
            return weight.reshape(weight.shape[0], chunks, width).transpose(1, 0, 2)

        def whole(pieces):
            return lax.all_gather(pieces, ("dp", "seq"), axis=1, tiled=True)

        early_full = to_slots(whole(jnp.stack([w_query, w_key, w_value, pos_table.T])))
        vectors = jnp.concatenate([norm_gain, norm_bias], 0)
        vectors = lax.all_gather(vectors, ("dp", "seq"), axis=1, tiled=True)
        vectors = jnp.pad(vectors, ((0, width - 4), (0, 0)))
        late_whole = whole(jnp.concatenate([w_out[None], columns(w_up), columns(w_down.T)], 0))
        late_full = to_slots(jnp.concatenate([late_whole, vectors[None]], 0))

    groups = width // LANES
    first, low, low_queries, queries, key_rows, values, probs, mixed = call(
        functools.partial(attend_body, direct, early_layout),
        [
            ((rows, width), F32, VMEM),
            ((keys, width), BF, VMEM),
            ((rows, width), BF, VMEM),
            ((rows, width), BF, VMEM),
            ((keys, width), BF, VMEM),
            ((keys, width), BF, VMEM),
            ((groups, 2 * rows, keys), BF, VMEM),
            ((rows, width), BF, VMEM),
        ],
        [SMEM] * 2 + [VMEM] * 5 + [HBM] * len(early_layout),
        [
            pltpu.VMEM((early_pieces, width, width), BF),
            pltpu.VMEM((width, width), F32),
            pltpu.VMEM((keys, width), F32),
            pltpu.SemaphoreType.DMA,
        ],
        (8 * keys * square, 10 * MIB),
        "attend",
        24,
    )(long_lengths, short_lengths, long_tokens, short_tokens, got1, got2, got3, *early_full)

    if direct:
        near3, first = lax.optimization_barrier((near3, first))
        late_near = [column, near1, near2]
        late_far = [swap_dp(part, 1) for part in late_near + list(near3)]
        late_full = late_near + list(near3) + late_far
    block = (n_long, width)
    middle_outs = call(
        functools.partial(middle_body, direct, late_layout),
        [((keys, width), BF, VMEM)]
        + [((rows, width), F32, VMEM), ((rows, width), BF, VMEM)]
        + slot_outs(late_pieces),
        [VMEM] * 7 + [HBM] * len(late_layout),
        [
            pltpu.VMEM((late_pieces, width, width), BF),
            pltpu.VMEM((late_pieces, width, width), BF),
            pltpu.VMEM((chunks, rows, width), BF),
            pltpu.VMEM((chunks, rows, width), F32),
            pltpu.VMEM((rows, width), F32),
            pltpu.SemaphoreType.DMA,
        ],
        (16 * rows * square * chunks, 20 * MIB),
        "middle",
        32,
    )(first, mixed, long_cot, short_cot, got1, got2, got3, *late_full)
    out_blocks, grad_sum, grad_mixed = middle_outs[:3]
    late_parts = middle_outs[3:]

    def core_sums(parts, arrived):
        return [
            (parts[k].astype(F32) + arrived[4 * k : 4 * k + 4].astype(F32)).astype(BF)
            for k in range(1, layers)
        ]

    if direct:
        late_arrived = swap_dp(late_parts[-1], 1)

    grad_q, grad_k, grad_v, back_rows, *grad_blocks = call(
        functools.partial(attend_back_body, direct, early_layout),
        [
            ((rows, width), BF, VMEM),
            ((keys, width), BF, VMEM),
            ((keys, width), BF, VMEM),
            ((keys, width), F32, VMEM),
            (block, F32, VMEM),
            ((2 * n_long, width), BF, VMEM),
            (block, BF, VMEM),
            (block, BF, VMEM),
        ],
        [VMEM] * 7 + [HBM] * len(early_layout),
        [pltpu.VMEM((early_pieces, width, width), BF), pltpu.SemaphoreType.DMA],
        (16 * keys * square, 12 * MIB),
        "attend_back",
        24,
    )(grad_mixed, queries, key_rows, values, probs, grad_sum, out_blocks, *early_full)
    early_parts = call(
        functools.partial(leave_body, direct),
        slot_outs(early_pieces),
        [VMEM] * 6,
        [
            pltpu.VMEM((early_pieces, width, width), BF),
            pltpu.VMEM((width, width), F32),
            pltpu.SemaphoreType.DMA,
        ],
        (6 * keys * square, 8 * MIB),
        "leave",
        24,
    )(low, low_queries, grad_q, grad_k, grad_v, back_rows)

    back = lambda source, target: source != 1
    got = [swap_seq(grad_blocks[1], 1)] + [swap_seq(grad_blocks[k], k, back) for k in (2, 3)]
    row_outs = [(item.shape, BF, VMEM) for item in (long_tokens, short_tokens)] * 2
    if direct:
        half = late_pieces // 2
        near0, near1, near2, near3 = late_parts[:4]
        far = late_arrived
        single = ((4, half, BAND, width), BF, 0)
        to_x, to_y, last_x, last_y = sum_call(
            functools.partial(first_sums_body, half),
            [single] * 4,
            [near1, near2, near3, far, far, far],
            [one_place(item) for item in (near1, near2, near3)] + [one_place(far, k) for k in (1, 2, 3)],
            4,
            "late_sums_1",
        )
        from_x, from_y = (swap_dp(to_x, 2), swap_dp(to_y, 4))
        last_x, last_y = (swap_dp(last_x, 2), swap_dp(last_y, 4))
        early_far = early_parts[-1]
        early_arrived = swap_dp(early_far, 1)
        early_sums = core_sums(early_parts, early_arrived)
        from_x, from_y, early_sums = lax.optimization_barrier((from_x, from_y, early_sums))
        then_x, then_y = sum_call(
            functools.partial(second_sums_body, half),
            [single, single],
            [near1, near2, far, far, from_x, from_y],
            [one_place(near1), one_place(near2), one_place(far, 1), one_place(far, 2), one_place(from_x), one_place(from_y)],
            4,
            "late_sums_2",
        )
        then_x, then_y = (swap_dp(then_x, 2), swap_dp(then_y, 4))
        early_sums = lax.optimization_barrier((early_sums, last_x, last_y))[0]
        early_layers = [swap_dp(part, 2 * k) for k, part in enumerate(early_sums, 1)]
        then_x, then_y, got = lax.optimization_barrier((then_x, then_y, got))
        late_cut = cut_sums(
            functools.partial(last_sums_body, half),
            [near0, far, last_x, last_y, then_x, then_y],
            late_pieces,
            "late_sums_3",
        )
        late_ends = [late_cut[0]] + [swap_seq(late_cut[k], k) for k in range(1, 4)]
        early_cut = cut_sums(
            four_sums_body, [early_parts[0], early_arrived] + early_layers, early_pieces, "early_sums"
        )
        early_ends = [early_cut[0]] + [swap_seq(early_cut[k], k) for k in range(1, 4)]
        row_ins = [grad_blocks[0], out_blocks, *got]
        ends = call(
            finish_body,
            row_outs
            + [((shard, width), F32, VMEM)] * 5
            + [((shard, hidden), F32, VMEM)] * 2
            + [((2, shard), F32, VMEM)] * 2,
            [VMEM] * 13,
            [],
            (0, MIB),
            "finish",
            16,
        )(*late_ends, *early_ends, *row_ins)
        row_grads, early_sum = (ends[:4], ends[4:8])
        grad_out, grad_up, grad_down, grad_gain, grad_bias = ends[8:]
    else:

        def scatter(parts):
            whole_sum = from_slots(parts).astype(F32)
            return lax.psum_scatter(whole_sum, ("dp", "seq"), scatter_dimension=1, tiled=True)

        def join(pieces):
            return pieces.transpose(1, 0, 2).reshape(shard, hidden)

        late_sum = scatter(late_parts)
        early_sum = scatter(early_parts)
        grad_out, grad_up, grad_down = (
            late_sum[0],
            join(late_sum[1 : 1 + chunks]),
            join(late_sum[1 + chunks : 1 + 2 * chunks]),
        )
        norms = lax.psum(from_slots(late_parts)[-1, :BAND].astype(F32), ("dp", "seq"))
        norms = lax.dynamic_slice(norms, (0, device * shard), (BAND, shard))
        grad_gain, grad_bias = (norms[:2], norms[2:4])
        row_grads = call(
            return_rows, row_outs, [VMEM] * 5, [], (0, MIB), "return", 16
        )(grad_blocks[0], out_blocks, *got)
    long_grad, short_grad, long_out, short_out = row_grads
    return (
        long_out,
        short_out,
        long_grad,
        short_grad,
        early_sum[0],
        early_sum[1],
        early_sum[2],
        grad_out,
        grad_up,
        grad_down.T,
        early_sum[3].T,
        grad_gain,
        grad_bias,
    )


def solution(mesh):
    rows = P(("dp", "seq"), None)
    cols = P(None, ("dp", "seq"))
    acts = P("dp", "seq", None)
    return jax.shard_map(
        functools.partial(local, mesh.shape["dp"], mesh.shape["seq"]),
        mesh=mesh,
        in_specs=(acts,) * 4 + (P("dp"),) * 2 + (rows,) * 5 + (cols,) * 4,
        out_specs=(acts,) * 4 + (rows,) * 5 + (cols,) * 4,
        check_vma=False,
    )
```
